32 devices in a mesh: dp: 2 (over core), expert: 16 (over z, y, x).
Axes of the slice: x: 2, y: 2, z: 4, core: 2. Of those that a mesh axis runs over, the one named last changes fastest.
Arguments:
- tokens_in: bfloat16 [12288, 1280], P(('dp', 'expert')), may hold values from -6 to 6
- lengths: int32 [32], P(('dp', 'expert')), may hold values from 48 to 384, as said below
- key_keep: int32 [12288], P(('dp', 'expert')), may hold values 0 or 1
- routes: int32 [12288, 7], P(('dp', 'expert')), may hold values from 0 to 15, all different within a row; in each aligned block of 384 rows (0 to 383, 384 to 767, ...) at most 189 rows name the same one
- cotangent: bfloat16 [12288, 1280], P(('dp', 'expert')), may hold values from -6 to 6
- attention_in: float32 [3, 1280, 1280], P(None, None, ('dp', 'expert')), may hold values from -0.15625 to 0.15625
- attention_in_momentum: float32 [3, 1280, 1280], P(None, None, ('dp', 'expert'))
- attention_in_average: float32 [3, 1280, 1280], P(None, None, ('dp', 'expert')), may hold values from -0.15625 to 0.15625
- attention_out: float32 [1280, 1280], P(None, ('dp', 'expert')), may hold values from -1.25 to 1.25
- attention_out_momentum: float32 [1280, 1280], P(None, ('dp', 'expert'))
- attention_out_average: float32 [1280, 1280], P(None, ('dp', 'expert')), may hold values from -1.25 to 1.25
- shared_in: float32 [2, 1280, 896], P(None, ('dp', 'expert')), may hold values from -0.15625 to 0.15625
- shared_in_momentum: float32 [2, 1280, 896], P(None, ('dp', 'expert'))
- shared_in_average: float32 [2, 1280, 896], P(None, ('dp', 'expert')), may hold values from -0.15625 to 0.15625
- shared_down: float32 [896, 1280], P(None, ('dp', 'expert')), may hold values from -0.375 to 0.375
- shared_down_momentum: float32 [896, 1280], P(None, ('dp', 'expert'))
- shared_down_average: float32 [896, 1280], P(None, ('dp', 'expert')), may hold values from -0.375 to 0.375
- router: float32 [1280, 16], P(('dp', 'expert')), may hold values from -0.078125 to 0.078125
- router_momentum: float32 [1280, 16], P(('dp', 'expert'))
- router_average: float32 [1280, 16], P(('dp', 'expert')), may hold values from -0.078125 to 0.078125
- norm_gains: float32 [2, 1280], P(None, ('dp', 'expert')), may hold values from 0.5 to 1.5
- norm_gains_momentum: float32 [2, 1280], P(None, ('dp', 'expert'))
- norm_gains_average: float32 [2, 1280], P(None, ('dp', 'expert')), may hold values from 0.5 to 1.5
- expert_in: float32 [16, 2, 1280, 896], P('expert', None, 'dp'), may hold values from -0.15625 to 0.15625
- expert_in_momentum: float32 [16, 2, 1280, 896], P('expert', None, 'dp')
- expert_in_average: float32 [16, 2, 1280, 896], P('expert', None, 'dp'), may hold values from -0.15625 to 0.15625
- expert_down: float32 [16, 896, 1280], P('expert', 'dp'), may hold values from -0.75 to 0.75
- expert_down_momentum: float32 [16, 896, 1280], P('expert', 'dp')
- expert_down_average: float32 [16, 896, 1280], P('expert', 'dp'), may hold values from -0.75 to 0.75
Outputs:
- output: bfloat16 [12288, 1280], P(('dp', 'expert'))
- input_grad: float32 [12288, 1280], P(('dp', 'expert'))
- new_attention_in: float32 [3, 1280, 1280], P(None, None, ('dp', 'expert'))
- new_attention_in_momentum: float32 [3, 1280, 1280], P(None, None, ('dp', 'expert'))
- new_attention_in_average: float32 [3, 1280, 1280], P(None, None, ('dp', 'expert'))
- new_attention_out: float32 [1280, 1280], P(None, ('dp', 'expert'))
- new_attention_out_momentum: float32 [1280, 1280], P(None, ('dp', 'expert'))
- new_attention_out_average: float32 [1280, 1280], P(None, ('dp', 'expert'))
- new_shared_in: float32 [2, 1280, 896], P(None, ('dp', 'expert'))
- new_shared_in_momentum: float32 [2, 1280, 896], P(None, ('dp', 'expert'))
- new_shared_in_average: float32 [2, 1280, 896], P(None, ('dp', 'expert'))
- new_shared_down: float32 [896, 1280], P(None, ('dp', 'expert'))
- new_shared_down_momentum: float32 [896, 1280], P(None, ('dp', 'expert'))
- new_shared_down_average: float32 [896, 1280], P(None, ('dp', 'expert'))
- new_router: float32 [1280, 16], P(('dp', 'expert'))
- new_router_momentum: float32 [1280, 16], P(('dp', 'expert'))
- new_router_average: float32 [1280, 16], P(('dp', 'expert'))
- new_norm_gains: float32 [2, 1280], P(None, ('dp', 'expert'))
- new_norm_gains_momentum: float32 [2, 1280], P(None, ('dp', 'expert'))
- new_norm_gains_average: float32 [2, 1280], P(None, ('dp', 'expert'))
- new_expert_in: float32 [16, 2, 1280, 896], P('expert', None, 'dp')
- new_expert_in_momentum: float32 [16, 2, 1280, 896], P('expert', None, 'dp')
- new_expert_in_average: float32 [16, 2, 1280, 896], P('expert', None, 'dp')
- new_expert_down: float32 [16, 896, 1280], P('expert', 'dp')
- new_expert_down_momentum: float32 [16, 896, 1280], P('expert', 'dp')
- new_expert_down_average: float32 [16, 896, 1280], P('expert', 'dp')
The draws below stay inside these ranges and needn't reach their ends.
Inputs may be any that keep to these rules, and one draw needn't show every extreme that they name: `lengths`: every sequence has at least 48 used tokens, and some sequence uses all 384. `routes`: the 7 experts of a token differ; among the rows of one device at most 189 name one expert, a bound that some block reaches.
All inputs are finite; a program needn't handle non-finite values. No bound on the sum of `key_keep` on one device may be relied on, other than what follows from the above.
Results may differ from the reference program's by a relative error of at most 0.015.
The reference program's roundings to bfloat16 on the way count: a program that leaves them out, or rounds other values in their place, can miss the bound.
Values may be sent and summed in bfloat16 or wider, within the bound.
A program may use at most 320 MiB of HBM per device.

```python
import math
import jax
import jax.numpy as jnp
import numpy as np
from jax import lax

D = 1280
HEADS = 10
HD = 128
FF = 896
TOPK = 7
TOK_DEV = 384
STEP = 4
EXPERTS = 16
CAP = 189
SEQS = 32
TOKENS = 12288


def scaled_normal(key, shape, magnitude):
    return (magnitude * jnp.clip(jax.random.normal(key, shape, jnp.float32), -6.0, 6.0)).astype(jnp.float32)


def draw_lengths(key, part):
    key = jax.random.fold_in(key, 11)
    first_key, second_key = jax.random.split(key)
    drawn = jax.random.randint(first_key, (SEQS,), TOK_DEV // 8, TOK_DEV + 1, dtype=jnp.int32)
    picked = jax.random.randint(second_key, (), 0, SEQS, dtype=jnp.int32)
    return drawn.at[picked].set(TOK_DEV)


def draw_attention_in_momentum(key, part):
    key = jax.random.fold_in(key, 21)
    return scaled_normal(key, (3, D, D), 3.0 * math.sqrt(TOKENS))


def draw_attention_out_momentum(key, part):
    key = jax.random.fold_in(key, 22)
    return scaled_normal(key, (D, D), 0.17 * math.sqrt(TOKENS))


def draw_shared_in_momentum(key, part):
    key = jax.random.fold_in(key, 23)
    return scaled_normal(key, (2, D, FF), 1.5 * math.sqrt(TOKENS))


def draw_shared_down_momentum(key, part):
    key = jax.random.fold_in(key, 24)
    return scaled_normal(key, (FF, D), 0.6 * math.sqrt(TOKENS))


def draw_router_momentum(key, part):
    key = jax.random.fold_in(key, 25)
    return scaled_normal(key, (D, EXPERTS), 1.7 * math.sqrt(TOKENS))


def draw_norm_gains_momentum(key, part):
    key = jax.random.fold_in(key, 26)
    return scaled_normal(key, (2, D), 5.0 * math.sqrt(TOKENS))


def draw_expert_in_momentum(key, part):
    key = jax.random.fold_in(key, 27)
    return scaled_normal(key, (EXPERTS, 2, D, FF), 0.4 * math.sqrt(TOKENS * TOPK / EXPERTS))


def draw_expert_down_momentum(key, part):
    key = jax.random.fold_in(key, 28)
    return scaled_normal(key, (EXPERTS, FF, D), 0.084 * math.sqrt(TOKENS * TOPK / EXPERTS))


def with_ends(entries, stream_key, least, largest):
    dims = entries.shape
    spot = [jax.random.randint(jax.random.fold_in(stream_key, axis), (), 0, dims[axis]) for axis in range(len(dims))]
    entries = entries.at[tuple(spot)].set(least)
    longest = dims.index(max(dims))
    spot[longest] = (spot[longest] + 1) % dims[longest]
    return entries.at[tuple(spot)].set(largest)


def strengthened(values, own_key, source, target, blocks, factor):
    def block_of(dim):
        return (jnp.arange(values.shape[dim]) // (values.shape[dim] // blocks)).reshape((-1,) + (1,) * (values.ndim - 1 - dim))

    first = jax.random.permutation(own_key, blocks)[block_of(target)]
    second = (block_of(target) + blocks // 2) % blocks
    return jnp.where((block_of(source) == first) | (block_of(source) == second), factor * values, values)


def steps_of(own_key, extent, shards, low, largest):
    def one(axis_at, blocks):
        draws = jax.random.uniform(jax.random.fold_in(jax.random.fold_in(own_key, 6), axis_at), (blocks,), jnp.float32, low / len(shards), largest / len(shards))
        return jnp.repeat(jnp.exp(draws), extent[axis_at] // blocks).reshape((-1,) + (1,) * (len(extent) - axis_at - 1))

    level = one(*shards[0])
    for cut in shards[1:]:
        level = level * one(*cut)
    return level


def shared_out(key, own, number, rows, count, top, reach, lean):
    sequence = jax.random.permutation(key, count)
    crowded, usual = load_shares(count, rows * top, reach, lean, True), load_shares(count, rows * top, reach, lean, False)
    places = jnp.arange(count)

    def named(tallies, offset_by):
        used = int((tallies > 0).sum())
        fixed = max(1, used // 4)
        passed = fixed + (places - fixed + offset_by * (used - fixed)) % max(1, count - fixed)
        return jnp.zeros((count,), jnp.int32).at[sequence[jnp.where(places < fixed, places, passed)]].set(jnp.asarray(tallies, jnp.int32))

    tallies = jnp.where(number % 4 == 0, named(crowded, number // 4), named(usual, number - number // 4 - 1))
    mixed = jax.random.permutation(jax.random.fold_in(own, 3), count)
    giver, taker = mixed[0:count // 2 * 2:2], mixed[1:count // 2 * 2:2]
    margin = jnp.minimum(tallies[giver] - 1, reach - tallies[taker]) // 2
    margin = jnp.where((giver == sequence[0]) | (taker == sequence[0]) | (tallies[taker] == 0), 0, jnp.maximum(margin, 0))
    passed = jax.random.randint(jax.random.fold_in(own, 4), (count // 2,), 0, 1 << 20) % (margin + 1)
    tallies = tallies.at[giver].add(-passed).at[taker].add(passed)
    labels = jnp.searchsorted(jnp.cumsum(tallies), jnp.arange(rows * top), side="right").astype(jnp.int32)
    listing = labels.reshape(top, rows).T
    listing = listing[jax.random.permutation(jax.random.fold_in(own, 1), rows)]
    offset_by = jax.random.randint(jax.random.fold_in(own, 2), (rows, 1), 0, top)
    return jnp.take_along_axis(listing, (jnp.arange(top)[None, :] + offset_by) % top, axis=1)


def load_shares(number_of, total, bound, slope, full):
    loads = [(1 << 20) // math.isqrt(grade ** slope) + 1 for grade in range(1, number_of + 1)]
    largest = bound if full else min(bound, max(-(-total // number_of), total * loads[0] // sum(loads)))
    least = 1 if total - largest >= number_of - 1 else 0
    given, spare = [largest] + [least] * (number_of - 1), total - largest - least * (number_of - 1)
    while spare > 0:
        candidates = [i for i in range(1, number_of) if given[i] < largest] or [i for i in range(1, number_of) if given[i] < bound]
        whole, budget = sum([loads[i] for i in candidates]), spare
        for i in candidates:
            addition = min(bound - given[i], max(1, budget * loads[i] // whole), spare)
            given[i] = given[i] + addition
            spare = spare - addition
    return np.array(given)


def bell_draw(stream_key, shape, spread, limit, cuts=(), kind=jnp.bfloat16):
    factor_of = steps_of(stream_key, shape, cuts, -0.22, 0.18) if cuts else 1.0
    entries = jax.random.normal(stream_key, shape, jnp.float32) * spread * factor_of
    return jnp.minimum(jnp.maximum(entries, -limit), limit).astype(kind)


def gaussian_with(own_key, extent, spread, reach, pieces, heavy, held_as=jnp.bfloat16):
    entries = spread * jax.random.normal(own_key, extent, jnp.float32)
    if pieces:
        entries = entries * steps_of(own_key, extent, pieces, -0.22, 0.18)
    return jnp.clip(strengthened(entries, jax.random.fold_in(own_key, 3), *heavy), -reach, reach).astype(held_as)


def setup_inputs(seed: int = 0) -> dict:
    splits = jax.random.split(jax.random.key(seed), 30)
    tokens_in = bell_draw(splits[0], (TOKENS, D), 1.0, 6.0, ((0, 32),))
    lengths = draw_lengths(jax.random.fold_in(splits[29], 71), 0)
    key_keep = with_ends((jax.random.randint(splits[2], (TOKENS,), 0, 8) < 7).astype(jnp.int32), jax.random.fold_in(splits[2], 1), 0, 1)
    routes_keys = jax.random.split(jax.random.fold_in(splits[3], 1), TOKENS // TOK_DEV)
    routes_turns = jax.random.permutation(jax.random.fold_in(splits[3], 3), TOKENS // TOK_DEV)
    routes = jax.vmap(lambda own, number: shared_out(jax.random.fold_in(splits[3], 2), own, number, TOK_DEV, EXPERTS, TOPK, CAP, 1))(routes_keys, routes_turns).reshape((TOKENS, TOPK))
    cotangent = gaussian_with(splits[4], (TOKENS, D), 1.0, 6.0, ((0, 32),), (0, 1, 32, 2.75))
    attention_in = bell_draw(splits[5], (3, D, D), D ** -0.5, 0.15625, ((2, 32),), jnp.float32)
    attention_in_momentum = draw_attention_in_momentum(jax.random.fold_in(splits[29], 71), 0)
    attention_in_average = bell_draw(splits[7], (3, D, D), D ** -0.5, 0.15625, ((2, 32),), jnp.float32)
    attention_out = bell_draw(splits[8], (D, D), (D // 64) ** -0.5, 1.25, ((1, 32),), jnp.float32)
    attention_out_momentum = draw_attention_out_momentum(jax.random.fold_in(splits[29], 71), 0)
    attention_out_average = bell_draw(splits[10], (D, D), (D // 64) ** -0.5, 1.25, ((1, 32),), jnp.float32)
    shared_in = bell_draw(splits[11], (2, D, FF), D ** -0.5, 0.15625, ((1, 32),), jnp.float32)
    shared_in_momentum = draw_shared_in_momentum(jax.random.fold_in(splits[29], 71), 0)
    shared_in_average = bell_draw(splits[13], (2, D, FF), D ** -0.5, 0.15625, ((1, 32),), jnp.float32)
    shared_down = bell_draw(splits[14], (FF, D), (FF // 4) ** -0.5, 0.375, ((1, 32),), jnp.float32)
    shared_down_momentum = draw_shared_down_momentum(jax.random.fold_in(splits[29], 71), 0)
    shared_down_average = bell_draw(splits[16], (FF, D), (FF // 4) ** -0.5, 0.375, ((1, 32),), jnp.float32)
    router = bell_draw(splits[17], (D, EXPERTS), (4 * D) ** -0.5, 0.078125, ((0, 32),), jnp.float32)
    router_momentum = draw_router_momentum(jax.random.fold_in(splits[29], 71), 0)
    router_average = bell_draw(splits[19], (D, EXPERTS), (4 * D) ** -0.5, 0.078125, ((0, 32),), jnp.float32)
    norm_gains = jnp.clip(1.0 + 0.1 * jax.random.normal(splits[20], (2, D), jnp.float32), 0.5, 1.5)
    norm_gains_momentum = draw_norm_gains_momentum(jax.random.fold_in(splits[29], 71), 0)
    norm_gains_average = jnp.clip(1.0 + 0.1 * jax.random.normal(splits[22], (2, D), jnp.float32), 0.5, 1.5)
    expert_in = bell_draw(splits[23], (EXPERTS, 2, D, FF), D ** -0.5, 0.15625, ((0, 16), (2, 2)), jnp.float32)
    expert_in_momentum = draw_expert_in_momentum(jax.random.fold_in(splits[29], 71), 0)
    expert_in_average = bell_draw(splits[25], (EXPERTS, 2, D, FF), D ** -0.5, 0.15625, ((0, 16), (2, 2)), jnp.float32)
    expert_down = bell_draw(splits[26], (EXPERTS, FF, D), (FF // 16) ** -0.5, 0.75, ((0, 16), (1, 2)), jnp.float32)
    expert_down_momentum = draw_expert_down_momentum(jax.random.fold_in(splits[29], 71), 0)
    expert_down_average = bell_draw(splits[28], (EXPERTS, FF, D), (FF // 16) ** -0.5, 0.75, ((0, 16), (1, 2)), jnp.float32)
    return dict(tokens_in=tokens_in, lengths=lengths, key_keep=key_keep, routes=routes, cotangent=cotangent, attention_in=attention_in, attention_in_momentum=attention_in_momentum, attention_in_average=attention_in_average, attention_out=attention_out, attention_out_momentum=attention_out_momentum, attention_out_average=attention_out_average, shared_in=shared_in, shared_in_momentum=shared_in_momentum, shared_in_average=shared_in_average, shared_down=shared_down, shared_down_momentum=shared_down_momentum, shared_down_average=shared_down_average, router=router, router_momentum=router_momentum, router_average=router_average, norm_gains=norm_gains, norm_gains_momentum=norm_gains_momentum, norm_gains_average=norm_gains_average, expert_in=expert_in, expert_in_momentum=expert_in_momentum, expert_in_average=expert_in_average, expert_down=expert_down, expert_down_momentum=expert_down_momentum, expert_down_average=expert_down_average)


eps_norm = 1e-06
theta_base = 10000.0
momentum_decay = 0.9
mask_fill = -1e+30
rate_attention_in = 2e-05
rate_attention_out = 0.002
rate_shared_in = 3e-05
rate_shared_down = 0.0002
rate_router = 1.5e-05
rate_gains = 0.0002
rate_expert_in = 0.0004
rate_expert_down = 0.008
highest = lax.Precision.HIGHEST

@jax.custom_vjp
def low(v):
    return lax.optimization_barrier(v.astype(jnp.bfloat16)).astype(jnp.float32)

@jax.custom_vjp
def low_back(v):
    return v

def low_keep(v):
    return (low(v), None)

def low_pass(kept, grad):
    return (grad,)

def back_keep(v):
    return (v, None)

def back_low(kept, grad):
    return (low(grad),)
low.defvjp(low_keep, low_pass)
low_back.defvjp(back_keep, back_low)

def rope_tables(length, head_width):
    half_width = head_width // 2
    frequency = theta_base ** (-(jnp.arange(half_width, dtype=jnp.float32) * 2.0 / head_width))
    angles = jnp.arange(length, dtype=jnp.float32)[:, None] * frequency[None, :]
    return (jnp.cos(angles)[:, None, :], jnp.sin(angles)[:, None, :])

def rotate(values, cosine, sine_table):
    half_width = values.shape[-1] // 2
    front_half = values[..., :half_width]
    back_half = values[..., half_width:]
    return jnp.concatenate([front_half * cosine - back_half * sine_table, back_half * cosine + front_half * sine_table], axis=-1)

def allowed_keys(length, keep_flags):
    amount = keep_flags.shape[0]
    position = jnp.arange(amount)
    causal = position[None, :] <= position[:, None]
    usable = (position < length) & (keep_flags == 1)
    return causal & (usable[None, :] | (position[None, :] == position[:, None]))

def attend_one(packed):
    query, key_rot, value, length, keep_flags = packed
    allowed = allowed_keys(length, keep_flags)
    scores = jnp.einsum('qhd,khd->hqk', query, key_rot, precision=highest) * HD ** (-0.5)
    scores = low_back(scores)
    scores = jnp.where(allowed[None], scores, mask_fill)
    row_top = lax.optimization_barrier(jnp.max(scores, axis=-1, keepdims=True))
    exps = jnp.exp(scores - row_top)
    probs = low(exps / lax.optimization_barrier(jnp.sum(exps, axis=-1, keepdims=True)))
    return jnp.einsum('hqk,khd->qhd', probs, value, precision=highest)

def expert_rows(rows, pair, down):
    rows = low_back(rows)
    gate_rows = low_back(jnp.dot(rows, pair[0], precision=highest))
    up_rows = low_back(jnp.dot(rows, pair[1], precision=highest))
    inner = low(gate_rows * jax.nn.sigmoid(gate_rows) * up_rows)
    return low(low_back(jnp.dot(inner, down, precision=highest)))

def slot_targets(routes, usable):
    ids_flat = routes.reshape(SEQS, TOK_DEV * TOPK)
    live_flat = jnp.repeat(usable, TOPK).reshape(SEQS, TOK_DEV * TOPK)
    chosen_hot = ((ids_flat[:, :, None] == jnp.arange(EXPERTS, dtype=jnp.int32)[None, None, :]) & live_flat[:, :, None]).astype(jnp.int32)
    slot_index = lax.optimization_barrier(jnp.sum((jnp.cumsum(chosen_hot, axis=1) - chosen_hot) * chosen_hot, axis=2)).astype(jnp.int32)
    expert_rows_all = SEQS * CAP
    target = ids_flat * expert_rows_all + jnp.arange(SEQS, dtype=jnp.int32)[:, None] * CAP + slot_index
    target = jnp.where(live_flat, target, EXPERTS * expert_rows_all).reshape(TOKENS * TOPK).astype(jnp.int32)
    slot_table = jnp.full((EXPERTS * expert_rows_all,), TOKENS * TOPK, jnp.int32)
    slot_table = slot_table.at[target].set(jnp.arange(TOKENS * TOPK, dtype=jnp.int32), mode='drop')
    return (target, slot_table)

def forward(inputs, attention_in, attention_out, shared_in, shared_down, router, norm_gains, expert_in, expert_down, lengths, key_keep, routes):
    gain_low = low(norm_gains)
    rstd_one = lax.rsqrt(lax.optimization_barrier(jnp.mean(inputs * inputs, axis=-1, keepdims=True)) + eps_norm)
    normed_one = low(inputs * rstd_one * gain_low[0])
    weights_in = low(attention_in)
    projected = [low_back(jnp.dot(normed_one, weights_in[member], precision=highest)) for member in range(3)]
    cosine, sine_table = rope_tables(TOK_DEV, HD)
    grouped = (SEQS, TOK_DEV, HEADS, HD)
    query = low(rotate(projected[0].reshape(grouped), cosine, sine_table))
    key_rot = low(rotate(projected[1].reshape(grouped), cosine, sine_table))
    value = low(projected[2].reshape(grouped))
    attended = lax.map(jax.checkpoint(attend_one), (query, key_rot, value, lengths, key_keep.reshape(SEQS, TOK_DEV)))
    attended = low_back(low(attended.reshape(TOKENS, D)))
    branch = low_back(jnp.dot(attended, low(attention_out), precision=highest))
    hidden = inputs + branch
    rstd_two = lax.rsqrt(lax.optimization_barrier(jnp.mean(hidden * hidden, axis=-1, keepdims=True)) + eps_norm)
    normed_two = low(hidden * rstd_two * gain_low[1])
    logits = low_back(jnp.dot(normed_two, low(router), precision=highest))
    chosen = jnp.take_along_axis(logits, routes, axis=1)
    row_top = lax.optimization_barrier(jnp.max(chosen, axis=-1, keepdims=True))
    exps = jnp.exp(chosen - row_top)
    gating = exps / lax.optimization_barrier(jnp.sum(exps, axis=-1, keepdims=True))
    usable = jnp.arange(TOKENS, dtype=jnp.int32) % TOK_DEV < jnp.repeat(lengths, TOK_DEV)
    gating_live = gating * usable[:, None].astype(jnp.float32)
    shared_pair = low(shared_in)
    shared_gate = low_back(jnp.dot(normed_two, shared_pair[0], precision=highest))
    shared_up = low_back(jnp.dot(normed_two, shared_pair[1], precision=highest))
    shared_hidden = low(shared_gate * jax.nn.sigmoid(shared_gate) * shared_up)
    shared_result = low_back(jnp.dot(shared_hidden, low(shared_down), precision=highest))
    target, slot_table = slot_targets(routes, usable)
    rows_padded = jnp.concatenate([normed_two, jnp.zeros((1, D), jnp.float32)], axis=0)
    owner_rows = (slot_table // TOPK).reshape(EXPERTS, SEQS * CAP)

    def run_expert(packed):
        owner_row, pair, down = packed
        return expert_rows(rows_padded[owner_row], pair, down)
    results = lax.map(jax.checkpoint(run_expert), (owner_rows, low(expert_in), low(expert_down)))
    flat_results = jnp.concatenate([results.reshape(EXPERTS * SEQS * CAP, D), jnp.zeros((1, D), jnp.float32)], axis=0)
    target_pairs = target.reshape(TOKENS, TOPK)
    routed = jnp.zeros((TOKENS, D), jnp.float32)
    for member in range(TOPK):
        routed = routed + gating_live[:, member:member + 1] * flat_results[target_pairs[:, member]]
    return hidden + shared_result + routed

def advance(weight, moment, average, gradient, step_rate):
    moment_new = momentum_decay * moment + gradient
    weight_new = weight - step_rate * (gradient + momentum_decay * moment_new)
    average_new = average + (weight_new - average) / (STEP + 1)
    return (weight_new, moment_new, average_new)

def reference(tokens_in, lengths, key_keep, routes, cotangent, attention_in, attention_in_momentum, attention_in_average, attention_out, attention_out_momentum, attention_out_average, shared_in, shared_in_momentum, shared_in_average, shared_down, shared_down_momentum, shared_down_average, router, router_momentum, router_average, norm_gains, norm_gains_momentum, norm_gains_average, expert_in, expert_in_momentum, expert_in_average, expert_down, expert_down_momentum, expert_down_average):

    def wrapped(inputs, w_attn_in, w_attn_out, w_shared_in, w_shared_down, w_router, w_gains, w_expert_in, w_expert_down):
        return forward(inputs, w_attn_in, w_attn_out, w_shared_in, w_shared_down, w_router, w_gains, w_expert_in, w_expert_down, lengths, key_keep, routes)
    result, pull = jax.vjp(wrapped, tokens_in.astype(jnp.float32), attention_in, attention_out, shared_in, shared_down, router, norm_gains, expert_in, expert_down)
    grads = pull(cotangent.astype(jnp.float32))
    upd_attn_in = advance(attention_in, attention_in_momentum, attention_in_average, grads[1], rate_attention_in)
    upd_attn_out = advance(attention_out, attention_out_momentum, attention_out_average, grads[2], rate_attention_out)
    upd_shared_in = advance(shared_in, shared_in_momentum, shared_in_average, grads[3], rate_shared_in)
    upd_shared_down = advance(shared_down, shared_down_momentum, shared_down_average, grads[4], rate_shared_down)
    upd_router = advance(router, router_momentum, router_average, grads[5], rate_router)
    upd_gains = advance(norm_gains, norm_gains_momentum, norm_gains_average, grads[6], rate_gains)
    upd_expert_in = advance(expert_in, expert_in_momentum, expert_in_average, grads[7], rate_expert_in)
    upd_expert_down = advance(expert_down, expert_down_momentum, expert_down_average, grads[8], rate_expert_down)
    return (result.astype(jnp.bfloat16), grads[0], upd_attn_in[0], upd_attn_in[1], upd_attn_in[2], upd_attn_out[0], upd_attn_out[1], upd_attn_out[2], upd_shared_in[0], upd_shared_in[1], upd_shared_in[2], upd_shared_down[0], upd_shared_down[1], upd_shared_down[2], upd_router[0], upd_router[1], upd_router[2], upd_gains[0], upd_gains[1], upd_gains[2], upd_expert_in[0], upd_expert_in[1], upd_expert_in[2], upd_expert_down[0], upd_expert_down[1], upd_expert_down[2])
```

```python
import jax
import jax.numpy as jnp
from jax import lax
from jax.sharding import PartitionSpec as P

HD = 128
STEP = 4


eps_norm = 1e-06
theta_base = 10000.0
momentum_decay = 0.9
mask_fill = -1e30
rate_attention_in = 2e-05
rate_attention_out = 0.002
rate_shared_in = 3e-05
rate_shared_down = 0.0002
rate_router = 1.5e-05
rate_gains = 0.0002
rate_expert_in = 0.0004
rate_expert_down = 0.008


def rope_tables(length, head_width):
    half_width = head_width // 2
    frequency = theta_base ** (-(jnp.arange(half_width, dtype=jnp.float32) * 2.0 / head_width))
    angles = jnp.arange(length, dtype=jnp.float32)[:, None] * frequency[None, :]
    return (jnp.cos(angles)[:, None, :], jnp.sin(angles)[:, None, :])


def rotate(values, cosine, sine_table):
    half_width = values.shape[-1] // 2
    front_half = values[..., :half_width]
    back_half = values[..., half_width:]
    return jnp.concatenate(
        [
            front_half * cosine - back_half * sine_table,
            back_half * cosine + front_half * sine_table,
        ],
        axis=-1,
    )


def unrotate(values, cosine, sine_table):
    half_width = values.shape[-1] // 2
    front_half = values[..., :half_width]
    back_half = values[..., half_width:]
    return jnp.concatenate(
        [
            front_half * cosine + back_half * sine_table,
            back_half * cosine - front_half * sine_table,
        ],
        axis=-1,
    )


def allowed_keys(length, keep_flags):
    amount = keep_flags.shape[0]
    position = jnp.arange(amount)
    causal = position[None, :] <= position[:, None]
    usable = (position < length) & (keep_flags == 1)
    return causal & (usable[None, :] | (position[None, :] == position[:, None]))


def silu_parts(values):
    logistic = jax.nn.sigmoid(values)
    return (values * logistic, logistic * (1.0 + values * (1.0 - logistic)))


def advance(weight, moment, average, gradient, step_rate):
    moment_new = momentum_decay * moment + gradient
    weight_new = weight - step_rate * (gradient + momentum_decay * moment_new)
    average_new = average + (weight_new - average) / (STEP + 1)
    return (weight_new, moment_new, average_new)


def dot_nn(a, b):
    return lax.dot_general(a, b, (((1,), (0,)), ((), ())), preferred_element_type=jnp.float32)


def dot_nt(a, b):
    return lax.dot_general(a, b, (((1,), (1,)), ((), ())), preferred_element_type=jnp.float32)


def dot_tn(a, b):
    return lax.dot_general(a, b, (((0,), (0,)), ((), ())), preferred_element_type=jnp.float32)


PLANE = 4


class Grid:
    def __init__(self, experts):
        self.experts = experts
        self.line = experts // PLANE
        here = lax.axis_index("expert")
        self.core = lax.axis_index("dp")
        self.at_line = here // PLANE
        self.at_plane = here % PLANE

    def shift(self, block, amount):
        pairs = [
            (i, ((i // PLANE + amount) % self.line) * PLANE + i % PLANE)
            for i in range(self.experts)
        ]
        return lax.ppermute(block, "expert", pairs)

    def swap(self, block, flip):
        pairs = [(i, (i // PLANE) * PLANE + ((i % PLANE) ^ flip)) for i in range(self.experts)]
        return lax.ppermute(block, "expert", pairs)

    def line_gather(self, block):
        found = [block] + [None] * (self.line - 1)
        for i in range(1, self.line // 2 + 1):
            found[i] = self.shift(found[i - 1], 1)
        last = block
        for i in range(1, (self.line - 1) // 2 + 1):
            last = self.shift(last, -1)
            found[self.line - i] = last
        return found


def halves(array, axis, index):
    mine = lax.dynamic_index_in_dim(array, index, axis, keepdims=False)
    other = lax.dynamic_index_in_dim(array, 1 - index, axis, keepdims=False)
    return mine, other


def add_low(a, b):
    return (a.astype(jnp.float32) + b.astype(jnp.float32)).astype(jnp.bfloat16)


def scatter_sum(grid, grads, splits):
    rows, columns = grads.shape
    block = rows // (2 * grid.experts)
    parts = grads.reshape(2, grid.line, 2, 2, block, columns)
    mine, other = halves(parts, 0, grid.core)
    total = add_low(mine, lax.ppermute(other, "dp", [(0, 1), (1, 0)]))
    bit_y, bit_x = grid.at_plane // 2, grid.at_plane % 2

    def over_y(array, axis):
        mine, other = halves(array, axis, bit_y)
        return add_low(mine, grid.swap(other, 2))

    def over_x(array, axis):
        mine, other = halves(array, axis, bit_x)
        return add_low(mine, grid.swap(other, 1))

    def over_line(array):
        def pick(offset):
            index = lax.rem(grid.at_line + offset + grid.line, grid.line)
            return lax.dynamic_index_in_dim(array, index, 0, keepdims=False)

        half, rest = grid.line // 2, (grid.line - 1) // 2
        low = pick(-half)
        for i in range(half, 0, -1):
            low = add_low(pick(-(i - 1)), grid.shift(low, -1))
        if rest:
            high = pick(rest)
            for i in range(rest, 0, -1):
                got = grid.shift(high, 1)
                if i > 1:
                    high = add_low(pick(i - 1), got)
            low = add_low(low, got)
        return low

    out = []
    start = 0
    for order, width in enumerate(splits):
        piece = lax.slice_in_dim(total, start, start + width, axis=4)
        start += width
        if order == 0:
            piece = over_x(over_y(over_line(piece), 0), 0)
        elif order == 1:
            piece = over_y(over_line(over_x(piece, 2)), 0)
        else:
            piece = over_line(over_x(over_y(piece, 1), 1))
        out.append(piece)
    return jnp.concatenate(out, axis=1)


def local(
    tokens_in,
    lengths,
    key_keep,
    routes,
    cotangent,
    attention_in,
    attention_in_momentum,
    attention_in_average,
    attention_out,
    attention_out_momentum,
    attention_out_average,
    shared_in,
    shared_in_momentum,
    shared_in_average,
    shared_down,
    shared_down_momentum,
    shared_down_average,
    router,
    router_momentum,
    router_average,
    norm_gains,
    norm_gains_momentum,
    norm_gains_average,
    expert_in,
    expert_in_momentum,
    expert_in_average,
    expert_down,
    expert_down_momentum,
    expert_down_average,
):
    low = jnp.bfloat16
    full = jnp.float32
    tokens = tokens_in.shape[0]
    model_width = tokens_in.shape[1]
    head_count = model_width // HD
    top_count = routes.shape[1]
    block_rows = router.shape[0]
    experts = router.shape[1]
    hidden_width = shared_in.shape[2]
    grid = Grid(experts)
    capacity = 9 * tokens * top_count // (8 * experts)
    slots = -(-capacity // 16) * 16
    scaling = HD ** (-0.5)
    extra_width = -(-(experts + 2) // 128) * 128

    pack_one = jnp.concatenate(
        [attention_in[m].astype(low).T for m in range(3)]
        + [
            router.astype(low),
            norm_gains.astype(low).T,
            jnp.zeros((block_rows, extra_width - experts - 2), low),
        ],
        axis=1,
    )
    pack_two = jnp.concatenate(
        [
            attention_out.astype(low).T,
            shared_in[0].astype(low),
            shared_in[1].astype(low),
            shared_down.astype(low).T,
        ],
        axis=1,
    )
    all_one = lax.all_gather(pack_one, ("dp", "expert"), axis=0, tiled=True)
    all_two = lax.all_gather(pack_two, ("dp", "expert"), axis=0, tiled=True)
    turned_in = [all_one[:, m * model_width : (m + 1) * model_width] for m in range(3)]
    extra = all_one[:, 3 * model_width :]
    router_low = extra[:, :experts]
    gains = extra[:, experts : experts + 2].astype(full).T
    gain_one, gain_two = gains[0], gains[1]
    turned_out = all_two[:, :model_width]
    at = model_width
    shared_pair = [all_two[:, at + m * hidden_width : at + (m + 1) * hidden_width] for m in range(2)]
    turned_down = all_two[:, at + 2 * hidden_width :]
    expert_pair = lax.all_gather(expert_in[0].astype(low), "dp", axis=1, tiled=True)
    expert_back = lax.all_gather(expert_down[0].astype(low), "dp", axis=0, tiled=True)

    position = jnp.arange(tokens, dtype=jnp.int32)
    usable = position < lengths[0]
    named = jnp.any(
        routes.T[None, :, :] == jnp.arange(experts, dtype=jnp.int32)[:, None, None], axis=1
    )
    member = named & usable[None, :]
    earlier = (position[:, None] < position[None, :]).astype(low)
    counted = dot_nn(member.astype(low), earlier)
    slot_of = jnp.where(member, counted, -1.0)
    line_slots = grid.line_gather(slot_of)
    wanted = grid.at_line * PLANE + (grid.at_plane ^ jnp.arange(PLANE, dtype=jnp.int32))
    choose = (wanted[:, None] == jnp.arange(experts, dtype=jnp.int32)[None, :]).astype(low)
    slot_ids = jnp.arange(slots, dtype=jnp.int32).astype(full)
    places = []
    for r in range(grid.line):
        chosen_slots = dot_nn(choose, line_slots[r].astype(low))
        places.append(
            (chosen_slots[:, None, :] == slot_ids[None, :, None])
            .astype(low)
            .reshape(PLANE * slots, tokens)
        )

    def dispatch(line_rows):
        rows = dot_nn(places_now, line_rows).astype(low)
        return [rows[:slots]] + [
            grid.swap(rows[q * slots : (q + 1) * slots], q) for q in range(1, PLANE)
        ]

    line_grads = grid.line_gather(cotangent)
    grads_in = []
    for r in range(grid.line):
        places_now = places[r]
        grads_in.append(dispatch(line_grads[r]))

    inputs = tokens_in.astype(full)
    rstd_one = lax.rsqrt(jnp.mean(inputs * inputs, axis=-1, keepdims=True) + eps_norm)
    normed_one = (inputs * rstd_one * gain_one).astype(low)
    projected = [dot_nt(normed_one, turned_in[m]) for m in range(3)]
    cosine, sine_table = rope_tables(tokens, HD)
    split_shape = (tokens, head_count, HD)
    query = rotate(projected[0].reshape(split_shape), cosine, sine_table).astype(low)
    key_rot = rotate(projected[1].reshape(split_shape), cosine, sine_table).astype(low)
    value = projected[2].reshape(split_shape).astype(low)
    allowed = allowed_keys(lengths[0], key_keep)[None]

    def attention_scores():
        raw = jnp.einsum("qhd,khd->hqk", query, key_rot, preferred_element_type=full) * scaling
        return jnp.where(allowed, raw, mask_fill)

    scores = attention_scores()
    row_top = jnp.max(scores, axis=-1, keepdims=True)
    exps = jnp.exp(scores - row_top)
    totals = jnp.sum(exps, axis=-1, keepdims=True)
    log_total = row_top + jnp.log(totals)
    attended = jnp.einsum(
        "hqk,khd->qhd", (exps / totals).astype(low), value, preferred_element_type=full
    )
    attended = attended.reshape(tokens, model_width).astype(low)
    hidden = inputs + dot_nt(attended, turned_out)
    rstd_two = lax.rsqrt(jnp.mean(hidden * hidden, axis=-1, keepdims=True) + eps_norm)
    normed_two = (hidden * rstd_two * gain_two).astype(low)

    logits = lax.dot_general(
        router_low, normed_two, (((0,), (1,)), ((), ())), preferred_element_type=full
    )
    logits = jnp.where(named, logits, mask_fill)
    logit_exps = jnp.exp(logits - jnp.max(logits, axis=0, keepdims=True))
    gating = logit_exps / jnp.sum(logit_exps, axis=0, keepdims=True)
    gating_live = jnp.where(member, gating, 0.0)
    at_slot = slot_of[:, None, :] == slot_ids[None, :, None]
    slot_gates = jnp.sum(jnp.where(at_slot, gating_live[:, None, :], 0.0), axis=2)
    offsets = jnp.arange(grid.line, dtype=jnp.int32)
    source_line = (grid.at_line - offsets + grid.line) % grid.line
    sources = (source_line[:, None] * PLANE + (grid.at_plane ^ jnp.arange(PLANE))[None, :]).reshape(
        experts
    )
    order = (sources[:, None] == jnp.arange(experts, dtype=jnp.int32)[None, :]).astype(full)
    gates_in = lax.all_to_all(slot_gates, "expert", split_axis=0, concat_axis=0, tiled=True)
    gates_in = jnp.dot(order, gates_in, precision=lax.Precision.HIGHEST)

    line_rows = grid.line_gather(normed_two)
    kept = []
    grads_back, results_back, gate_grads = [], [], []
    for r in range(grid.line):
        places_now = places[r]
        rows = jnp.concatenate(dispatch(line_rows[r]), axis=0)
        grad_rows = jnp.concatenate(grads_in[r], axis=0).astype(full)
        gate_col = gates_in[r * PLANE : (r + 1) * PLANE].reshape(PLANE * slots, 1)
        gate_rows = dot_nn(rows, expert_pair[0])
        up_rows = dot_nn(rows, expert_pair[1])
        silu_rows, slope_rows = silu_parts(gate_rows)
        inner = (silu_rows * up_rows).astype(low)
        result_rows = dot_nn(inner, expert_back)
        gate_grads.append(jnp.sum(result_rows * grad_rows, axis=1).reshape(PLANE, slots))
        sent_results = (result_rows * gate_col).astype(low)
        gated = (grad_rows * gate_col).astype(low)
        grad_inner = dot_nt(gated, expert_back)
        grad_gate_rows = (grad_inner * up_rows * slope_rows).astype(low)
        grad_up_rows = (grad_inner * silu_rows).astype(low)
        sent_grads = (
            dot_nt(grad_gate_rows, expert_pair[0]) + dot_nt(grad_up_rows, expert_pair[1])
        ).astype(low)
        kept.append((rows, inner, gated, grad_gate_rows, grad_up_rows))
        grads_back.append(sent_grads)
        results_back.append(sent_results)

    def collect(blocks):
        total = None
        for r in range(grid.line):
            back = jnp.concatenate(
                [blocks[r][:slots]]
                + [
                    grid.swap(blocks[r][q * slots : (q + 1) * slots], q) for q in range(1, PLANE)
                ],
                axis=0,
            )
            part = dot_tn(places[r], back)
            if r:
                part = grid.shift(part.astype(low), -r).astype(full)
            total = part if total is None else total + part
        return total

    routed_grad = collect(grads_back)
    gate_grads = jnp.dot(
        order.T, jnp.concatenate(gate_grads, axis=0), precision=lax.Precision.HIGHEST
    )
    gate_grads = lax.all_to_all(gate_grads, "expert", split_axis=0, concat_axis=0, tiled=True)
    grad_gating = jnp.sum(jnp.where(at_slot, gate_grads[:, :, None], 0.0), axis=1)
    grad_chosen = gating * (grad_gating - jnp.sum(gating * grad_gating, axis=0, keepdims=True))
    grad_logits = grad_chosen.astype(low)
    grad_router = lax.dot_general(
        normed_two, grad_logits, (((0,), (1,)), ((), ())), preferred_element_type=full
    )

    grad_out = cotangent.astype(full)
    shared_gate = dot_nn(normed_two, shared_pair[0])
    shared_up = dot_nn(normed_two, shared_pair[1])
    shared_silu, shared_slope = silu_parts(shared_gate)
    shared_hidden = (shared_silu * shared_up).astype(low)
    shared_result = dot_nt(shared_hidden, turned_down)
    grad_shared_hidden = dot_nn(cotangent, turned_down)
    grad_shared_gate = (grad_shared_hidden * shared_up * shared_slope).astype(low)
    grad_shared_up = (grad_shared_hidden * shared_silu).astype(low)
    grad_normed_two = dot_nt(grad_shared_gate, shared_pair[0]) + dot_nt(
        grad_shared_up, shared_pair[1]
    )
    grad_normed_two = grad_normed_two + lax.dot_general(
        grad_logits, router_low, (((0,), (1,)), ((), ())), preferred_element_type=full
    )

    grad_normed_two = grad_normed_two + routed_grad
    scaled_two = grad_normed_two * gain_two
    grad_gain_two = jnp.sum(grad_normed_two * hidden * rstd_two, axis=0)
    grad_hidden = (
        grad_out
        + rstd_two * scaled_two
        - hidden * rstd_two**3 * jnp.mean(scaled_two * hidden, axis=-1, keepdims=True)
    )
    grad_branch = grad_hidden.astype(low)
    grads_two = jnp.concatenate(
        [
            dot_tn(grad_branch, attended).astype(low),
            dot_tn(normed_two, grad_shared_gate).astype(low),
            dot_tn(normed_two, grad_shared_up).astype(low),
            dot_tn(cotangent, shared_hidden).astype(low),
        ],
        axis=1,
    )
    units = grads_two.shape[1] // 128
    first = 3 * units // 8
    summed_two = scatter_sum(
        grid, grads_two, ((units - 2 * first) * 128, first * 128, first * 128)
    ).astype(full)

    grad_attended = dot_nn(grad_branch, turned_out).astype(low).reshape(split_shape)
    probs = jnp.exp(attention_scores() - log_total)
    grad_probs = jnp.einsum("qhd,khd->hqk", grad_attended, value, preferred_element_type=full)
    grad_scores = (
        probs * (grad_probs - jnp.sum(probs * grad_probs, axis=-1, keepdims=True))
    ).astype(low)
    grad_query = (
        jnp.einsum("hqk,khd->qhd", grad_scores, key_rot, preferred_element_type=full) * scaling
    )
    grad_key = (
        jnp.einsum("hqk,qhd->khd", grad_scores, query, preferred_element_type=full) * scaling
    )
    grad_value = jnp.einsum(
        "hqk,qhd->khd", probs.astype(low), grad_attended, preferred_element_type=full
    )
    grad_projected = [
        part.reshape(tokens, model_width).astype(low)
        for part in (
            unrotate(grad_query, cosine, sine_table),
            unrotate(grad_key, cosine, sine_table),
            grad_value,
        )
    ]
    grad_normed_one = (
        dot_nn(grad_projected[0], turned_in[0])
        + dot_nn(grad_projected[1], turned_in[1])
        + dot_nn(grad_projected[2], turned_in[2])
    )
    scaled_one = grad_normed_one * gain_one
    grad_gain_one = jnp.sum(grad_normed_one * inputs * rstd_one, axis=0)
    input_grad = (
        grad_hidden
        + rstd_one * scaled_one
        - inputs * rstd_one**3 * jnp.mean(scaled_one * inputs, axis=-1, keepdims=True)
    )
    grads_one = jnp.concatenate(
        [dot_tn(part, normed_one).astype(low) for part in grad_projected]
        + [
            grad_router.astype(low),
            jnp.stack([grad_gain_one, grad_gain_two], axis=1).astype(low),
            jnp.zeros((model_width, extra_width - experts - 2), low),
        ],
        axis=1,
    )
    units = grads_one.shape[1] // 128
    first = 3 * units // 8
    summed_one = scatter_sum(
        grid, grads_one, ((units - 2 * first) * 128, first * 128, first * 128)
    ).astype(full)

    output = (hidden + shared_result + collect(results_back)).astype(low)

    rows, inner, gated, grad_gate_rows, grad_up_rows = [
        jnp.concatenate(parts, axis=0) for parts in zip(*kept)
    ]
    grad_expert_down = dot_tn(inner, gated).astype(low)
    grad_expert_in = jnp.stack(
        [dot_tn(rows, grad_gate_rows).astype(low), dot_tn(rows, grad_up_rows).astype(low)], axis=0
    )
    summed_expert_in = lax.psum_scatter(
        grad_expert_in, "dp", scatter_dimension=1, tiled=True
    ).astype(full)[None]
    summed_expert_down = lax.psum_scatter(
        grad_expert_down, "dp", scatter_dimension=0, tiled=True
    ).astype(full)[None]

    summed_in = jnp.stack(
        [summed_one[:, m * model_width : (m + 1) * model_width].T for m in range(3)], axis=0
    )
    summed_extra = summed_one[:, 3 * model_width :]
    summed_router = summed_extra[:, :experts]
    summed_gains = summed_extra[:, experts : experts + 2].T
    summed_out = summed_two[:, :model_width].T
    summed_shared_in = jnp.stack(
        [summed_two[:, at + m * hidden_width : at + (m + 1) * hidden_width] for m in range(2)],
        axis=0,
    )
    summed_shared_down = summed_two[:, at + 2 * hidden_width :].T
    upd_attn_in = advance(
        attention_in, attention_in_momentum, attention_in_average, summed_in, rate_attention_in
    )
    upd_attn_out = advance(
        attention_out, attention_out_momentum, attention_out_average, summed_out, rate_attention_out
    )
    upd_shared_in = advance(
        shared_in, shared_in_momentum, shared_in_average, summed_shared_in, rate_shared_in
    )
    upd_shared_down = advance(
        shared_down, shared_down_momentum, shared_down_average, summed_shared_down, rate_shared_down
    )
    upd_router = advance(router, router_momentum, router_average, summed_router, rate_router)
    upd_gains = advance(
        norm_gains, norm_gains_momentum, norm_gains_average, summed_gains, rate_gains
    )
    upd_expert_in = advance(
        expert_in, expert_in_momentum, expert_in_average, summed_expert_in, rate_expert_in
    )
    upd_expert_down = advance(
        expert_down, expert_down_momentum, expert_down_average, summed_expert_down, rate_expert_down
    )
    return (
        output,
        input_grad,
        upd_attn_in[0],
        upd_attn_in[1],
        upd_attn_in[2],
        upd_attn_out[0],
        upd_attn_out[1],
        upd_attn_out[2],
        upd_shared_in[0],
        upd_shared_in[1],
        upd_shared_in[2],
        upd_shared_down[0],
        upd_shared_down[1],
        upd_shared_down[2],
        upd_router[0],
        upd_router[1],
        upd_router[2],
        upd_gains[0],
        upd_gains[1],
        upd_gains[2],
        upd_expert_in[0],
        upd_expert_in[1],
        upd_expert_in[2],
        upd_expert_down[0],
        upd_expert_down[1],
        upd_expert_down[2],
    )


def solution(mesh):
    in_specs = (
        P(("dp", "expert"), None),
        P(("dp", "expert")),
        P(("dp", "expert")),
        P(("dp", "expert"), None),
        P(("dp", "expert"), None),
        P(None, None, ("dp", "expert")),
        P(None, None, ("dp", "expert")),
        P(None, None, ("dp", "expert")),
        P(None, ("dp", "expert")),
        P(None, ("dp", "expert")),
        P(None, ("dp", "expert")),
        P(None, ("dp", "expert"), None),
        P(None, ("dp", "expert"), None),
        P(None, ("dp", "expert"), None),
        P(None, ("dp", "expert")),
        P(None, ("dp", "expert")),
        P(None, ("dp", "expert")),
        P(("dp", "expert"), None),
        P(("dp", "expert"), None),
        P(("dp", "expert"), None),
        P(None, ("dp", "expert")),
        P(None, ("dp", "expert")),
        P(None, ("dp", "expert")),
        P("expert", None, "dp", None),
        P("expert", None, "dp", None),
        P("expert", None, "dp", None),
        P("expert", "dp", None),
        P("expert", "dp", None),
        P("expert", "dp", None),
    )
    out_specs = (
        P(("dp", "expert"), None),
        P(("dp", "expert"), None),
        P(None, None, ("dp", "expert")),
        P(None, None, ("dp", "expert")),
        P(None, None, ("dp", "expert")),
        P(None, ("dp", "expert")),
        P(None, ("dp", "expert")),
        P(None, ("dp", "expert")),
        P(None, ("dp", "expert"), None),
        P(None, ("dp", "expert"), None),
        P(None, ("dp", "expert"), None),
        P(None, ("dp", "expert")),
        P(None, ("dp", "expert")),
        P(None, ("dp", "expert")),
        P(("dp", "expert"), None),
        P(("dp", "expert"), None),
        P(("dp", "expert"), None),
        P(None, ("dp", "expert")),
        P(None, ("dp", "expert")),
        P(None, ("dp", "expert")),
        P("expert", None, "dp", None),
        P("expert", None, "dp", None),
        P("expert", None, "dp", None),
        P("expert", "dp", None),
        P("expert", "dp", None),
        P("expert", "dp", None),
    )
    return jax.shard_map(local, mesh=mesh, in_specs=in_specs, out_specs=out_specs, check_vma=False)
```

```python
import functools

import jax
import jax.numpy as jnp
from jax import lax
from jax.experimental import pallas as pl
from jax.experimental.pallas import tpu as pltpu
from jax.sharding import PartitionSpec as P

HD = 128
STEP = 4


eps_norm = 1e-06
theta_base = 10000.0
momentum_decay = 0.9
mask_fill = -1e30
rate_attention_in = 2e-05
rate_attention_out = 0.002
rate_shared_in = 3e-05
rate_shared_down = 0.0002
rate_router = 1.5e-05
rate_gains = 0.0002
rate_expert_in = 0.0004
rate_expert_down = 0.008


def rope_tables(length, head_width):
    half_width = head_width // 2
    frequency = theta_base ** (-(jnp.arange(half_width, dtype=jnp.float32) * 2.0 / head_width))
    angles = jnp.arange(length, dtype=jnp.float32)[:, None] * frequency[None, :]
    cosine, sine_table = jnp.cos(angles), jnp.sin(angles)
    return (
        jnp.concatenate([cosine, cosine], axis=1),
        jnp.concatenate([-sine_table, sine_table], axis=1),
    )


def allowed_keys(length, keep_flags):
    amount = keep_flags.shape[0]
    position = jnp.arange(amount)
    causal = position[None, :] <= position[:, None]
    usable = (position < length) & (keep_flags == 1)
    return causal & (usable[None, :] | (position[None, :] == position[:, None]))


def silu_parts(values):
    logistic = jax.nn.sigmoid(values)
    return (values * logistic, logistic * (1.0 + values * (1.0 - logistic)))


def advance(weight, moment, average, gradient, step_rate):
    moment_new = momentum_decay * moment + gradient
    weight_new = weight - step_rate * (gradient + momentum_decay * moment_new)
    average_new = average + (weight_new - average) / (STEP + 1)
    return (weight_new, moment_new, average_new)


def dot_nn(a, b):
    return lax.dot_general(a, b, (((1,), (0,)), ((), ())), preferred_element_type=jnp.float32)


def dot_nt(a, b):
    return lax.dot_general(a, b, (((1,), (1,)), ((), ())), preferred_element_type=jnp.float32)


def dot_tn(a, b):
    return lax.dot_general(a, b, (((0,), (0,)), ((), ())), preferred_element_type=jnp.float32)


PLANE = 4
MESH = pl.DeviceIdType.MESH


class Spot:
    def __init__(self, line):
        here = lax.axis_index("expert")
        self.line = line
        self.core = lax.axis_index("dp")
        self.at = lax.div(here, PLANE)
        rest = lax.rem(here, PLANE)
        self.y, self.x = lax.div(rest, 2), lax.rem(rest, 2)

    def chip(self, at, y, x):
        return (self.core, at * PLANE + y * 2 + x)

    def around(self, amount):
        return lax.rem(self.at + amount + self.line, self.line)

    def partner(self, way):
        if way == "core":
            return (1 - self.core, self.at * PLANE + self.y * 2 + self.x)
        if way == "x":
            return self.chip(self.at, self.y, 1 - self.x)
        if way == "y":
            return self.chip(self.at, 1 - self.y, self.x)
        return self.chip(self.around(1 if way == "up" else -1), self.y, self.x)


def meet(spot):
    barrier = pltpu.get_barrier_semaphore()
    for way in ("core", "x", "y", "up", "down"):
        pl.semaphore_signal(barrier, inc=1, device_id=spot.partner(way), device_id_type=MESH)
    pl.semaphore_wait(barrier, 5)


class Moves:
    def __init__(self, spot, send_sems, recv_sems, local_sems):
        self.spot, self.send_sems, self.recv_sems = spot, send_sems, recv_sems
        self.local_sems = local_sems
        self.made, self.kept, self.loose = 0, 0, []

    def start(self, source, target, way, later=False):
        copy = pltpu.make_async_remote_copy(
            src_ref=source,
            dst_ref=target,
            send_sem=self.send_sems.at[self.made],
            recv_sem=self.recv_sems.at[self.made],
            device_id=self.spot.partner(way),
            device_id_type=MESH,
        )
        self.made += 1
        copy.start()
        if later:
            self.loose.append(copy)
        return copy

    def keep(self, source, target, later=False):
        copy = pltpu.make_async_copy(source, target, self.local_sems.at[self.kept])
        self.kept += 1
        copy.start()
        if later:
            self.loose.append(copy)
        return copy

    def finish(self):
        for copy in self.loose:
            copy.wait()


def in_turn(chains):
    while chains:
        left = []
        for chain in chains:
            try:
                next(chain)
                left.append(chain)
            except StopIteration:
                pass
        chains = left


def line_chain(moves, own, whole):
    line = moves.spot.line
    half, rest = line // 2, (line - 1) // 2
    moves.keep(own, whole.at[0], later=True)
    up, down = own, own
    for i in range(1, half + 1):
        rising = moves.start(up, whole.at[i], "up")
        if i <= rest:
            falling = moves.start(down, whole.at[line - i], "down")
        yield
        rising.wait()
        up = whole.at[i]
        if i <= rest:
            falling.wait()
            down = whole.at[line - i]


def swap_chain(moves, own, whole, way):
    core = moves.spot.core
    copy = moves.start(own, whole.at[core], way)
    yield
    copy.wait()
    moves.start(whole.at[core], whole.at[core], "core", later=True)


def core_chain(moves, own, whole):
    core = moves.spot.core
    moves.keep(own, whole.at[core], later=True)
    moves.start(own, whole.at[core], "core", later=True)
    yield


def dense_chain(moves, whole, columns, order):
    spot = moves.spot
    half, rest = spot.line // 2, (spot.line - 1) // 2
    everything = slice(None)
    held = {"z": spot.at, "y": spot.y, "x": spot.x}

    def region(**other):
        at = dict(held, **other)
        return whole.at[spot.core, at["z"], at["y"], at["x"], everything, columns]

    def forward(part):
        moves.start(part, part, "core", later=True)

    for stage, dim in enumerate(order):
        if dim == "z":
            up = down = None
            for i in range(1, half + 1):
                part = region(z=spot.around(1 - i))
                up = moves.start(part, part, "up")
                if i <= rest:
                    part = region(z=spot.around(i - 1))
                    down = moves.start(part, part, "down")
                if stage == 0 and i == 1:
                    forward(region())
                yield
                up.wait()
                forward(region(z=spot.around(-i)))
                if i <= rest:
                    down.wait()
                    forward(region(z=spot.around(i)))
        else:
            part = region()
            copy = moves.start(part, part, dim)
            if stage == 0:
                forward(region())
            yield
            copy.wait()
            forward(region(**{dim: 1 - held[dim]}))
        held[dim] = everything


ORDERS = ("xyz", "yzx", "zxy", "zyx")


def first_kernel(line, plans, *refs):
    count = len(plans)
    shards, refs = refs[:count], refs[count:]
    grads, gate, up, down = refs[:4]
    results, refs = refs[4 : 4 + count], refs[4 + count :]
    line_grads, gates, ups, downs = refs[0], refs[1:4], refs[4:5], refs[5:8]
    refs = refs[8:]
    wholes, refs = refs[:count], refs[count:]
    spot = Spot(line)
    meet(spot)
    moves = Moves(spot, *refs)
    loads = [
        moves.keep(shards[n], wholes[n].at[spot.core, spot.at, spot.y, spot.x])
        for n in range(count)
    ]
    for copy in loads:
        copy.wait()
    chains = []
    for n, plan in enumerate(plans):
        start = 0
        for order, width in plan:
            columns = slice(start, start + width)
            chains.append(dense_chain(moves, wholes[n], columns, ORDERS[order]))
            start += width
    chains.append(line_chain(moves, grads, line_grads))
    for own, whole in ((gate, gates), (down, downs)):
        chains.append(swap_chain(moves, own, whole[1], "x"))
        chains.append(swap_chain(moves, own, whole[2], "y"))
    for own, whole in ((gate, gates), (up, ups), (down, downs)):
        chains.append(core_chain(moves, own, whole[0]))
    in_turn(chains)
    moves.finish()
    stores = [moves.keep(wholes[n], results[n]) for n in range(count)]
    for copy in stores:
        copy.wait()


def hbm(count):
    return [pl.BlockSpec(memory_space=pl.ANY)] * count


def semaphores(remote, local):
    return [
        pltpu.SemaphoreType.DMA((remote,)),
        pltpu.SemaphoreType.DMA((remote,)),
        pltpu.SemaphoreType.DMA((local,)),
    ]


def both_halves(array):
    return jax.ShapeDtypeStruct((2,) + array.shape, array.dtype)


def first_exchange(experts, shards, plans, grads, gate, up, down):
    line = experts // PLANE
    count = len(shards)
    chains = sum(len(plan) for plan in plans)
    remote = chains * (2 * line + 3) + line + 4 * 2 + 3
    out_shape = [
        jax.ShapeDtypeStruct((2, line, 2, 2) + shard.shape, shard.dtype) for shard in shards
    ]
    out_shape += [jax.ShapeDtypeStruct((line,) + grads.shape, grads.dtype)]
    out_shape += [both_halves(gate)] * 3 + [both_halves(up)] + [both_halves(down)] * 3
    out = pl.pallas_call(
        functools.partial(first_kernel, line, plans),
        out_shape=out_shape,
        in_specs=hbm(count + 4),
        out_specs=hbm(count + 8),
        scratch_shapes=[
            pltpu.VMEM((2, line, 2, 2) + shard.shape, shard.dtype) for shard in shards
        ]
        + semaphores(remote, 2 * count + 4),
        compiler_params=pltpu.CompilerParams(
            collective_id=1, has_side_effects=True, vmem_limit_bytes=48 * 1024 * 1024
        ),
    )(*shards, grads, gate, up, down)
    return out[:count], out[count], out[count + 1 : count + 4], out[count + 4], out[count + 5 :]


def second_kernel(line, *refs):
    rows, up, gate_x, down_x, down_y = refs[:5]
    line_rows, up_x, up_y, far_gate, far_up, far_down = refs[5:11]
    spot = Spot(line)
    meet(spot)
    moves = Moves(spot, *refs[11:])
    core = spot.core
    half = down_x.shape[1] // 2

    def far_up_chain():
        yield
        copy = moves.start(up_y.at[core], far_up.at[core], "x")
        yield
        copy.wait()
        moves.start(far_up.at[core], far_up.at[core], "core", later=True)

    def part_chain(source, whole, part, way):
        copy = moves.start(source.at[core, part], whole.at[core, part], way)
        yield
        copy.wait()
        moves.start(whole.at[core, part], whole.at[core, part], "core", later=True)

    everything = slice(None)
    in_turn(
        [
            swap_chain(moves, up, up_x, "x"),
            swap_chain(moves, up, up_y, "y"),
            line_chain(moves, rows, line_rows),
            far_up_chain(),
            part_chain(down_y, far_down, slice(half, 2 * half), "x"),
            part_chain(down_x, far_down, slice(0, half), "y"),
            part_chain(gate_x, far_gate, everything, "y"),
        ]
    )
    moves.finish()


def second_exchange(experts, rows, up, gate_x, down_x, down_y):
    line = experts // PLANE
    out_shape = [jax.ShapeDtypeStruct((line,) + rows.shape, rows.dtype)]
    out_shape += [both_halves(up)] * 2
    out_shape += [jax.ShapeDtypeStruct(array.shape, array.dtype) for array in (gate_x, gate_x, down_x)]
    return pl.pallas_call(
        functools.partial(second_kernel, line),
        out_shape=out_shape,
        in_specs=hbm(5),
        out_specs=hbm(6),
        scratch_shapes=semaphores(line + 12, 1),
        compiler_params=pltpu.CompilerParams(collective_id=3, has_side_effects=True),
    )(rows, up, gate_x, down_x, down_y)


def third_kernel(line, *refs):
    low, full = jnp.bfloat16, jnp.float32
    grads = refs[0]
    kept = [refs[1 + 5 * q : 6 + 5 * q] for q in range(PLANE)]
    refs = refs[1 + 5 * PLANE :]
    total = refs[0]
    owns = [refs[1 + 3 * q : 4 + 3 * q] for q in range(PLANE - 1)]
    refs = refs[1 + 3 * (PLANE - 1) :]
    crossed = [refs[3 * q : 3 + 3 * q] for q in range(PLANE - 1)]
    refs = refs[3 * (PLANE - 1) :]
    far_in, refs = refs[:4], refs[4:]
    boxes, extra, refs = refs[0], refs[1:3], refs[3:]
    loaded, refs = [refs[:5], refs[5:10]], refs[10:]
    results, refs = [refs[:6], refs[6:12]], refs[12:]
    far_box, down_grad, total_box, refs = refs[:3], refs[3], refs[4], refs[5:]
    spot = Spot(line)
    meet(spot)
    moves = Moves(spot, *refs)
    half, rest = line // 2, (line - 1) // 2
    order = (3, 1, 2, 0)
    loads = {}

    def load(n):
        loads[n] = [moves.keep(kept[order[n]][i], loaded[n % 2][i]) for i in range(5)]

    def add(target, source):
        target[...] = (target[...].astype(full) + source[...].astype(full)).astype(low)

    def sums(way, sign, steps):
        at = lambda i: i if sign > 0 else (line - i) % line
        source = grads.at[at(steps)]
        box = extra[0 if sign > 0 else 1]
        for i in range(steps, 0, -1):
            copy = moves.start(source, boxes.at[at(i) - 1], way)
            if i > 1:
                part = moves.keep(grads.at[at(i - 1)], box)
            yield
            copy.wait()
            source = boxes.at[at(i) - 1]
            if i > 1:
                part.wait()
                add(source, box)
            else:
                total_box[...] += source[...].astype(full)

    own_part = moves.keep(grads.at[0], extra[0])
    load(0)
    own_part.wait()
    total_box[...] = extra[0][...].astype(full)

    rows_half = results[0][0].shape[0]
    down_half = results[0][2].shape[0]
    sent = {}

    def weights(n):
        if n + 1 < PLANE:
            load(n + 1)
        for copy in loads[n]:
            copy.wait()
        rows, inner, gated, grad_gate, grad_up = loaded[n % 2]
        buffers = results[n % 2]
        if n == 3:
            for copy in sent[1]:
                copy.wait()
        down_grad[...] = dot_tn(inner[...], gated[...]).astype(low)
        for which in (1, 0):
            place = jnp.bitwise_xor(spot.core, which)
            gate_out, up_out, down_out = buffers[3 * which : 3 * which + 3]
            part = rows[:, pl.ds(pl.multiple_of(place * rows_half, 128), rows_half)]
            gate_out[...] = dot_tn(part, grad_gate[...]).astype(low)
            up_out[...] = dot_tn(part, grad_up[...]).astype(low)
            down_out[...] = down_grad[pl.ds(pl.multiple_of(place * down_half, 16), down_half), :]
            q = order[n]
            targets = far_box if q == PLANE - 1 else crossed[q]
            if which:
                sent[n] = [
                    moves.start(buffers[3 + i], targets[i], "core") for i in range(3)
                ]
            elif q < PLANE - 1:
                sent[n] += [moves.keep(buffers[i], owns[q][i]) for i in range(3)]

    def far():
        for copy in sent[0]:
            copy.wait()
        mine = results[0][:3]
        for i in range(3):
            add(far_box[i], mine[i])
        edge = down_half // 2
        moves.start(far_box[0], far_in[0], "y", later=True)
        moves.start(far_box[1], far_in[1], "x", later=True)
        moves.start(far_box[2].at[pl.ds(0, edge)], far_in[2], "y", later=True)
        moves.start(far_box[2].at[pl.ds(edge, edge)], far_in[3], "x", later=True)

    chains = [sums("down", 1, half), sums("up", -1, rest)]
    for chain in chains:
        next(chain, None)
    weights(0)
    weights(1)
    far()
    weights(2)
    for chain in chains:
        next(chain, None)
    weights(3)
    in_turn(chains)
    store = moves.keep(total_box, total)
    for n in (2, 3):
        for copy in sent[n]:
            copy.wait()
    store.wait()
    moves.finish()


def third_exchange(experts, grads, kept):
    line = experts // PLANE
    low = jnp.bfloat16
    rows, inner = kept[0][0], kept[0][1]
    width, hidden_width = rows.shape[1], inner.shape[1]
    half, down_half = width // 2, hidden_width // 2
    pieces = [(half, hidden_width), (half, hidden_width), (down_half, width)]
    far = pieces[:2] + [(down_half // 2, width)] * 2
    shape = lambda size, dtype=low: jax.ShapeDtypeStruct(size, dtype)
    out = pl.pallas_call(
        functools.partial(third_kernel, line),
        out_shape=[shape(grads.shape[1:], jnp.float32)]
        + [shape(size) for size in pieces * (2 * (PLANE - 1))]
        + [shape(size) for size in far],
        in_specs=hbm(1 + 5 * PLANE),
        out_specs=hbm(1 + 6 * (PLANE - 1) + 4),
        scratch_shapes=[pltpu.VMEM((line - 1,) + grads.shape[1:], low)]
        + [pltpu.VMEM(grads.shape[1:], low)] * 2
        + [pltpu.VMEM(array.shape, low) for array in kept[0]] * 2
        + [pltpu.VMEM(size, low) for size in pieces * 4]
        + [pltpu.VMEM(size, low) for size in pieces]
        + [pltpu.VMEM((hidden_width, width), low), pltpu.VMEM(grads.shape[1:], jnp.float32)]
        + semaphores(line + 3 * PLANE + 4, line + 8 * PLANE + 2),
        compiler_params=pltpu.CompilerParams(
            collective_id=4, has_side_effects=True, vmem_limit_bytes=62 * 1024 * 1024
        ),
    )(grads, *[array for parts in kept for array in parts])
    total, out = out[0], out[1:]
    count = 3 * (PLANE - 1)
    triples = lambda arrays: [arrays[3 * q : 3 * q + 3] for q in range(PLANE - 1)]
    return total, triples(out[:count]), triples(out[count : 2 * count]), out[2 * count :]


def sum_kernel(line, plans, ways, *refs):
    count = len(plans)
    given = sum(len(order) for plan in plans for order in plan)
    grads, refs = refs[:given], refs[given:]
    moved, refs = refs[: len(ways)], refs[len(ways) :]
    sums, refs = refs[:count], refs[count:]
    arrived, refs = refs[: len(ways)], refs[len(ways) :]
    kept, refs = refs[: 3 * count], refs[3 * count :]
    core_in, refs = refs[: 3 * count], refs[3 * count :]
    first_in, refs = refs[: 3 * count], refs[3 * count :]
    second_in, refs = refs[: 3 * count], refs[3 * count :]
    third_in, refs = refs[: 3 * count], refs[3 * count :]
    spot = Spot(line)
    meet(spot)
    moves = Moves(spot, *refs)
    half, rest = line // 2, (line - 1) // 2
    everything = slice(None)
    orders = ("xyz", "yzx", "zxy")

    loads, swaps = [], []
    at = 0
    for n, plan in enumerate(plans):
        for o, pieces in enumerate(plan):
            mine, theirs = [], []
            start = 0
            for first, width in pieces:
                ref = grads[at]
                source = slice(first, first + width)
                target = slice(start, start + width)
                mine.append(
                    moves.keep(
                        ref.at[spot.core, :, :, :, :, source],
                        kept[3 * n + o].at[:, :, :, :, target],
                    )
                )
                theirs.append(
                    moves.start(
                        ref.at[1 - spot.core, :, :, :, :, source],
                        core_in[3 * n + o].at[:, :, :, :, target],
                        "core",
                    )
                )
                at += 1
                start += width
            loads.append(mine)
            swaps.append(theirs)

    for way, source, target in zip(ways, moved, arrived):
        moves.start(source, target, way, later=True)

    def add(target, source):
        lead = target.shape[:-2]
        total = 1
        for extent in lead:
            total *= extent

        def one(i, carry):
            index = []
            for extent in reversed(lead):
                index.insert(0, lax.rem(i, extent))
                i = lax.div(i, extent)
            index = tuple(index)
            target[index] = (
                target[index].astype(jnp.float32) + source[index].astype(jnp.float32)
            ).astype(target.dtype)
            return carry

        lax.fori_loop(0, total, one, 0)

    def chain(n, o):
        buffer = kept[3 * n + o]
        mine, theirs = loads[3 * n + o], swaps[3 * n + o]
        for copy in mine:
            copy.wait()
        for copy in theirs:
            copy.wait()
        add(buffer, core_in[3 * n + o])
        inbox = [first_in[3 * n + o], second_in[3 * n + o], third_in[3 * n + o]]
        held = {"z": everything, "y": everything, "x": everything}

        def region(**other):
            at = dict(held, **other)
            return buffer.at[at["z"], at["y"], at["x"]]

        for stage, dim in enumerate(orders[o]):
            box = inbox[stage]
            if dim == "z":
                up = down = None
                for i in range(half, 0, -1):
                    down = moves.start(region(z=spot.around(-i)), box.at[i - 1], "down")
                    if i <= rest:
                        up = moves.start(region(z=spot.around(i)), box.at[half + i - 1], "up")
                    yield
                    down.wait()
                    add(region(z=spot.around(1 - i)), box.at[i - 1])
                    if i <= rest:
                        up.wait()
                        add(region(z=spot.around(i - 1)), box.at[half + i - 1])
                held[dim] = spot.at
            else:
                own = spot.y if dim == "y" else spot.x
                copy = moves.start(region(**{dim: 1 - own}), box, dim)
                yield
                copy.wait()
                held[dim] = own
                add(region(), box)
        start = sum(sum(width for _, width in pieces) for pieces in plans[n][:o])
        width = sum(width for _, width in plans[n][o])
        result = moves.keep(region(), sums[n].at[:, slice(start, start + width)])
        yield
        result.wait()

    in_turn([chain(n, o) for n in range(count) for o in range(3)])
    moves.finish()


def sum_all(experts, grads, plans, moved, ways):
    line = experts // PLANE
    half, rest = line // 2, (line - 1) // 2
    rows = grads[0].shape[0] // (2 * experts)
    dtype = grads[0].dtype
    operands, kernel_plans, shapes = [], [], []
    boxes = [[], [], [], [], []]
    for plan in plans:
        kernel_plan = []
        for o, pieces in enumerate(plan):
            for which, _, _ in pieces:
                array = grads[which]
                operands.append(array.reshape(2, line, 2, 2, rows, array.shape[1]))
            kernel_plan.append(tuple((first, width) for _, first, width in pieces))
            width = sum(width for _, _, width in pieces)
            steps = half + rest
            block = (rows, width)
            boxes[0].append((line, 2, 2) + block)
            boxes[1].append((line, 2, 2) + block)
            if o == 0:
                inboxes = [(line, 2), (line,), (steps,)]
            elif o == 1:
                inboxes = [(line, 2), (steps, 2), ()]
            else:
                inboxes = [(steps, 2, 2), (2,), ()]
            for i, lead in enumerate(inboxes):
                boxes[2 + i].append(lead + block)
        kernel_plans.append(tuple(kernel_plan))
        total = sum(width for pieces in kernel_plan for _, width in pieces)
        shapes.append(jax.ShapeDtypeStruct((rows, total), dtype))
    count = len(plans)
    number = len(operands) + 3 * count * (line + 1) + len(moved)
    shapes += [jax.ShapeDtypeStruct(array.shape, array.dtype) for array in moved]
    return pl.pallas_call(
        functools.partial(sum_kernel, line, tuple(kernel_plans), ways),
        out_shape=shapes,
        in_specs=hbm(len(operands) + len(moved)),
        out_specs=hbm(count + len(moved)),
        scratch_shapes=[pltpu.VMEM(shape, dtype) for kind in boxes for shape in kind]
        + semaphores(number, len(operands) + 3 * count),
        compiler_params=pltpu.CompilerParams(
            collective_id=2, has_side_effects=True, vmem_limit_bytes=60 * 1024 * 1024
        ),
    )(*operands, *moved)


def turn(values, cosine, sine_table):
    return values * cosine + pltpu.roll(values, HD // 2, 1) * sine_table


def turn_back(values, cosine, sine_table):
    return values * cosine - pltpu.roll(values, HD // 2, 1) * sine_table


def probabilities(query, key, bias):
    scores = dot_nt(query, key) * HD ** (-0.5) + bias
    exps = jnp.exp(scores - jnp.max(scores, axis=1, keepdims=True))
    return exps / jnp.sum(exps, axis=1, keepdims=True)


def attend_kernel(
    steps,
    normed,
    query_weight,
    key_weight,
    value_weight,
    out_weight,
    bias,
    cosine,
    sine_table,
    inputs,
    gain,
    query_out,
    key_out,
    value_out,
    attended_out,
    hidden_out,
    normed_out,
):
    step = pl.program_id(0)
    low = jnp.bfloat16
    n1 = normed[...]
    cos, sin = cosine[...], sine_table[...]
    query = dot_nt(n1, query_weight[...])
    key = dot_nt(n1, key_weight[...])
    value_out[...] = dot_nt(n1, value_weight[...]).astype(low)
    for part in range(query.shape[1] // HD):
        columns = slice(part * HD, (part + 1) * HD)
        q = turn(query[:, columns], cos, sin).astype(low)
        k = turn(key[:, columns], cos, sin).astype(low)
        query_out[:, columns] = q
        key_out[:, columns] = k
        probs = probabilities(q, k, bias[...])
        attended_out[:, columns] = dot_nn(probs.astype(low), value_out[:, columns]).astype(low)
    branch = dot_nt(attended_out[...], out_weight[...])

    @pl.when(step == 0)
    def _():
        hidden_out[...] = inputs[...].astype(jnp.float32) + branch

    @pl.when(step > 0)
    def _():
        hidden_out[...] += branch

    @pl.when(step == steps - 1)
    def _():
        hidden = hidden_out[...]
        rstd = lax.rsqrt(jnp.mean(hidden * hidden, axis=1, keepdims=True) + eps_norm)
        normed_out[...] = (hidden * rstd * gain[...]).astype(low)


def attend(normed, weights, out_weight, bias, cosine, sine_table, inputs, gain):
    tokens, width = normed.shape
    group = 2 * HD
    steps = width // group
    low = jnp.bfloat16
    whole = lambda *shape: pl.BlockSpec(shape, lambda i: (0,) * len(shape))
    columns = pl.BlockSpec((tokens, group), lambda i: (0, i))
    return pl.pallas_call(
        functools.partial(attend_kernel, steps),
        grid=(steps,),
        in_specs=[whole(tokens, width)]
        + [pl.BlockSpec((group, width), lambda i, m=m: (i, m)) for m in range(3)]
        + [
            pl.BlockSpec((width, group), lambda i: (0, i)),
            whole(tokens, tokens),
            whole(tokens, HD),
            whole(tokens, HD),
            whole(tokens, width),
            whole(1, width),
        ],
        out_specs=[columns] * 4 + [whole(tokens, width)] * 2,
        out_shape=[jax.ShapeDtypeStruct((tokens, width), low)] * 4
        + [
            jax.ShapeDtypeStruct((tokens, width), jnp.float32),
            jax.ShapeDtypeStruct((tokens, width), low),
        ],
        compiler_params=pltpu.CompilerParams(vmem_limit_bytes=48 * 1024 * 1024),
        cost_estimate=pl.CostEstimate(
            flops=8 * tokens * width * width, bytes_accessed=20 * width * width, transcendentals=0
        ),
    )(normed, weights, weights, weights, out_weight, bias, cosine, sine_table, inputs, gain)


def attend_back_kernel(
    grad_branch,
    normed,
    query_in,
    key_in,
    value_in,
    attended_in,
    query_weight,
    key_weight,
    value_weight,
    out_weight,
    bias,
    cosine,
    sine_table,
    grad_query_weight,
    grad_key_weight,
    grad_value_weight,
    grad_out_weight,
    grad_normed,
    grads,
):
    step = pl.program_id(0)
    low = jnp.bfloat16
    da = grad_branch[...]
    n1 = normed[...]
    cos, sin = cosine[...], sine_table[...]
    scaling = HD ** (-0.5)
    group = query_in.shape[1]
    grad_out_weight[...] = dot_tn(da, attended_in[...]).astype(low)
    grad_attended = dot_nn(da, out_weight[...]).astype(low)
    for part in range(group // HD):
        columns = slice(part * HD, (part + 1) * HD)
        q, k, v = query_in[:, columns], key_in[:, columns], value_in[:, columns]
        do = grad_attended[:, columns]
        probs = probabilities(q, k, bias[...])
        grad_probs = dot_nt(do, v)
        grad_scores = probs * (grad_probs - jnp.sum(probs * grad_probs, axis=1, keepdims=True))
        grad_scores = grad_scores.astype(low)
        grads[0, :, columns] = turn_back(dot_nn(grad_scores, k) * scaling, cos, sin).astype(low)
        grads[1, :, columns] = turn_back(dot_tn(grad_scores, q) * scaling, cos, sin).astype(low)
        grads[2, :, columns] = dot_tn(probs.astype(low), do).astype(low)
    grad_query_weight[...] = dot_tn(grads[0], n1).astype(low)
    grad_key_weight[...] = dot_tn(grads[1], n1).astype(low)
    grad_value_weight[...] = dot_tn(grads[2], n1).astype(low)
    total = (
        dot_nn(grads[0], query_weight[...])
        + dot_nn(grads[1], key_weight[...])
        + dot_nn(grads[2], value_weight[...])
    )

    @pl.when(step == 0)
    def _():
        grad_normed[...] = total

    @pl.when(step > 0)
    def _():
        grad_normed[...] += total


def attend_back(
    grad_branch, normed, query, key, value, attended, weights, out_weight, bias, cosine, sine_table
):
    tokens, width = normed.shape
    group = 2 * HD
    steps = width // group
    low = jnp.bfloat16
    whole = lambda *shape: pl.BlockSpec(shape, lambda i: (0,) * len(shape))
    columns = pl.BlockSpec((tokens, group), lambda i: (0, i))
    return pl.pallas_call(
        attend_back_kernel,
        grid=(steps,),
        in_specs=[whole(tokens, width)] * 2
        + [columns] * 4
        + [pl.BlockSpec((group, width), lambda i, m=m: (i, m)) for m in range(3)]
        + [
            pl.BlockSpec((width, group), lambda i: (0, i)),
            whole(tokens, tokens),
            whole(tokens, HD),
            whole(tokens, HD),
        ],
        out_specs=[pl.BlockSpec((group, width), lambda i: (i, 0))] * 3
        + [pl.BlockSpec((width, group), lambda i: (0, i)), whole(tokens, width)],
        out_shape=[jax.ShapeDtypeStruct((width, width), low)] * 4
        + [jax.ShapeDtypeStruct((tokens, width), jnp.float32)],
        scratch_shapes=[pltpu.VMEM((3, tokens, group), low)],
        compiler_params=pltpu.CompilerParams(vmem_limit_bytes=48 * 1024 * 1024),
        cost_estimate=pl.CostEstimate(
            flops=16 * tokens * width * width, bytes_accessed=40 * width * width, transcendentals=0
        ),
    )(
        grad_branch,
        normed,
        query,
        key,
        value,
        attended,
        weights,
        weights,
        weights,
        out_weight,
        bias,
        cosine,
        sine_table,
    )


def expert_kernel(
    place,
    rows_in,
    grads_in,
    slots_in,
    gates_in,
    gate_weight,
    up_weight,
    down_weight,
    *refs,
    slots,
    add,
):
    if add:
        grad_before, result_before, *refs = refs
    (
        grad_total,
        result_total,
        rows_out,
        inner_out,
        gated_out,
        grad_gate_out,
        grad_up_out,
    ) = refs
    low, full = jnp.bfloat16, jnp.float32
    group, tokens = slots_in.shape[0], slots_in.shape[2]
    width = rows_in.shape[2]

    slot_ids = lax.broadcasted_iota(jnp.int32, (slots, tokens), 0).astype(full)
    places = [slots_in[r] == slot_ids for r in range(group)]
    hot = [here.astype(low) for here in places]
    gate_col = jnp.concatenate(
        [
            jnp.sum(jnp.where(places[r], gates_in[r], 0.0), axis=1, keepdims=True)
            for r in range(group)
        ],
        axis=0,
    )
    for r in range(group):
        rows_out[r * slots : (r + 1) * slots, :] = dot_nn(hot[r], rows_in[r, :tokens]).astype(low)
    grad_rows = jnp.concatenate(
        [dot_nn(hot[r], grads_in[r, :tokens]) for r in range(group)], axis=0
    )
    gated = (grad_rows * gate_col).astype(low)
    gated_out[...] = gated
    rows = rows_out[...]
    gate_rows = dot_nn(rows, gate_weight[...])
    up_rows = dot_nn(rows, up_weight[...])
    logistic = jax.nn.sigmoid(gate_rows)
    silu_rows = gate_rows * logistic
    slope_rows = logistic * (1.0 + gate_rows * (1.0 - logistic))
    inner = (silu_rows * up_rows).astype(low)
    inner_out[...] = inner
    grad_inner = dot_nt(gated, down_weight[...])
    grad_gate_rows = (grad_inner * up_rows * slope_rows).astype(low)
    grad_up_rows = (grad_inner * silu_rows).astype(low)
    grad_gate_out[...] = grad_gate_rows
    grad_up_out[...] = grad_up_rows
    sent_grads = (
        dot_nt(grad_gate_rows, gate_weight[...]) + dot_nt(grad_up_rows, up_weight[...])
    ).astype(low)
    result_rows = dot_nn(inner, down_weight[...])
    gate_grad = jnp.sum(result_rows * grad_rows, axis=1, keepdims=True)
    sent_results = (result_rows * gate_col).astype(low)
    experts = grad_total.shape[1] - tokens
    for r in range(group):
        part = slice(r * slots, (r + 1) * slots)
        grad_sum = dot_tn(hot[r], sent_grads[part])
        result_sum = dot_tn(hot[r], sent_results[part])
        token_grad = jnp.sum(jnp.where(places[r], gate_grad[part], 0.0), axis=0, keepdims=True)
        words = jnp.concatenate(
            split_words(token_grad) + [jnp.zeros((1, width - 3 * tokens), low)], axis=1
        )
        expert_ids = lax.broadcasted_iota(jnp.int32, (experts, width), 0)
        words = jnp.where(expert_ids == place[0], words.astype(full), 0.0)
        if add:
            grad_sum = grad_sum + grad_before[r, :tokens].astype(full)
            result_sum = result_sum + result_before[r].astype(full)
            words = words + grad_before[r, tokens:].astype(full)
        grad_total[r, :tokens] = grad_sum.astype(low)
        grad_total[r, tokens:] = words.astype(low)
        result_total[r] = result_sum.astype(low)


def run_expert(place, rows, grads, slot_rows, gate_rows, weights, before, slots):
    line, _, width = rows.shape
    tokens = slot_rows.shape[2]
    low = jnp.bfloat16
    hidden_width = weights[0].shape[1]
    group = 2
    steps = line // group
    whole = lambda array: pl.BlockSpec(
        array.shape, lambda i, place: (0,) * array.ndim, pipeline_mode=pl.Buffered(1)
    )
    per_line = lambda size: pl.BlockSpec((group, size, width), lambda i, place: (i, 0, 0))
    per_token = pl.BlockSpec((group, 1, tokens), lambda i, place: (i, 0, 0))
    per_row = lambda size: pl.BlockSpec((group * slots, size), lambda i, place: (i, 0))
    count = line * slots
    extended = rows.shape[1]
    return pl.pallas_call(
        functools.partial(expert_kernel, slots=slots, add=bool(before)),
        grid_spec=pltpu.PrefetchScalarGridSpec(
            num_scalar_prefetch=1,
            grid=(steps,),
            in_specs=[per_line(extended), per_line(extended), per_token, per_token]
            + [whole(array) for array in weights]
            + [per_line(extended), per_line(tokens)][: len(before)],
            out_specs=[per_line(extended), per_line(tokens)]
            + [
                per_row(width),
                per_row(hidden_width),
                per_row(width),
                per_row(hidden_width),
                per_row(hidden_width),
            ],
        ),
        out_shape=[jax.ShapeDtypeStruct((line, size, width), low) for size in (extended, tokens)]
        + [
            jax.ShapeDtypeStruct((count, size), low)
            for size in (width, hidden_width, width, hidden_width, hidden_width)
        ],
        compiler_params=pltpu.CompilerParams(vmem_limit_bytes=62 * 1024 * 1024),
        cost_estimate=pl.CostEstimate(
            flops=10 * count * width * hidden_width + 8 * line * slots * tokens * width,
            bytes_accessed=16 * line * tokens * width,
            transcendentals=0,
        ),
    )(place, rows, grads, slot_rows, gate_rows, *weights, *before)


FIRST_ORDERS = (2, 3, 2, 3)


def gather_plan(units, orders):
    least, more = divmod(units, len(orders))
    count = len(orders)
    return tuple((order, 128 * (least + (i >= count - more))) for i, order in enumerate(orders))


def split_words(values):
    words = []
    for _ in range(3):
        words.append(values.astype(jnp.bfloat16))
        values = values - words[-1].astype(jnp.float32)
    return words


def after(value, other):
    return lax.optimization_barrier((value, other))[0]


def add_low(a, b):
    return (a.astype(jnp.float32) + b.astype(jnp.float32)).astype(jnp.bfloat16)


class Grid:
    def __init__(self, experts):
        self.experts = experts
        self.line = experts // PLANE
        here = lax.axis_index("expert")
        self.core = lax.axis_index("dp")
        self.at_line = here // PLANE
        self.at_plane = here % PLANE

    def shift(self, block, amount):
        pairs = [
            (i, ((i // PLANE + amount) % self.line) * PLANE + i % PLANE)
            for i in range(self.experts)
        ]
        return lax.ppermute(block, "expert", pairs)

    def line_sum(self, parts):
        half, rest = self.line // 2, (self.line - 1) // 2
        low = parts[half]
        for i in range(half, 0, -1):
            low = self.shift(low, -1)
            if i > 1:
                low = add_low(parts[i - 1], low)
        total = parts[0].astype(jnp.float32) + low.astype(jnp.float32)
        if rest:
            high = parts[self.line - rest]
            for i in range(rest, 0, -1):
                high = self.shift(high, 1)
                if i > 1:
                    high = add_low(parts[self.line - i + 1], high)
            total = total + high.astype(jnp.float32)
        return total


def local(
    tokens_in,
    lengths,
    key_keep,
    routes,
    cotangent,
    attention_in,
    attention_in_momentum,
    attention_in_average,
    attention_out,
    attention_out_momentum,
    attention_out_average,
    shared_in,
    shared_in_momentum,
    shared_in_average,
    shared_down,
    shared_down_momentum,
    shared_down_average,
    router,
    router_momentum,
    router_average,
    norm_gains,
    norm_gains_momentum,
    norm_gains_average,
    expert_in,
    expert_in_momentum,
    expert_in_average,
    expert_down,
    expert_down_momentum,
    expert_down_average,
):
    low = jnp.bfloat16
    full = jnp.float32
    tokens = tokens_in.shape[0]
    model_width = tokens_in.shape[1]
    top_count = routes.shape[1]
    block_rows = router.shape[0]
    experts = router.shape[1]
    hidden_width = shared_in.shape[2]
    grid = Grid(experts)
    capacity = 9 * tokens * top_count // (8 * experts)
    slots = -(-capacity // 16) * 16
    extra_width = -(-(experts + 2) // 128) * 128

    pack_one = jnp.concatenate(
        [attention_in[m].astype(low).T for m in range(3)]
        + [
            router.astype(low),
            norm_gains.astype(low).T,
            jnp.zeros((block_rows, extra_width - experts - 2), low),
        ],
        axis=1,
    )
    pack_out = attention_out.astype(low).T
    pack_shared = jnp.concatenate(
        [shared_in[0].astype(low), shared_in[1].astype(low), shared_down.astype(low).T], axis=1
    )
    position = jnp.arange(tokens, dtype=jnp.int32)
    usable = position < lengths[0]
    named = jnp.any(
        routes.T[None, :, :] == jnp.arange(experts, dtype=jnp.int32)[:, None, None], axis=1
    )
    member = named & usable[None, :]
    earlier = (position[:, None] < position[None, :]).astype(low)
    counted = dot_nn(member.astype(low), earlier)
    slot_of = jnp.where(member, counted, -1.0)
    wanted = grid.at_line * PLANE + (grid.at_plane ^ jnp.arange(PLANE, dtype=jnp.int32))
    choose = (wanted[:, None] == jnp.arange(experts, dtype=jnp.int32)[None, :]).astype(low)

    def widen(rows):
        return jnp.pad(rows, ((0, 0), (0, model_width - rows.shape[1])))

    gate, up, down = (
        expert_in[0, 0].astype(low),
        expert_in[0, 1].astype(low),
        expert_down[0].astype(low),
    )
    plans = (
        gather_plan(pack_one.shape[1] // 128, FIRST_ORDERS),
        gather_plan(model_width // 128, FIRST_ORDERS),
    )
    (all_one, turned_out), line_grads, gates, up_own, downs = first_exchange(
        experts,
        [pack_one, pack_out],
        plans,
        jnp.concatenate([cotangent, widen(slot_of.astype(low))], axis=0),
        gate,
        up,
        down,
    )
    slot_rows = jnp.stack(
        [dot_nn(choose, line_grads[r, tokens:, :tokens]) for r in range(grid.line)]
    )
    all_one = all_one.reshape(model_width, -1)
    turned_out = turned_out.reshape(model_width, model_width)
    extra = all_one[:, 3 * model_width :]
    router_low = extra[:, :experts]
    gains = extra[:, experts : experts + 2].astype(full).T
    gain_one, gain_two = gains[0], gains[1]
    pack_shared, _ = lax.optimization_barrier((pack_shared, turned_out))
    all_shared = lax.all_gather(pack_shared, ("dp", "expert"), axis=0, tiled=True)
    shared_pair = [all_shared[:, m * hidden_width : (m + 1) * hidden_width] for m in range(2)]
    turned_down = all_shared[:, 2 * hidden_width :]
    inputs = tokens_in.astype(full)
    rstd_one = lax.rsqrt(jnp.mean(inputs * inputs, axis=-1, keepdims=True) + eps_norm)
    normed_one = (inputs * rstd_one * gain_one).astype(low)
    cosine, sine_table = rope_tables(tokens, HD)
    bias = jnp.where(allowed_keys(lengths[0], key_keep), 0.0, mask_fill)
    query, key_rot, value, attended, hidden, normed_two = attend(
        normed_one, all_one, turned_out, bias, cosine, sine_table, tokens_in, gain_two[None]
    )
    rstd_two = lax.rsqrt(jnp.mean(hidden * hidden, axis=-1, keepdims=True) + eps_norm)

    logits = lax.dot_general(
        router_low, normed_two, (((0,), (1,)), ((), ())), preferred_element_type=full
    )
    logits = jnp.where(named, logits, mask_fill)
    logit_exps = jnp.exp(logits - jnp.max(logits, axis=0, keepdims=True))
    gating = logit_exps / jnp.sum(logit_exps, axis=0, keepdims=True)
    gating_live = jnp.where(member, gating, 0.0)
    gate_words = jnp.concatenate(split_words(gating_live), axis=1)
    line_rows, up_x, up_y, *far = second_exchange(
        experts,
        jnp.concatenate([normed_two, widen(gate_words)], axis=0),
        up,
        gates[1],
        downs[1],
        downs[2],
    )
    weights = list(zip(gates, (up_own, up_x, up_y), downs)) + [(far[0], far[1], far[2])]
    weights = [[part.reshape(-1, part.shape[-1]) for part in parts] for parts in weights]
    gate_rows = []
    for r in range(grid.line):
        words = dot_nn(choose, line_rows[r, tokens:, : 3 * tokens])
        gate_rows.append(
            words[:, :tokens] + words[:, tokens : 2 * tokens] + words[:, 2 * tokens :]
        )
    gate_rows = jnp.stack(gate_rows)

    before, kept = [], []
    for q in range(PLANE):
        *before, rows, inner, gated, grad_gate, grad_up = run_expert(
            wanted[q : q + 1],
            line_rows,
            line_grads,
            slot_rows[:, q : q + 1],
            gate_rows[:, q : q + 1],
            weights[q],
            before,
            slots,
        )
        kept.append((rows, inner, gated, grad_gate, grad_up))
    routed_grad, routed_result = before
    routed_grad, owns, crossed, far = third_exchange(experts, routed_grad, kept)
    routed_result = grid.line_sum(after(routed_result, routed_grad))
    gate_grads = routed_grad[tokens:]
    routed_grad = routed_grad[:tokens]
    grad_gating = (
        gate_grads[:, :tokens]
        + gate_grads[:, tokens : 2 * tokens]
        + gate_grads[:, 2 * tokens : 3 * tokens]
    )
    grad_chosen = gating * (grad_gating - jnp.sum(gating * grad_gating, axis=0, keepdims=True))
    grad_logits = grad_chosen.astype(low)
    grad_router = lax.dot_general(
        normed_two, grad_logits, (((0,), (1,)), ((), ())), preferred_element_type=full
    )

    grad_out = cotangent.astype(full)
    shared_gate = dot_nn(normed_two, shared_pair[0])
    shared_up = dot_nn(normed_two, shared_pair[1])
    shared_silu, shared_slope = silu_parts(shared_gate)
    shared_hidden = (shared_silu * shared_up).astype(low)
    shared_result = dot_nt(shared_hidden, turned_down)
    grad_shared_hidden = dot_nn(cotangent, turned_down)
    grad_shared_gate = (grad_shared_hidden * shared_up * shared_slope).astype(low)
    grad_shared_up = (grad_shared_hidden * shared_silu).astype(low)
    grad_normed_two = dot_nt(grad_shared_gate, shared_pair[0]) + dot_nt(
        grad_shared_up, shared_pair[1]
    )
    grad_normed_two = grad_normed_two + lax.dot_general(
        grad_logits, router_low, (((0,), (1,)), ((), ())), preferred_element_type=full
    )

    grad_normed_two = grad_normed_two + routed_grad
    scaled_two = grad_normed_two * gain_two
    grad_gain_two = jnp.sum(grad_normed_two * hidden * rstd_two, axis=0)
    grad_hidden = (
        grad_out
        + rstd_two * scaled_two
        - hidden * rstd_two**3 * jnp.mean(scaled_two * hidden, axis=-1, keepdims=True)
    )
    grad_branch = grad_hidden.astype(low)
    grads_shared = [
        dot_tn(normed_two, grad_shared_gate).astype(low),
        dot_tn(normed_two, grad_shared_up).astype(low),
        dot_tn(cotangent, shared_hidden).astype(low),
    ]
    *grads_attention, grad_normed_one = attend_back(
        grad_branch,
        normed_one,
        query,
        key_rot,
        value,
        attended,
        all_one,
        turned_out,
        bias,
        cosine,
        sine_table,
    )
    near_x = [add_low(*pair) for pair in zip(owns[1], crossed[1])]
    near_y = [add_low(*pair) for pair in zip(owns[2], crossed[2])]
    edge = far[2].shape[0]
    near_x[0] = add_low(near_x[0], far[0])
    near_y[1] = add_low(near_y[1], far[1])
    near_x[2] = jnp.concatenate([add_low(near_x[2][:edge], far[2]), near_x[2][edge:]], axis=0)
    near_y[2] = jnp.concatenate([near_y[2][:edge], add_low(near_y[2][edge:], far[3])], axis=0)
    scaled_one = grad_normed_one * gain_one
    grad_gain_one = jnp.sum(grad_normed_one * inputs * rstd_one, axis=0)
    input_grad = (
        grad_hidden
        + rstd_one * scaled_one
        - inputs * rstd_one**3 * jnp.mean(scaled_one * inputs, axis=-1, keepdims=True)
    )
    grad_extra = jnp.concatenate(
        [
            grad_router.astype(low),
            jnp.stack([grad_gain_one, grad_gain_two], axis=1).astype(low),
            jnp.zeros((model_width, extra_width - experts - 2), low),
        ],
        axis=1,
    )
    cut = 512
    summed_one, summed_two, *arrived = sum_all(
        experts,
        grads_attention + grads_shared + [grad_extra],
        [
            [
                [(0, 0, model_width), (2, 0, cut)],
                [(1, 0, model_width), (7, 0, extra_width)],
                [(2, cut, model_width - cut)],
            ],
            [
                [(4, 0, hidden_width), (5, 0, hidden_width)],
                [(3, 0, model_width)],
                [(6, 0, hidden_width)],
            ],
        ],
        near_x + near_y,
        ("x",) * 3 + ("y",) * 3,
    )
    summed_one, summed_two = summed_one.astype(full), summed_two.astype(full)

    output = (hidden + shared_result + routed_result).astype(low)

    summed_gate, summed_up, summed_expert_down = [
        sum(part.astype(full) for part in four)
        for four in zip(owns[0], crossed[0], arrived[:3], arrived[3:])
    ]
    summed_expert_in = jnp.stack([summed_gate, summed_up], axis=0)[None]
    summed_expert_down = summed_expert_down[None]

    def take(array, start, width):
        return array[:, start : start + width]

    at = model_width + cut
    summed_value = jnp.concatenate(
        [
            take(summed_one, model_width, cut),
            take(summed_one, at + model_width + extra_width, model_width - cut),
        ],
        axis=1,
    )
    summed_in = jnp.stack(
        [take(summed_one, 0, model_width).T, take(summed_one, at, model_width).T, summed_value.T],
        axis=0,
    )
    at = at + model_width
    summed_router = take(summed_one, at, experts)
    summed_gains = take(summed_one, at + experts, 2).T
    summed_shared_in = jnp.stack(
        [take(summed_two, 0, hidden_width), take(summed_two, hidden_width, hidden_width)], axis=0
    )
    at = 2 * hidden_width
    summed_out = take(summed_two, at, model_width).T
    summed_shared_down = take(summed_two, at + model_width, hidden_width).T
    upd_attn_in = advance(
        attention_in, attention_in_momentum, attention_in_average, summed_in, rate_attention_in
    )
    upd_attn_out = advance(
        attention_out, attention_out_momentum, attention_out_average, summed_out, rate_attention_out
    )
    upd_shared_in = advance(
        shared_in, shared_in_momentum, shared_in_average, summed_shared_in, rate_shared_in
    )
    upd_shared_down = advance(
        shared_down, shared_down_momentum, shared_down_average, summed_shared_down, rate_shared_down
    )
    upd_router = advance(router, router_momentum, router_average, summed_router, rate_router)
    upd_gains = advance(
        norm_gains, norm_gains_momentum, norm_gains_average, summed_gains, rate_gains
    )
    upd_expert_in = advance(
        expert_in, expert_in_momentum, expert_in_average, summed_expert_in, rate_expert_in
    )
    upd_expert_down = advance(
        expert_down, expert_down_momentum, expert_down_average, summed_expert_down, rate_expert_down
    )
    return (
        output,
        input_grad,
        upd_attn_in[0],
        upd_attn_in[1],
        upd_attn_in[2],
        upd_attn_out[0],
        upd_attn_out[1],
        upd_attn_out[2],
        upd_shared_in[0],
        upd_shared_in[1],
        upd_shared_in[2],
        upd_shared_down[0],
        upd_shared_down[1],
        upd_shared_down[2],
        upd_router[0],
        upd_router[1],
        upd_router[2],
        upd_gains[0],
        upd_gains[1],
        upd_gains[2],
        upd_expert_in[0],
        upd_expert_in[1],
        upd_expert_in[2],
        upd_expert_down[0],
        upd_expert_down[1],
        upd_expert_down[2],
    )


def solution(mesh):
    in_specs = (
        P(("dp", "expert"), None),
        P(("dp", "expert")),
        P(("dp", "expert")),
        P(("dp", "expert"), None),
        P(("dp", "expert"), None),
        P(None, None, ("dp", "expert")),
        P(None, None, ("dp", "expert")),
        P(None, None, ("dp", "expert")),
        P(None, ("dp", "expert")),
        P(None, ("dp", "expert")),
        P(None, ("dp", "expert")),
        P(None, ("dp", "expert"), None),
        P(None, ("dp", "expert"), None),
        P(None, ("dp", "expert"), None),
        P(None, ("dp", "expert")),
        P(None, ("dp", "expert")),
        P(None, ("dp", "expert")),
        P(("dp", "expert"), None),
        P(("dp", "expert"), None),
        P(("dp", "expert"), None),
        P(None, ("dp", "expert")),
        P(None, ("dp", "expert")),
        P(None, ("dp", "expert")),
        P("expert", None, "dp", None),
        P("expert", None, "dp", None),
        P("expert", None, "dp", None),
        P("expert", "dp", None),
        P("expert", "dp", None),
        P("expert", "dp", None),
    )
    out_specs = (
        P(("dp", "expert"), None),
        P(("dp", "expert"), None),
        P(None, None, ("dp", "expert")),
        P(None, None, ("dp", "expert")),
        P(None, None, ("dp", "expert")),
        P(None, ("dp", "expert")),
        P(None, ("dp", "expert")),
        P(None, ("dp", "expert")),
        P(None, ("dp", "expert"), None),
        P(None, ("dp", "expert"), None),
        P(None, ("dp", "expert"), None),
        P(None, ("dp", "expert")),
        P(None, ("dp", "expert")),
        P(None, ("dp", "expert")),
        P(("dp", "expert"), None),
        P(("dp", "expert"), None),
        P(("dp", "expert"), None),
        P(None, ("dp", "expert")),
        P(None, ("dp", "expert")),
        P(None, ("dp", "expert")),
        P("expert", None, "dp", None),
        P("expert", None, "dp", None),
        P("expert", None, "dp", None),
        P("expert", "dp", None),
        P("expert", "dp", None),
        P("expert", "dp", None),
    )
    return jax.shard_map(local, mesh=mesh, in_specs=in_specs, out_specs=out_specs, check_vma=False)
```

```python
import functools

import jax
import jax.numpy as jnp
from jax import lax
from jax.experimental import pallas as pl
from jax.experimental.pallas import tpu as pltpu
from jax.sharding import PartitionSpec as P

HD = 128
STEP = 4


eps_norm = 1e-06
theta_base = 10000.0
momentum_decay = 0.9
mask_fill = -1e30
rate_attention_in = 2e-05
rate_attention_out = 0.002
rate_shared_in = 3e-05
rate_shared_down = 0.0002
rate_router = 1.5e-05
rate_gains = 0.0002
rate_expert_in = 0.0004
rate_expert_down = 0.008


def rope_tables(length, head_width):
    half_width = head_width // 2
    frequency = theta_base ** (-(jnp.arange(half_width, dtype=jnp.float32) * 2.0 / head_width))
    angles = jnp.arange(length, dtype=jnp.float32)[:, None] * frequency[None, :]
    cosine, sine_table = jnp.cos(angles), jnp.sin(angles)
    return (
        jnp.concatenate([cosine, cosine], axis=1),
        jnp.concatenate([-sine_table, sine_table], axis=1),
    )


def allowed_keys(length, keep_flags):
    amount = keep_flags.shape[0]
    position = jnp.arange(amount)
    causal = position[None, :] <= position[:, None]
    usable = (position < length) & (keep_flags == 1)
    return causal & (usable[None, :] | (position[None, :] == position[:, None]))


def silu_parts(values):
    logistic = jax.nn.sigmoid(values)
    return (values * logistic, logistic * (1.0 + values * (1.0 - logistic)))


def advance(weight, moment, average, gradient, step_rate):
    moment_new = momentum_decay * moment + gradient
    weight_new = weight - step_rate * (gradient + momentum_decay * moment_new)
    average_new = average + (weight_new - average) / (STEP + 1)
    return (weight_new, moment_new, average_new)


def dot_nn(a, b):
    return lax.dot_general(a, b, (((1,), (0,)), ((), ())), preferred_element_type=jnp.float32)


def dot_nt(a, b):
    return lax.dot_general(a, b, (((1,), (1,)), ((), ())), preferred_element_type=jnp.float32)


def dot_tn(a, b):
    return lax.dot_general(a, b, (((0,), (0,)), ((), ())), preferred_element_type=jnp.float32)


PLANE = 4
MESH = pl.DeviceIdType.MESH


class Spot:
    def __init__(self, line):
        here = lax.axis_index("expert")
        self.line = line
        self.core = lax.axis_index("dp")
        self.at = lax.div(here, PLANE)
        rest = lax.rem(here, PLANE)
        self.y, self.x = lax.div(rest, 2), lax.rem(rest, 2)

    def chip(self, at, y, x):
        return (self.core, at * PLANE + y * 2 + x)

    def around(self, amount):
        return lax.rem(self.at + amount + self.line, self.line)

    def partner(self, way):
        if way == "core":
            return (1 - self.core, self.at * PLANE + self.y * 2 + self.x)
        if way == "x":
            return self.chip(self.at, self.y, 1 - self.x)
        if way == "y":
            return self.chip(self.at, 1 - self.y, self.x)
        return self.chip(self.around(1 if way == "up" else -1), self.y, self.x)


def meet(spot):
    barrier = pltpu.get_barrier_semaphore()
    for way in ("core", "x", "y", "up", "down"):
        pl.semaphore_signal(barrier, inc=1, device_id=spot.partner(way), device_id_type=MESH)
    pl.semaphore_wait(barrier, 5)


class Moves:
    def __init__(self, spot, send_sems, recv_sems, local_sems):
        self.spot, self.send_sems, self.recv_sems = spot, send_sems, recv_sems
        self.local_sems = local_sems
        self.made, self.kept, self.loose = 0, 0, []

    def start(self, source, target, way, later=False):
        copy = pltpu.make_async_remote_copy(
            src_ref=source,
            dst_ref=target,
            send_sem=self.send_sems.at[self.made],
            recv_sem=self.recv_sems.at[self.made],
            device_id=self.spot.partner(way),
            device_id_type=MESH,
        )
        self.made += 1
        copy.start()
        if later:
            self.loose.append(copy)
        return copy

    def keep(self, source, target, later=False):
        copy = pltpu.make_async_copy(source, target, self.local_sems.at[self.kept])
        self.kept += 1
        copy.start()
        if later:
            self.loose.append(copy)
        return copy

    def finish(self):
        for copy in self.loose:
            copy.wait()


def in_steps(chains):
    while chains:
        left = []
        for chain in chains:
            try:
                next(chain)
                left.append(chain)
            except StopIteration:
                pass
        chains = left
        yield


def in_turn(chains):
    for _ in in_steps(chains):
        pass


def place_chain(moves, source, buffer, target):
    copy = moves.keep(source, buffer)
    yield
    copy.wait()
    moves.keep(buffer, target, later=True)


def core_chain(moves, own, whole, buffer):
    core = moves.spot.core
    moves.start(own, whole.at[core], "core", later=True)
    return place_chain(moves, own, buffer, whole.at[core])


def dense_chain(moves, whole, columns, order):
    spot = moves.spot
    half, rest = spot.line // 2, (spot.line - 1) // 2
    everything = slice(None)
    held = {"z": spot.at, "y": spot.y, "x": spot.x}

    def region(**other):
        at = dict(held, **other)
        return whole.at[spot.core, at["z"], at["y"], at["x"], everything, columns]

    def forward(part):
        moves.start(part, part, "core", later=True)

    for stage, dim in enumerate(order):
        if dim == "z":
            up = down = None
            for i in range(1, half + 1):
                part = region(z=spot.around(1 - i))
                up = moves.start(part, part, "up")
                if i <= rest:
                    part = region(z=spot.around(i - 1))
                    down = moves.start(part, part, "down")
                if stage == 0 and i == 1:
                    forward(region())
                yield
                up.wait()
                forward(region(z=spot.around(-i)))
                if i <= rest:
                    down.wait()
                    forward(region(z=spot.around(i)))
        else:
            part = region()
            copy = moves.start(part, part, dim)
            if stage == 0:
                forward(region())
            yield
            copy.wait()
            forward(region(**{dim: 1 - held[dim]}))
        held[dim] = everything


ORDERS = ("xyz", "yzx", "zxy", "zyx")


def first_kernel(line, plans, *refs):
    count = len(plans)
    shards, down, refs = refs[:count], refs[count], refs[count + 1 :]
    results, over_x, over_y, refs = refs[:count], refs[count], refs[count + 1], refs[count + 2 :]
    wholes, refs = refs[:count], refs[count:]
    spot = Spot(line)
    meet(spot)
    moves = Moves(spot, *refs)
    loads = [
        moves.keep(shards[n], wholes[n].at[spot.core, spot.at, spot.y, spot.x])
        for n in range(count)
    ]
    for copy in loads:
        copy.wait()
    chains = []
    for n, plan in enumerate(plans):
        start = 0
        for order, width in plan:
            columns = slice(start, start + width)
            chains.append(dense_chain(moves, wholes[n], columns, ORDERS[order]))
            start += width
    stages = 0
    for _ in in_steps(chains):
        stages += 1
        if stages == 1:
            moves.start(down, over_x, "x", later=True)
            moves.start(down, over_y, "y", later=True)
    moves.finish()
    stores = [moves.keep(wholes[n], results[n]) for n in range(count)]
    for copy in stores:
        copy.wait()


def hbm(count):
    return [pl.BlockSpec(memory_space=pl.ANY)] * count


def semaphores(remote, local):
    return [
        pltpu.SemaphoreType.DMA((remote,)),
        pltpu.SemaphoreType.DMA((remote,)),
        pltpu.SemaphoreType.DMA((local,)),
    ]


def both_halves(array):
    return jax.ShapeDtypeStruct((2,) + array.shape, array.dtype)


def first_exchange(experts, shards, plans, down):
    line = experts // PLANE
    count = len(shards)
    remote = sum(len(plan) for plan in plans) * (2 * line + 3) + 2
    out = pl.pallas_call(
        functools.partial(first_kernel, line, plans),
        out_shape=[
            jax.ShapeDtypeStruct((2, line, 2, 2) + shard.shape, shard.dtype) for shard in shards
        ]
        + [jax.ShapeDtypeStruct(down.shape, down.dtype)] * 2,
        in_specs=hbm(count + 1),
        out_specs=hbm(count + 2),
        scratch_shapes=[
            pltpu.VMEM((2, line, 2, 2) + shard.shape, shard.dtype) for shard in shards
        ]
        + semaphores(remote, 2 * count),
        compiler_params=pltpu.CompilerParams(
            collective_id=1, has_side_effects=True, vmem_limit_bytes=60 * 1024 * 1024
        ),
    )(*shards, down)
    return out[:count], out[count], out[count + 1]


def second_kernel(line, *refs):
    rows, pairs, downs, refs = refs[0], refs[1:4], refs[4:7], refs[7:]
    rising, falling, wholes, refs = refs[0], refs[1], refs[2:5], refs[5:]
    buffers, refs = refs[:9], refs[9:]
    spot = Spot(line)
    meet(spot)
    moves = Moves(spot, *refs)
    core = spot.core
    gate, up, down = wholes
    (_, pair_x, pair_y), (_, down_x, down_y) = pairs, downs
    half = down_x.shape[0] // 2

    def far_chain(source, target, way):
        copy = moves.start(source, target, way)
        yield
        copy.wait()
        moves.start(target, target, "core", later=True)

    moves.start(rows, rising, "up", later=True)
    moves.start(rows, falling, "down", later=True)
    upper, lower = pl.ds(0, half), pl.ds(half, half)
    in_turn(
        [
            far_chain(pair_y.at[1], up.at[3, core], "x"),
            far_chain(pair_x.at[0], gate.at[3, core], "y"),
            far_chain(down_y.at[lower], down.at[3, core, lower], "x"),
            far_chain(down_x.at[upper], down.at[3, core, upper], "y"),
        ]
        + [
            core_chain(moves, half_of, wholes[i].at[q], buffers[3 * q + i])
            for q in range(3)
            for i, half_of in enumerate((pairs[q].at[0], pairs[q].at[1], downs[q]))
        ]
    )
    moves.finish()


def second_exchange(experts, rows, pairs, downs):
    line = experts // PLANE
    low = rows.dtype
    shapes = [pairs[0].shape[1:]] * 2 + [downs[0].shape]
    return pl.pallas_call(
        functools.partial(second_kernel, line),
        out_shape=[jax.ShapeDtypeStruct(rows.shape, low)] * 2
        + [jax.ShapeDtypeStruct((PLANE, 2) + shape, low) for shape in shapes],
        in_specs=hbm(7),
        out_specs=hbm(5),
        scratch_shapes=[pltpu.VMEM(shape, low) for shape in shapes * 3] + semaphores(19, 18),
        compiler_params=pltpu.CompilerParams(
            collective_id=3, has_side_effects=True, vmem_limit_bytes=60 * 1024 * 1024
        ),
    )(rows, *pairs, *downs)


def third_kernel(line, groups, *refs):
    low, full = jnp.bfloat16, jnp.float32
    kept = [refs[5 * r : 5 * r + 5] for r in range(groups)]
    refs = refs[5 * groups :]
    owns = [refs[3 * q : 3 + 3 * q] for q in range(PLANE - 1)]
    refs = refs[3 * (PLANE - 1) :]
    crossed = [refs[3 * q : 3 + 3 * q] for q in range(PLANE - 1)]
    refs = refs[3 * (PLANE - 1) :]
    far_in, refs = refs[:4], refs[4:]
    loaded, refs = [refs[:5], refs[5:10]], refs[10:]
    results, refs = [refs[:6], refs[6:12]], refs[12:]
    far_box, down_grad, refs = refs[:3], refs[3], refs[4:]
    spot = Spot(line)
    meet(spot)
    moves = Moves(spot, *refs)
    order = (3, 1, 2, 0)
    slots = kept[0][0].shape[1]
    loads = {}

    def load(n):
        loads[n] = [
            moves.keep(kept[r][i].at[order[n]], loaded[n % 2][i].at[pl.ds(r * slots, slots)])
            for r in range(groups)
            for i in range(5)
        ]

    def add(target, source):
        target[...] = (target[...].astype(full) + source[...].astype(full)).astype(low)

    load(0)
    rows_half = results[0][0].shape[0]
    down_half = results[0][2].shape[0]
    sent = {}

    def weights(n):
        if n + 1 < PLANE:
            load(n + 1)
        for copy in loads[n]:
            copy.wait()
        rows, inner, gated, grad_gate, grad_up = loaded[n % 2]
        buffers = results[n % 2]
        if n == 3:
            for copy in sent[1]:
                copy.wait()
        down_grad[...] = dot_tn(inner[...], gated[...]).astype(low)
        for which in (1, 0):
            place = jnp.bitwise_xor(spot.core, which)
            gate_out, up_out, down_out = buffers[3 * which : 3 * which + 3]
            part = rows[:, pl.ds(pl.multiple_of(place * rows_half, 128), rows_half)]
            gate_out[...] = dot_tn(part, grad_gate[...]).astype(low)
            up_out[...] = dot_tn(part, grad_up[...]).astype(low)
            down_out[...] = down_grad[pl.ds(pl.multiple_of(place * down_half, 16), down_half), :]
            q = order[n]
            targets = far_box if q == PLANE - 1 else crossed[q]
            if which:
                sent[n] = [moves.start(buffers[3 + i], targets[i], "core") for i in range(3)]
            elif q < PLANE - 1:
                sent[n] += [moves.keep(buffers[i], owns[q][i]) for i in range(3)]

    def far():
        for copy in sent[0]:
            copy.wait()
        mine = results[0][:3]
        for i in range(3):
            add(far_box[i], mine[i])
        edge = down_half // 2
        moves.start(far_box[0], far_in[0], "y", later=True)
        moves.start(far_box[1], far_in[1], "x", later=True)
        moves.start(far_box[2].at[pl.ds(0, edge)], far_in[2], "y", later=True)
        moves.start(far_box[2].at[pl.ds(edge, edge)], far_in[3], "x", later=True)

    weights(0)
    weights(1)
    far()
    weights(2)
    weights(3)
    for n in (2, 3):
        for copy in sent[n]:
            copy.wait()
    moves.finish()


def third_exchange(experts, kept):
    line = experts // PLANE
    low = jnp.bfloat16
    rows, inner = kept[0][0], kept[0][1]
    slots, width, hidden_width = rows.shape[1], rows.shape[2], inner.shape[2]
    half, down_half = width // 2, hidden_width // 2
    pieces = [(half, hidden_width), (half, hidden_width), (down_half, width)]
    far = pieces[:2] + [(down_half // 2, width)] * 2
    out = pl.pallas_call(
        functools.partial(third_kernel, line, len(kept)),
        out_shape=[
            jax.ShapeDtypeStruct(size, low) for size in pieces * (2 * (PLANE - 1)) + far
        ],
        in_specs=hbm(5 * len(kept)),
        out_specs=hbm(6 * (PLANE - 1) + 4),
        scratch_shapes=[
            pltpu.VMEM((len(kept) * slots, array.shape[2]), low) for array in list(kept[0]) * 2
        ]
        + [pltpu.VMEM(size, low) for size in pieces * 4]
        + [pltpu.VMEM(size, low) for size in pieces]
        + [pltpu.VMEM((hidden_width, width), low)]
        + semaphores(3 * PLANE + 4, 5 * PLANE * len(kept) + 3 * PLANE),
        compiler_params=pltpu.CompilerParams(
            collective_id=4, has_side_effects=True, vmem_limit_bytes=62 * 1024 * 1024
        ),
    )(*[array for parts in kept for array in parts])
    count = 3 * (PLANE - 1)
    triples = lambda arrays: [arrays[3 * q : 3 * q + 3] for q in range(PLANE - 1)]
    return triples(out[:count]), triples(out[count : 2 * count]), out[2 * count :]


def sum_kernel(line, plans, ways, *refs):
    count = len(plans)
    given = sum(len(order) for plan in plans for order in plan)
    grads, refs = refs[:given], refs[given:]
    moved, refs = refs[: len(ways)], refs[len(ways) :]
    sums, refs = refs[:count], refs[count:]
    arrived, refs = refs[: len(ways)], refs[len(ways) :]
    kept, refs = refs[: 3 * count], refs[3 * count :]
    core_in, refs = refs[: 3 * count], refs[3 * count :]
    first_in, refs = refs[: 3 * count], refs[3 * count :]
    second_in, refs = refs[: 3 * count], refs[3 * count :]
    third_in, refs = refs[: 3 * count], refs[3 * count :]
    spot = Spot(line)
    meet(spot)
    moves = Moves(spot, *refs)
    half, rest = line // 2, (line - 1) // 2
    everything = slice(None)
    orders = ("xyz", "yzx", "zxy")

    loads, swaps = [], []
    at = 0
    for n, plan in enumerate(plans):
        for o, pieces in enumerate(plan):
            mine, theirs = [], []
            start = 0
            for first, width in pieces:
                ref = grads[at]
                source = slice(first, first + width)
                target = slice(start, start + width)
                mine.append(
                    moves.keep(
                        ref.at[spot.core, :, :, :, :, source],
                        kept[3 * n + o].at[:, :, :, :, target],
                    )
                )
                theirs.append(
                    moves.start(
                        ref.at[1 - spot.core, :, :, :, :, source],
                        core_in[3 * n + o].at[:, :, :, :, target],
                        "core",
                    )
                )
                at += 1
                start += width
            loads.append(mine)
            swaps.append(theirs)

    for way, source, target in zip(ways, moved, arrived):
        moves.start(source, target, way, later=True)

    def add(target, source):
        lead = target.shape[:-2]
        total = 1
        for extent in lead:
            total *= extent

        def one(i, carry):
            index = []
            for extent in reversed(lead):
                index.insert(0, lax.rem(i, extent))
                i = lax.div(i, extent)
            index = tuple(index)
            target[index] = (
                target[index].astype(jnp.float32) + source[index].astype(jnp.float32)
            ).astype(target.dtype)
            return carry

        lax.fori_loop(0, total, one, 0)

    def chain(n, o):
        buffer = kept[3 * n + o]
        mine, theirs = loads[3 * n + o], swaps[3 * n + o]
        for copy in mine:
            copy.wait()
        for copy in theirs:
            copy.wait()
        add(buffer, core_in[3 * n + o])
        inbox = [first_in[3 * n + o], second_in[3 * n + o], third_in[3 * n + o]]
        held = {"z": everything, "y": everything, "x": everything}

        def region(**other):
            at = dict(held, **other)
            return buffer.at[at["z"], at["y"], at["x"]]

        for stage, dim in enumerate(orders[o]):
            box = inbox[stage]
            if dim == "z":
                up = down = None
                for i in range(half, 0, -1):
                    down = moves.start(region(z=spot.around(-i)), box.at[i - 1], "down")
                    if i <= rest:
                        up = moves.start(region(z=spot.around(i)), box.at[half + i - 1], "up")
                    yield
                    down.wait()
                    add(region(z=spot.around(1 - i)), box.at[i - 1])
                    if i <= rest:
                        up.wait()
                        add(region(z=spot.around(i - 1)), box.at[half + i - 1])
                held[dim] = spot.at
            else:
                own = spot.y if dim == "y" else spot.x
                copy = moves.start(region(**{dim: 1 - own}), box, dim)
                yield
                copy.wait()
                held[dim] = own
                add(region(), box)
        start = sum(sum(width for _, width in pieces) for pieces in plans[n][:o])
        width = sum(width for _, width in plans[n][o])
        result = moves.keep(region(), sums[n].at[:, slice(start, start + width)])
        yield
        result.wait()

    in_turn([chain(n, o) for n in range(count) for o in range(3)])
    moves.finish()


def sum_all(experts, grads, plans, moved, ways):
    line = experts // PLANE
    half, rest = line // 2, (line - 1) // 2
    rows = grads[0].shape[0] // (2 * experts)
    dtype = grads[0].dtype
    operands, kernel_plans, shapes = [], [], []
    boxes = [[], [], [], [], []]
    for plan in plans:
        kernel_plan = []
        for o, pieces in enumerate(plan):
            for which, _, _ in pieces:
                array = grads[which]
                operands.append(array.reshape(2, line, 2, 2, rows, array.shape[1]))
            kernel_plan.append(tuple((first, width) for _, first, width in pieces))
            width = sum(width for _, _, width in pieces)
            steps = half + rest
            block = (rows, width)
            boxes[0].append((line, 2, 2) + block)
            boxes[1].append((line, 2, 2) + block)
            if o == 0:
                inboxes = [(line, 2), (line,), (steps,)]
            elif o == 1:
                inboxes = [(line, 2), (steps, 2), ()]
            else:
                inboxes = [(steps, 2, 2), (2,), ()]
            for i, lead in enumerate(inboxes):
                boxes[2 + i].append(lead + block)
        kernel_plans.append(tuple(kernel_plan))
        total = sum(width for pieces in kernel_plan for _, width in pieces)
        shapes.append(jax.ShapeDtypeStruct((rows, total), dtype))
    count = len(plans)
    number = len(operands) + 3 * count * (line + 1) + len(moved)
    shapes += [jax.ShapeDtypeStruct(array.shape, array.dtype) for array in moved]
    return pl.pallas_call(
        functools.partial(sum_kernel, line, tuple(kernel_plans), ways),
        out_shape=shapes,
        in_specs=hbm(len(operands) + len(moved)),
        out_specs=hbm(count + len(moved)),
        scratch_shapes=[pltpu.VMEM(shape, dtype) for kind in boxes for shape in kind]
        + semaphores(number, len(operands) + 3 * count),
        compiler_params=pltpu.CompilerParams(
            collective_id=2, has_side_effects=True, vmem_limit_bytes=60 * 1024 * 1024
        ),
    )(*operands, *moved)


def turn(values, cosine, sine_table):
    return values * cosine + pltpu.roll(values, HD // 2, 1) * sine_table


def turn_back(values, cosine, sine_table):
    return values * cosine - pltpu.roll(values, HD // 2, 1) * sine_table


def probabilities(query, key, bias):
    scores = dot_nt(query, key) * HD ** (-0.5) + bias
    exps = jnp.exp(scores - jnp.max(scores, axis=1, keepdims=True))
    return exps / jnp.sum(exps, axis=1, keepdims=True)


def attend_kernel(
    steps,
    normed,
    query_weight,
    key_weight,
    value_weight,
    out_weight,
    bias,
    cosine,
    sine_table,
    inputs,
    gain,
    query_out,
    key_out,
    value_out,
    attended_out,
    hidden_out,
    normed_out,
):
    step = pl.program_id(0)
    low = jnp.bfloat16
    n1 = normed[...]
    cos, sin = cosine[...], sine_table[...]
    query = dot_nt(n1, query_weight[...])
    key = dot_nt(n1, key_weight[...])
    value_out[...] = dot_nt(n1, value_weight[...]).astype(low)
    for part in range(query.shape[1] // HD):
        columns = slice(part * HD, (part + 1) * HD)
        q = turn(query[:, columns], cos, sin).astype(low)
        k = turn(key[:, columns], cos, sin).astype(low)
        query_out[:, columns] = q
        key_out[:, columns] = k
        probs = probabilities(q, k, bias[...])
        attended_out[:, columns] = dot_nn(probs.astype(low), value_out[:, columns]).astype(low)
    branch = dot_nt(attended_out[...], out_weight[...])

    @pl.when(step == 0)
    def _():
        hidden_out[...] = inputs[...].astype(jnp.float32) + branch

    @pl.when(step > 0)
    def _():
        hidden_out[...] += branch

    @pl.when(step == steps - 1)
    def _():
        hidden = hidden_out[...]
        rstd = lax.rsqrt(jnp.mean(hidden * hidden, axis=1, keepdims=True) + eps_norm)
        normed_out[...] = (hidden * rstd * gain[...]).astype(low)


def attend(normed, weights, out_weight, bias, cosine, sine_table, inputs, gain):
    tokens, width = normed.shape
    group = 2 * HD
    steps = width // group
    low = jnp.bfloat16
    whole = lambda *shape: pl.BlockSpec(shape, lambda i: (0,) * len(shape))
    columns = pl.BlockSpec((tokens, group), lambda i: (0, i))
    return pl.pallas_call(
        functools.partial(attend_kernel, steps),
        grid=(steps,),
        in_specs=[whole(tokens, width)]
        + [pl.BlockSpec((group, width), lambda i, m=m: (i, m)) for m in range(3)]
        + [
            pl.BlockSpec((width, group), lambda i: (0, i)),
            whole(tokens, tokens),
            whole(tokens, HD),
            whole(tokens, HD),
            whole(tokens, width),
            whole(1, width),
        ],
        out_specs=[columns] * 4 + [whole(tokens, width)] * 2,
        out_shape=[jax.ShapeDtypeStruct((tokens, width), low)] * 4
        + [
            jax.ShapeDtypeStruct((tokens, width), jnp.float32),
            jax.ShapeDtypeStruct((tokens, width), low),
        ],
        compiler_params=pltpu.CompilerParams(vmem_limit_bytes=48 * 1024 * 1024),
        cost_estimate=pl.CostEstimate(
            flops=8 * tokens * width * width, bytes_accessed=20 * width * width, transcendentals=0
        ),
    )(normed, weights, weights, weights, out_weight, bias, cosine, sine_table, inputs, gain)


def attend_back_kernel(
    grad_branch,
    normed,
    query_in,
    key_in,
    value_in,
    attended_in,
    query_weight,
    key_weight,
    value_weight,
    out_weight,
    bias,
    cosine,
    sine_table,
    grad_query_weight,
    grad_key_weight,
    grad_value_weight,
    grad_out_weight,
    grad_normed,
    grads,
):
    step = pl.program_id(0)
    low = jnp.bfloat16
    da = grad_branch[...]
    n1 = normed[...]
    cos, sin = cosine[...], sine_table[...]
    scaling = HD ** (-0.5)
    group = query_in.shape[1]
    grad_out_weight[...] = dot_tn(da, attended_in[...]).astype(low)
    grad_attended = dot_nn(da, out_weight[...]).astype(low)
    for part in range(group // HD):
        columns = slice(part * HD, (part + 1) * HD)
        q, k, v = query_in[:, columns], key_in[:, columns], value_in[:, columns]
        do = grad_attended[:, columns]
        probs = probabilities(q, k, bias[...])
        grad_probs = dot_nt(do, v)
        grad_scores = probs * (grad_probs - jnp.sum(probs * grad_probs, axis=1, keepdims=True))
        grad_scores = grad_scores.astype(low)
        grads[0, :, columns] = turn_back(dot_nn(grad_scores, k) * scaling, cos, sin).astype(low)
        grads[1, :, columns] = turn_back(dot_tn(grad_scores, q) * scaling, cos, sin).astype(low)
        grads[2, :, columns] = dot_tn(probs.astype(low), do).astype(low)
    grad_query_weight[...] = dot_tn(grads[0], n1).astype(low)
    grad_key_weight[...] = dot_tn(grads[1], n1).astype(low)
    grad_value_weight[...] = dot_tn(grads[2], n1).astype(low)
    total = (
        dot_nn(grads[0], query_weight[...])
        + dot_nn(grads[1], key_weight[...])
        + dot_nn(grads[2], value_weight[...])
    )

    @pl.when(step == 0)
    def _():
        grad_normed[...] = total

    @pl.when(step > 0)
    def _():
        grad_normed[...] += total


def attend_back(
    grad_branch, normed, query, key, value, attended, weights, out_weight, bias, cosine, sine_table
):
    tokens, width = normed.shape
    group = 2 * HD
    steps = width // group
    low = jnp.bfloat16
    whole = lambda *shape: pl.BlockSpec(shape, lambda i: (0,) * len(shape))
    columns = pl.BlockSpec((tokens, group), lambda i: (0, i))
    return pl.pallas_call(
        attend_back_kernel,
        grid=(steps,),
        in_specs=[whole(tokens, width)] * 2
        + [columns] * 4
        + [pl.BlockSpec((group, width), lambda i, m=m: (i, m)) for m in range(3)]
        + [
            pl.BlockSpec((width, group), lambda i: (0, i)),
            whole(tokens, tokens),
            whole(tokens, HD),
            whole(tokens, HD),
        ],
        out_specs=[pl.BlockSpec((group, width), lambda i: (i, 0))] * 3
        + [pl.BlockSpec((width, group), lambda i: (0, i)), whole(tokens, width)],
        out_shape=[jax.ShapeDtypeStruct((width, width), low)] * 4
        + [jax.ShapeDtypeStruct((tokens, width), jnp.float32)],
        scratch_shapes=[pltpu.VMEM((3, tokens, group), low)],
        compiler_params=pltpu.CompilerParams(vmem_limit_bytes=48 * 1024 * 1024),
        cost_estimate=pl.CostEstimate(
            flops=16 * tokens * width * width, bytes_accessed=40 * width * width, transcendentals=0
        ),
    )(
        grad_branch,
        normed,
        query,
        key,
        value,
        attended,
        weights,
        weights,
        weights,
        out_weight,
        bias,
        cosine,
        sine_table,
    )


def expert_kernel(count, numbers, *refs):
    low, full = jnp.bfloat16, jnp.float32
    rows_in, grads_in, slots_in, gates_in = [refs[i * count : (i + 1) * count] for i in range(4)]
    gate_weight, up_weight, down_weight, *refs = refs[4 * count :]
    grad_total, result_total = refs[:count], refs[count : 2 * count]
    rows_out, inner_out, gated_out, grad_gate_out, grad_up_out = refs[2 * count : 2 * count + 5]
    hot_all, grad_all, result_all, word_sums = refs[2 * count + 5 :]
    tokens, width = slots_in[0].shape[2], rows_in[0].shape[1]
    slots = rows_out.shape[1] // count
    experts = word_sums.shape[1]
    q = pl.program_id(0)
    slot_ids = lax.broadcasted_iota(jnp.int32, (slots, tokens), 0).astype(full)
    parts = [slice(r * slots, (r + 1) * slots) for r in range(count)]
    here = pl.ds(pl.multiple_of(q * slots, slots), slots)
    places, gate_cols, grad_parts = [], [], []
    for r in range(count):
        place = slots_in[r][0] == slot_ids
        hot = place.astype(low)
        hot_all[r, here] = hot
        places.append(place)
        gate_cols.append(jnp.sum(jnp.where(place, gates_in[r][0], 0.0), axis=1, keepdims=True))
        rows_out[0, parts[r]] = dot_nn(hot, rows_in[r][:tokens]).astype(low)
        grad_parts.append(dot_nn(hot, grads_in[r][:tokens]))
    gate_col = jnp.concatenate(gate_cols, axis=0)
    grad_rows = jnp.concatenate(grad_parts, axis=0)
    rows = rows_out[0]
    gated = (grad_rows * gate_col).astype(low)
    gated_out[0] = gated
    gate_rows = dot_nn(rows, gate_weight[0])
    up_rows = dot_nn(rows, up_weight[0])
    logistic = jax.nn.sigmoid(gate_rows)
    silu_rows = gate_rows * logistic
    slope_rows = logistic * (1.0 + gate_rows * (1.0 - logistic))
    inner = (silu_rows * up_rows).astype(low)
    inner_out[0] = inner
    grad_inner = dot_nt(gated, down_weight[0])
    grad_gate_rows = (grad_inner * up_rows * slope_rows).astype(low)
    grad_up_rows = (grad_inner * silu_rows).astype(low)
    grad_gate_out[0] = grad_gate_rows
    grad_up_out[0] = grad_up_rows
    sent_grads = (
        dot_nt(grad_gate_rows, gate_weight[0]) + dot_nt(grad_up_rows, up_weight[0])
    ).astype(low)
    result_rows = dot_nn(inner, down_weight[0])
    gate_grad = jnp.sum(result_rows * grad_rows, axis=1, keepdims=True)
    sent_results = (result_rows * gate_col).astype(low)
    expert_ids = lax.broadcasted_iota(jnp.int32, (experts, width), 0)

    @pl.when(q == 0)
    def _():
        word_sums[...] = jnp.zeros_like(word_sums)

    for r in range(count):
        grad_all[r, here] = sent_grads[parts[r]]
        result_all[r, here] = sent_results[parts[r]]
        token_grad = jnp.sum(
            jnp.where(places[r], gate_grad[parts[r]], 0.0), axis=0, keepdims=True
        )
        words = jnp.concatenate(
            [word.astype(full) for word in split_words(token_grad)]
            + [jnp.zeros((1, width - 3 * tokens), full)],
            axis=1,
        )
        word_sums[r] += jnp.where(expert_ids == numbers[q], words, 0.0)

    @pl.when(q == PLANE - 1)
    def _():
        for r in range(count):
            grad_total[r][:tokens] = dot_tn(hot_all[r], grad_all[r]).astype(low)
            grad_total[r][tokens:] = word_sums[r].astype(low)
            result_total[r][...] = dot_tn(hot_all[r], result_all[r]).astype(low)


def run_experts(numbers, rows, grads, slot_rows, gate_rows, weights, slots):
    count = len(rows)
    extended, width = rows[0].shape
    tokens = slot_rows[0].shape[2]
    low = jnp.bfloat16
    hidden_width = weights[0].shape[2]
    whole = lambda *shape: pl.BlockSpec(shape, lambda q, numbers: (0,) * len(shape))
    each = lambda *shape: pl.BlockSpec((1,) + shape, lambda q, numbers: (q, 0, 0))
    sizes = (width, hidden_width, width, hidden_width, hidden_width)
    out = pl.pallas_call(
        functools.partial(expert_kernel, count),
        grid_spec=pltpu.PrefetchScalarGridSpec(
            num_scalar_prefetch=1,
            grid=(PLANE,),
            in_specs=[whole(extended, width)] * (2 * count)
            + [each(1, tokens)] * (2 * count)
            + [each(*array.shape[1:]) for array in weights],
            out_specs=[whole(extended, width)] * count
            + [whole(tokens, width)] * count
            + [each(count * slots, size) for size in sizes],
            scratch_shapes=[
                pltpu.VMEM((count, PLANE * slots, tokens), low),
                pltpu.VMEM((count, PLANE * slots, width), low),
                pltpu.VMEM((count, PLANE * slots, width), low),
                pltpu.VMEM((count, extended - tokens, width), jnp.float32),
            ],
        ),
        out_shape=[jax.ShapeDtypeStruct((extended, width), low)] * count
        + [jax.ShapeDtypeStruct((tokens, width), low)] * count
        + [jax.ShapeDtypeStruct((PLANE, count * slots, size), low) for size in sizes],
        compiler_params=pltpu.CompilerParams(vmem_limit_bytes=62 * 1024 * 1024),
        cost_estimate=pl.CostEstimate(
            flops=count * PLANE * slots * width * (10 * hidden_width + 8 * tokens),
            bytes_accessed=6 * PLANE * width * hidden_width,
            transcendentals=0,
        ),
    )(numbers, *rows, *grads, *slot_rows, *gate_rows, *weights)
    return out[:count], out[count : 2 * count], out[2 * count :]


FIRST_ORDERS = (0, 1, 2, 0, 1, 2)


def gather_plan(units, orders):
    least, more = divmod(units, len(orders))
    count = len(orders)
    return tuple((order, 128 * (least + (i >= count - more))) for i, order in enumerate(orders))


def split_words(values):
    words = []
    for _ in range(3):
        words.append(values.astype(jnp.bfloat16))
        values = values - words[-1].astype(jnp.float32)
    return words


def after(value, other):
    return lax.optimization_barrier((value, other))[0]


def add_low(a, b):
    return (a.astype(jnp.float32) + b.astype(jnp.float32)).astype(jnp.bfloat16)


class Grid:
    def __init__(self, experts):
        self.experts = experts
        self.line = experts // PLANE
        here = lax.axis_index("expert")
        self.core = lax.axis_index("dp")
        self.at_line = here // PLANE
        self.at_plane = here % PLANE

    def shift(self, block, amount):
        pairs = [
            (i, ((i // PLANE + amount) % self.line) * PLANE + i % PLANE)
            for i in range(self.experts)
        ]
        return lax.ppermute(block, "expert", pairs)

    def swap(self, block, flip):
        pairs = [(i, (i // PLANE) * PLANE + ((i % PLANE) ^ flip)) for i in range(self.experts)]
        return lax.ppermute(block, "expert", pairs)

    def line_gather(self, block, rising=None, falling=None):
        half, rest = self.line // 2, (self.line - 1) // 2
        rising = self.shift(block, 1) if rising is None else rising
        found = [block, rising] + [None] * (self.line - 2)
        for i in range(2, half + 1):
            found[i] = self.shift(found[i - 1], 1)
        if rest:
            found[-1] = self.shift(block, -1) if falling is None else falling
            for i in range(2, rest + 1):
                found[-i] = self.shift(found[1 - i], -1)
        return found


def local(
    tokens_in,
    lengths,
    key_keep,
    routes,
    cotangent,
    attention_in,
    attention_in_momentum,
    attention_in_average,
    attention_out,
    attention_out_momentum,
    attention_out_average,
    shared_in,
    shared_in_momentum,
    shared_in_average,
    shared_down,
    shared_down_momentum,
    shared_down_average,
    router,
    router_momentum,
    router_average,
    norm_gains,
    norm_gains_momentum,
    norm_gains_average,
    expert_in,
    expert_in_momentum,
    expert_in_average,
    expert_down,
    expert_down_momentum,
    expert_down_average,
):
    low = jnp.bfloat16
    full = jnp.float32
    tokens = tokens_in.shape[0]
    model_width = tokens_in.shape[1]
    top_count = routes.shape[1]
    block_rows = router.shape[0]
    experts = router.shape[1]
    hidden_width = shared_in.shape[2]
    grid = Grid(experts)
    capacity = 9 * tokens * top_count // (8 * experts)
    slots = -(-capacity // 16) * 16
    extra_width = -(-(experts + 2) // 128) * 128

    pack_one = jnp.concatenate(
        [attention_in[m].astype(low).T for m in range(3)]
        + [
            router.astype(low),
            norm_gains.astype(low).T,
            jnp.zeros((block_rows, extra_width - experts - 2), low),
        ],
        axis=1,
    )
    pack_out = attention_out.astype(low).T
    pack_shared = jnp.concatenate(
        [shared_in[0].astype(low), shared_in[1].astype(low), shared_down.astype(low).T], axis=1
    )
    position = jnp.arange(tokens, dtype=jnp.int32)
    usable = position < lengths[0]
    named = jnp.any(
        routes.T[None, :, :] == jnp.arange(experts, dtype=jnp.int32)[:, None, None], axis=1
    )
    member = named & usable[None, :]
    earlier = (position[:, None] < position[None, :]).astype(low)
    counted = dot_nn(member.astype(low), earlier)
    slot_of = jnp.where(member, counted, -1.0)
    wanted = grid.at_line * PLANE + (grid.at_plane ^ jnp.arange(PLANE, dtype=jnp.int32))
    choose = (wanted[:, None] == jnp.arange(experts, dtype=jnp.int32)[None, :]).astype(low)

    def widen(rows):
        return jnp.pad(rows, ((0, 0), (0, model_width - rows.shape[1])))

    pair, down = expert_in[0].astype(low), expert_down[0].astype(low)
    plans = (
        gather_plan(pack_one.shape[1] // 128, FIRST_ORDERS),
        gather_plan(model_width // 128, FIRST_ORDERS),
    )
    (all_one, turned_out), down_x, down_y = first_exchange(
        experts, [pack_one, pack_out], plans, down
    )
    line_grads, sent = after(
        (jnp.concatenate([cotangent, widen(slot_of.astype(low))], axis=0), pair), turned_out
    )
    line_grads = grid.line_gather(line_grads)
    pairs = [pair, grid.swap(sent, 1), grid.swap(sent, 2)]
    downs = [down, down_x, down_y]
    all_one = all_one.reshape(model_width, -1)
    turned_out = turned_out.reshape(model_width, model_width)
    extra = all_one[:, 3 * model_width :]
    router_low = extra[:, :experts]
    gains = extra[:, experts : experts + 2].astype(full).T
    gain_one, gain_two = gains[0], gains[1]
    inputs = tokens_in.astype(full)
    rstd_one = lax.rsqrt(jnp.mean(inputs * inputs, axis=-1, keepdims=True) + eps_norm)
    normed_one = (inputs * rstd_one * gain_one).astype(low)
    cosine, sine_table = rope_tables(tokens, HD)
    bias = jnp.where(allowed_keys(lengths[0], key_keep), 0.0, mask_fill)
    query, key_rot, value, attended, hidden, normed_two = attend(
        normed_one, all_one, turned_out, bias, cosine, sine_table, tokens_in, gain_two[None]
    )
    rstd_two = lax.rsqrt(jnp.mean(hidden * hidden, axis=-1, keepdims=True) + eps_norm)

    logits = lax.dot_general(
        router_low, normed_two, (((0,), (1,)), ((), ())), preferred_element_type=full
    )
    logits = jnp.where(named, logits, mask_fill)
    logit_exps = jnp.exp(logits - jnp.max(logits, axis=0, keepdims=True))
    gating = logit_exps / jnp.sum(logit_exps, axis=0, keepdims=True)
    gating_live = jnp.where(member, gating, 0.0)
    gate_words = jnp.concatenate(split_words(gating_live), axis=1)
    line_rows = jnp.concatenate([normed_two, widen(gate_words)], axis=0)
    rising, falling, *weights = second_exchange(experts, line_rows, pairs, downs)
    line_rows = grid.line_gather(line_rows, rising, falling)
    weights = [part.reshape(PLANE, -1, part.shape[-1]) for part in weights]

    kept, grad_parts, result_parts = [], [], []
    last = weights
    for start in range(0, grid.line, 2):
        group = range(start, start + 2)
        line_part = [line_rows[r] for r in group], [line_grads[r] for r in group]
        rows, grads = after(line_part, last)
        slot_rows, gate_rows = [], []
        for part in rows:
            words = dot_nn(choose, part[tokens:, : 3 * tokens])
            gate_row = words[:, :tokens] + words[:, tokens : 2 * tokens] + words[:, 2 * tokens :]
            gate_rows.append(gate_row[:, None])
        for part in grads:
            slot_rows.append(dot_nn(choose, part[tokens:, :tokens])[:, None])
        grad_part, result_part, parts = run_experts(
            wanted, rows, grads, slot_rows, gate_rows, weights, slots
        )
        kept.append(parts)
        last = grad_part
        grad_parts += [grid.shift(part, -r) if r else part for r, part in zip(group, grad_part)]
        result_parts += result_part
    routed_grad = sum(part.astype(full) for part in grad_parts)
    result_parts = after(result_parts, routed_grad)
    routed_result = sum(
        (grid.shift(part, -r) if r else part).astype(full) for r, part in enumerate(result_parts)
    )
    owns, crossed, far = third_exchange(experts, after(kept, last))
    near_x = [add_low(*pair) for pair in zip(owns[1], crossed[1])]
    near_y = [add_low(*pair) for pair in zip(owns[2], crossed[2])]
    edge = far[2].shape[0]
    near_x[0] = add_low(near_x[0], far[0])
    near_y[1] = add_low(near_y[1], far[1])
    near_x[2] = jnp.concatenate([add_low(near_x[2][:edge], far[2]), near_x[2][edge:]], axis=0)
    near_y[2] = jnp.concatenate([near_y[2][:edge], add_low(near_y[2][edge:], far[3])], axis=0)
    arrived = []
    for (gate, up, down), flip in ((near_x, 1), (near_y, 2)):
        arrived.append(grid.swap(jnp.stack([gate, up, down.reshape(up.shape)]), flip))
    gate_grads = routed_grad[tokens:]
    routed_grad = routed_grad[:tokens]
    grad_gating = (
        gate_grads[:, :tokens]
        + gate_grads[:, tokens : 2 * tokens]
        + gate_grads[:, 2 * tokens : 3 * tokens]
    )
    grad_chosen = gating * (grad_gating - jnp.sum(gating * grad_gating, axis=0, keepdims=True))
    grad_logits = grad_chosen.astype(low)
    grad_router = lax.dot_general(
        normed_two, grad_logits, (((0,), (1,)), ((), ())), preferred_element_type=full
    )

    all_shared = lax.all_gather(
        after(pack_shared, weights), ("dp", "expert"), axis=0, tiled=True
    )
    shared_pair = [all_shared[:, m * hidden_width : (m + 1) * hidden_width] for m in range(2)]
    turned_down = all_shared[:, 2 * hidden_width :]
    grad_out = cotangent.astype(full)
    shared_gate = dot_nn(normed_two, shared_pair[0])
    shared_up = dot_nn(normed_two, shared_pair[1])
    shared_silu, shared_slope = silu_parts(shared_gate)
    shared_hidden = (shared_silu * shared_up).astype(low)
    shared_result = dot_nt(shared_hidden, turned_down)
    grad_shared_hidden = dot_nn(cotangent, turned_down)
    grad_shared_gate = (grad_shared_hidden * shared_up * shared_slope).astype(low)
    grad_shared_up = (grad_shared_hidden * shared_silu).astype(low)
    grad_normed_two = dot_nt(grad_shared_gate, shared_pair[0]) + dot_nt(
        grad_shared_up, shared_pair[1]
    )
    grad_normed_two = grad_normed_two + lax.dot_general(
        grad_logits, router_low, (((0,), (1,)), ((), ())), preferred_element_type=full
    )

    grad_normed_two = grad_normed_two + routed_grad
    scaled_two = grad_normed_two * gain_two
    grad_gain_two = jnp.sum(grad_normed_two * hidden * rstd_two, axis=0)
    grad_hidden = (
        grad_out
        + rstd_two * scaled_two
        - hidden * rstd_two**3 * jnp.mean(scaled_two * hidden, axis=-1, keepdims=True)
    )
    grad_branch = grad_hidden.astype(low)
    grads_shared = [
        dot_tn(normed_two, grad_shared_gate).astype(low),
        dot_tn(normed_two, grad_shared_up).astype(low),
        dot_tn(cotangent, shared_hidden).astype(low),
    ]
    *grads_attention, grad_normed_one = attend_back(
        grad_branch,
        normed_one,
        query,
        key_rot,
        value,
        attended,
        all_one,
        turned_out,
        bias,
        cosine,
        sine_table,
    )
    scaled_one = grad_normed_one * gain_one
    grad_gain_one = jnp.sum(grad_normed_one * inputs * rstd_one, axis=0)
    input_grad = (
        grad_hidden
        + rstd_one * scaled_one
        - inputs * rstd_one**3 * jnp.mean(scaled_one * inputs, axis=-1, keepdims=True)
    )
    grad_extra = jnp.concatenate(
        [
            grad_router.astype(low),
            jnp.stack([grad_gain_one, grad_gain_two], axis=1).astype(low),
            jnp.zeros((model_width, extra_width - experts - 2), low),
        ],
        axis=1,
    )
    cut = 7 * 128
    summed_one, summed_two = sum_all(
        experts,
        grads_attention + grads_shared + [grad_extra],
        [
            [
                [(0, 0, model_width), (2, 0, cut)],
                [(1, 0, model_width), (7, 0, extra_width)],
                [(2, cut, model_width - cut)],
            ],
            [
                [(4, 0, hidden_width), (5, 0, hidden_width)],
                [(3, 0, model_width)],
                [(6, 0, hidden_width)],
            ],
        ],
        [],
        (),
    )
    summed_one, summed_two = summed_one.astype(full), summed_two.astype(full)

    output = (hidden + shared_result + routed_result).astype(low)

    arrived = after(arrived, summed_one)
    summed_expert_in = jnp.stack(
        [
            sum(
                part.astype(full)
                for part in (owns[0][i], crossed[0][i], arrived[0][i], arrived[1][i])
            )
            for i in range(2)
        ]
    )[None]
    brought = add_low(arrived[0][2], arrived[1][2]).reshape(owns[0][2].shape)
    summed_expert_down = sum(
        part.astype(full) for part in (owns[0][2], crossed[0][2], brought)
    )[None]

    def take(array, start, width):
        return array[:, start : start + width]

    at = model_width + cut
    summed_value = jnp.concatenate(
        [
            take(summed_one, model_width, cut),
            take(summed_one, at + model_width + extra_width, model_width - cut),
        ],
        axis=1,
    )
    summed_in = jnp.stack(
        [take(summed_one, 0, model_width).T, take(summed_one, at, model_width).T, summed_value.T],
        axis=0,
    )
    at = at + model_width
    summed_router = take(summed_one, at, experts)
    summed_gains = take(summed_one, at + experts, 2).T
    summed_shared_in = jnp.stack(
        [take(summed_two, 0, hidden_width), take(summed_two, hidden_width, hidden_width)], axis=0
    )
    at = 2 * hidden_width
    summed_out = take(summed_two, at, model_width).T
    summed_shared_down = take(summed_two, at + model_width, hidden_width).T
    upd_attn_in = advance(
        attention_in, attention_in_momentum, attention_in_average, summed_in, rate_attention_in
    )
    upd_attn_out = advance(
        attention_out, attention_out_momentum, attention_out_average, summed_out, rate_attention_out
    )
    upd_shared_in = advance(
        shared_in, shared_in_momentum, shared_in_average, summed_shared_in, rate_shared_in
    )
    upd_shared_down = advance(
        shared_down, shared_down_momentum, shared_down_average, summed_shared_down, rate_shared_down
    )
    upd_router = advance(router, router_momentum, router_average, summed_router, rate_router)
    upd_gains = advance(
        norm_gains, norm_gains_momentum, norm_gains_average, summed_gains, rate_gains
    )
    upd_expert_in = advance(
        expert_in, expert_in_momentum, expert_in_average, summed_expert_in, rate_expert_in
    )
    upd_expert_down = advance(
        expert_down, expert_down_momentum, expert_down_average, summed_expert_down, rate_expert_down
    )
    return (
        output,
        input_grad,
        upd_attn_in[0],
        upd_attn_in[1],
        upd_attn_in[2],
        upd_attn_out[0],
        upd_attn_out[1],
        upd_attn_out[2],
        upd_shared_in[0],
        upd_shared_in[1],
        upd_shared_in[2],
        upd_shared_down[0],
        upd_shared_down[1],
        upd_shared_down[2],
        upd_router[0],
        upd_router[1],
        upd_router[2],
        upd_gains[0],
        upd_gains[1],
        upd_gains[2],
        upd_expert_in[0],
        upd_expert_in[1],
        upd_expert_in[2],
        upd_expert_down[0],
        upd_expert_down[1],
        upd_expert_down[2],
    )


def solution(mesh):
    in_specs = (
        P(("dp", "expert"), None),
        P(("dp", "expert")),
        P(("dp", "expert")),
        P(("dp", "expert"), None),
        P(("dp", "expert"), None),
        P(None, None, ("dp", "expert")),
        P(None, None, ("dp", "expert")),
        P(None, None, ("dp", "expert")),
        P(None, ("dp", "expert")),
        P(None, ("dp", "expert")),
        P(None, ("dp", "expert")),
        P(None, ("dp", "expert"), None),
        P(None, ("dp", "expert"), None),
        P(None, ("dp", "expert"), None),
        P(None, ("dp", "expert")),
        P(None, ("dp", "expert")),
        P(None, ("dp", "expert")),
        P(("dp", "expert"), None),
        P(("dp", "expert"), None),
        P(("dp", "expert"), None),
        P(None, ("dp", "expert")),
        P(None, ("dp", "expert")),
        P(None, ("dp", "expert")),
        P("expert", None, "dp", None),
        P("expert", None, "dp", None),
        P("expert", None, "dp", None),
        P("expert", "dp", None),
        P("expert", "dp", None),
        P("expert", "dp", None),
    )
    out_specs = (
        P(("dp", "expert"), None),
        P(("dp", "expert"), None),
        P(None, None, ("dp", "expert")),
        P(None, None, ("dp", "expert")),
        P(None, None, ("dp", "expert")),
        P(None, ("dp", "expert")),
        P(None, ("dp", "expert")),
        P(None, ("dp", "expert")),
        P(None, ("dp", "expert"), None),
        P(None, ("dp", "expert"), None),
        P(None, ("dp", "expert"), None),
        P(None, ("dp", "expert")),
        P(None, ("dp", "expert")),
        P(None, ("dp", "expert")),
        P(("dp", "expert"), None),
        P(("dp", "expert"), None),
        P(("dp", "expert"), None),
        P(None, ("dp", "expert")),
        P(None, ("dp", "expert")),
        P(None, ("dp", "expert")),
        P("expert", None, "dp", None),
        P("expert", None, "dp", None),
        P("expert", None, "dp", None),
        P("expert", "dp", None),
        P("expert", "dp", None),
        P("expert", "dp", None),
    )
    return jax.shard_map(local, mesh=mesh, in_specs=in_specs, out_specs=out_specs, check_vma=False)
```

```python
import functools

import jax
import jax.numpy as jnp
from jax import lax
from jax.experimental import pallas as pl
from jax.experimental.pallas import tpu as pltpu
from jax.sharding import PartitionSpec as P

HD = 128
STEP = 4


eps_norm = 1e-06
theta_base = 10000.0
momentum_decay = 0.9
mask_fill = -1e30
rate_attention_in = 2e-05
rate_attention_out = 0.002
rate_shared_in = 3e-05
rate_shared_down = 0.0002
rate_router = 1.5e-05
rate_gains = 0.0002
rate_expert_in = 0.0004
rate_expert_down = 0.008


def rope_tables(length, head_width):
    half_width = head_width // 2
    frequency = theta_base ** (-(jnp.arange(half_width, dtype=jnp.float32) * 2.0 / head_width))
    angles = jnp.arange(length, dtype=jnp.float32)[:, None] * frequency[None, :]
    cosine, sine_table = jnp.cos(angles), jnp.sin(angles)
    return (
        jnp.concatenate([cosine, cosine], axis=1),
        jnp.concatenate([-sine_table, sine_table], axis=1),
    )


def allowed_keys(length, keep_flags):
    amount = keep_flags.shape[0]
    position = jnp.arange(amount)
    causal = position[None, :] <= position[:, None]
    usable = (position < length) & (keep_flags == 1)
    return causal & (usable[None, :] | (position[None, :] == position[:, None]))


def silu_parts(values):
    logistic = jax.nn.sigmoid(values)
    return (values * logistic, logistic * (1.0 + values * (1.0 - logistic)))


def advance(weight, moment, average, gradient, step_rate):
    moment_new = momentum_decay * moment + gradient
    weight_new = weight - step_rate * (gradient + momentum_decay * moment_new)
    average_new = average + (weight_new - average) / (STEP + 1)
    return (weight_new, moment_new, average_new)


def dot_nn(a, b):
    return lax.dot_general(a, b, (((1,), (0,)), ((), ())), preferred_element_type=jnp.float32)


def dot_nt(a, b):
    return lax.dot_general(a, b, (((1,), (1,)), ((), ())), preferred_element_type=jnp.float32)


def dot_tn(a, b):
    return lax.dot_general(a, b, (((0,), (0,)), ((), ())), preferred_element_type=jnp.float32)


PLANE = 4
MESH = pl.DeviceIdType.MESH


class Spot:
    def __init__(self, line):
        here = lax.axis_index("expert")
        self.line = line
        self.core = lax.axis_index("dp")
        self.at = lax.div(here, PLANE)
        rest = lax.rem(here, PLANE)
        self.y, self.x = lax.div(rest, 2), lax.rem(rest, 2)

    def chip(self, at, y, x):
        return (self.core, at * PLANE + y * 2 + x)

    def around(self, amount):
        return lax.rem(self.at + amount + self.line, self.line)

    def partner(self, way):
        if way == "core":
            return (1 - self.core, self.at * PLANE + self.y * 2 + self.x)
        if way == "x":
            return self.chip(self.at, self.y, 1 - self.x)
        if way == "y":
            return self.chip(self.at, 1 - self.y, self.x)
        return self.chip(self.around(1 if way == "up" else -1), self.y, self.x)


def meet(spot):
    barrier = pltpu.get_barrier_semaphore()
    for way in ("core", "x", "y", "up", "down"):
        pl.semaphore_signal(barrier, inc=1, device_id=spot.partner(way), device_id_type=MESH)
    pl.semaphore_wait(barrier, 5)


class Moves:
    def __init__(self, spot, send_sems, recv_sems, local_sems):
        self.spot, self.send_sems, self.recv_sems = spot, send_sems, recv_sems
        self.local_sems = local_sems
        self.made, self.kept, self.loose = 0, 0, []

    def start(self, source, target, way, later=False):
        copy = pltpu.make_async_remote_copy(
            src_ref=source,
            dst_ref=target,
            send_sem=self.send_sems.at[self.made],
            recv_sem=self.recv_sems.at[self.made],
            device_id=self.spot.partner(way),
            device_id_type=MESH,
        )
        self.made += 1
        copy.start()
        if later:
            self.loose.append(copy)
        return copy

    def keep(self, source, target, later=False):
        copy = pltpu.make_async_copy(source, target, self.local_sems.at[self.kept])
        self.kept += 1
        copy.start()
        if later:
            self.loose.append(copy)
        return copy

    def finish(self):
        for copy in self.loose:
            copy.wait()


def in_steps(chains):
    while chains:
        left = []
        for chain in chains:
            try:
                next(chain)
                left.append(chain)
            except StopIteration:
                pass
        chains = left
        yield


def in_turn(chains):
    for _ in in_steps(chains):
        pass


def place_chain(moves, source, buffer, target):
    copy = moves.keep(source, buffer)
    yield
    copy.wait()
    moves.keep(buffer, target, later=True)


def core_chain(moves, own, whole, buffer):
    core = moves.spot.core
    moves.start(own, whole.at[core], "core", later=True)
    return place_chain(moves, own, buffer, whole.at[core])


def dense_chain(moves, whole, columns, order):
    spot = moves.spot
    half, rest = spot.line // 2, (spot.line - 1) // 2
    everything = slice(None)
    held = {"z": spot.at, "y": spot.y, "x": spot.x}

    def region(**other):
        at = dict(held, **other)
        return whole.at[spot.core, at["z"], at["y"], at["x"], everything, columns]

    def forward(part):
        moves.start(part, part, "core", later=True)

    for stage, dim in enumerate(order):
        if dim == "z":
            up = down = None
            for i in range(1, half + 1):
                part = region(z=spot.around(1 - i))
                up = moves.start(part, part, "up")
                if i <= rest:
                    part = region(z=spot.around(i - 1))
                    down = moves.start(part, part, "down")
                if stage == 0 and i == 1:
                    forward(region())
                yield
                up.wait()
                forward(region(z=spot.around(-i)))
                if i <= rest:
                    down.wait()
                    forward(region(z=spot.around(i)))
        else:
            part = region()
            copy = moves.start(part, part, dim)
            if stage == 0:
                forward(region())
            yield
            copy.wait()
            forward(region(**{dim: 1 - held[dim]}))
        held[dim] = everything


ORDERS = ("xyz", "yzx", "zxy", "zyx")


def first_kernel(line, plans, *refs):
    count = len(plans)
    shards, down, refs = refs[:count], refs[count], refs[count + 1 :]
    results, over_x, over_y, refs = refs[:count], refs[count], refs[count + 1], refs[count + 2 :]
    wholes, refs = refs[:count], refs[count:]
    spot = Spot(line)
    meet(spot)
    moves = Moves(spot, *refs)
    loads = [
        moves.keep(shards[n], wholes[n].at[spot.core, spot.at, spot.y, spot.x])
        for n in range(count)
    ]
    for copy in loads:
        copy.wait()
    chains = []
    for n, plan in enumerate(plans):
        start = 0
        for order, width in plan:
            columns = slice(start, start + width)
            chains.append(dense_chain(moves, wholes[n], columns, ORDERS[order]))
            start += width
    stages = 0
    for _ in in_steps(chains):
        stages += 1
        if stages == 1:
            moves.start(down, over_x, "x", later=True)
            moves.start(down, over_y, "y", later=True)
    moves.finish()
    stores = [moves.keep(wholes[n], results[n]) for n in range(count)]
    for copy in stores:
        copy.wait()


def hbm(count):
    return [pl.BlockSpec(memory_space=pl.ANY)] * count


def semaphores(remote, local):
    return [
        pltpu.SemaphoreType.DMA((remote,)),
        pltpu.SemaphoreType.DMA((remote,)),
        pltpu.SemaphoreType.DMA((local,)),
    ]


def both_halves(array):
    return jax.ShapeDtypeStruct((2,) + array.shape, array.dtype)


def first_exchange(experts, shards, plans, down):
    line = experts // PLANE
    count = len(shards)
    remote = sum(len(plan) for plan in plans) * (2 * line + 3) + 2
    out = pl.pallas_call(
        functools.partial(first_kernel, line, plans),
        out_shape=[
            jax.ShapeDtypeStruct((2, line, 2, 2) + shard.shape, shard.dtype) for shard in shards
        ]
        + [jax.ShapeDtypeStruct(down.shape, down.dtype)] * 2,
        in_specs=hbm(count + 1),
        out_specs=hbm(count + 2),
        scratch_shapes=[
            pltpu.VMEM((2, line, 2, 2) + shard.shape, shard.dtype) for shard in shards
        ]
        + semaphores(remote, 2 * count),
        compiler_params=pltpu.CompilerParams(
            collective_id=1, has_side_effects=True, vmem_limit_bytes=60 * 1024 * 1024
        ),
    )(*shards, down)
    return out[:count], out[count], out[count + 1]


def second_kernel(line, *refs):
    rows, pairs, downs, refs = refs[0], refs[1:4], refs[4:7], refs[7:]
    rising, falling, wholes, refs = refs[0], refs[1], refs[2:5], refs[5:]
    buffers, refs = refs[:9], refs[9:]
    spot = Spot(line)
    meet(spot)
    moves = Moves(spot, *refs)
    core = spot.core
    gate, up, down = wholes
    (_, pair_x, pair_y), (_, down_x, down_y) = pairs, downs
    half = down_x.shape[0] // 2

    def far_chain(source, target, way):
        copy = moves.start(source, target, way)
        yield
        copy.wait()
        moves.start(target, target, "core", later=True)

    moves.start(rows, rising, "up", later=True)
    moves.start(rows, falling, "down", later=True)
    upper, lower = pl.ds(0, half), pl.ds(half, half)
    in_turn(
        [
            far_chain(pair_y.at[1], up.at[3, core], "x"),
            far_chain(pair_x.at[0], gate.at[3, core], "y"),
            far_chain(down_y.at[lower], down.at[3, core, lower], "x"),
            far_chain(down_x.at[upper], down.at[3, core, upper], "y"),
        ]
        + [
            core_chain(moves, half_of, wholes[i].at[q], buffers[3 * q + i])
            for q in range(3)
            for i, half_of in enumerate((pairs[q].at[0], pairs[q].at[1], downs[q]))
        ]
    )
    moves.finish()


def second_exchange(experts, rows, pairs, downs):
    line = experts // PLANE
    low = rows.dtype
    shapes = [pairs[0].shape[1:]] * 2 + [downs[0].shape]
    return pl.pallas_call(
        functools.partial(second_kernel, line),
        out_shape=[jax.ShapeDtypeStruct(rows.shape, low)] * 2
        + [jax.ShapeDtypeStruct((PLANE, 2) + shape, low) for shape in shapes],
        in_specs=hbm(7),
        out_specs=hbm(5),
        scratch_shapes=[pltpu.VMEM(shape, low) for shape in shapes * 3] + semaphores(19, 18),
        compiler_params=pltpu.CompilerParams(
            collective_id=3, has_side_effects=True, vmem_limit_bytes=60 * 1024 * 1024
        ),
    )(rows, *pairs, *downs)


def packed(half, hidden_width, down_half, width):
    edge, more = down_half // 2, width - hidden_width
    below = 2 * half + down_half
    full = slice(0, hidden_width)
    rest = slice(hidden_width, width)
    places = [
        (0, slice(0, half), full, slice(0, half), full),
        (1, slice(half, 2 * half), full, slice(0, half), full),
        (2, slice(2 * half, 2 * half + edge), full, slice(0, edge), full),
        (2, slice(2 * half + edge, below), full, slice(edge, down_half), full),
        (2, slice(below, below + edge), slice(0, more), slice(0, edge), rest),
        (2, slice(below, below + edge), slice(more, 2 * more), slice(edge, down_half), rest),
    ]
    return places, below + edge, 2 * more


def third_kernel(line, groups, *refs):
    low, full = jnp.bfloat16, jnp.float32
    kept = [refs[5 * r : 5 * r + 5] for r in range(groups)]
    refs = refs[5 * groups :]
    owns, crossed, nears, refs = refs[:3], refs[3:6], refs[6:8], refs[8:]
    loaded, refs = [refs[:5], refs[5:10]], refs[10:]
    results, refs = [refs[:6], refs[6:12]], refs[12:]
    far_box, far_in, near_box, down_grad, refs = refs[:3], refs[3:7], refs[7:9], refs[9], refs[10:]
    spot = Spot(line)
    meet(spot)
    moves = Moves(spot, *refs)
    order = (3, 1, 2, 0)
    slots = kept[0][0].shape[1]
    loads = {}
    rows_half, hidden_width = results[0][0].shape
    down_half, width = results[0][2].shape
    edge = down_half // 2
    places, _, used = packed(rows_half, hidden_width, down_half, width)

    def load(n):
        loads[n] = [
            moves.keep(kept[r][i].at[order[n]], loaded[n % 2][i].at[pl.ds(r * slots, slots)])
            for r in range(groups)
            for i in range(5)
        ]

    def add(target, source):
        target[...] = (target[...].astype(full) + source[...].astype(full)).astype(low)

    load(0)
    for box in near_box:
        spare = (slice(2 * rows_half + down_half, box.shape[0]), slice(used, hidden_width))
        box[spare] = jnp.zeros((edge, hidden_width - used), low)
    sent = {}

    def weights(n):
        if n + 1 < PLANE:
            load(n + 1)
        for copy in loads[n]:
            copy.wait()
        rows, inner, gated, grad_gate, grad_up = loaded[n % 2]
        buffers = results[n % 2]
        down_grad[...] = dot_tn(inner[...], gated[...]).astype(low)
        q = order[n]
        for which in (1, 0):
            place = jnp.bitwise_xor(spot.core, which)
            gate_out, up_out, down_out = buffers[3 * which : 3 * which + 3]
            part = rows[:, pl.ds(pl.multiple_of(place * rows_half, 128), rows_half)]
            gate_out[...] = dot_tn(part, grad_gate[...]).astype(low)
            up_out[...] = dot_tn(part, grad_up[...]).astype(low)
            down_out[...] = down_grad[pl.ds(pl.multiple_of(place * down_half, 16), down_half), :]
            if which and q in (0, 3):
                targets = crossed if q == 0 else far_box
                sent[n] = [moves.start(buffers[3 + i], targets[i], "core") for i in range(3)]
            elif which:
                sent[n] = [
                    moves.start(
                        buffers[3 + i].at[rows_at, columns_at],
                        near_box[q - 1].at[to_rows, to_columns],
                        "core",
                    )
                    for i, to_rows, to_columns, rows_at, columns_at in places
                ]
            elif q == 0:
                sent[n] += [moves.keep(buffers[i], owns[i]) for i in range(3)]

    def far():
        for copy in sent[0]:
            copy.wait()
        mine = results[0][:3]
        for i in range(3):
            add(far_box[i], mine[i])
        upper, lower = pl.ds(0, edge), pl.ds(edge, edge)
        return [
            moves.start(far_box[0], far_in[0], "y"),
            moves.start(far_box[1], far_in[1], "x"),
            moves.start(far_box[2].at[upper], far_in[2], "y"),
            moves.start(far_box[2].at[lower], far_in[3], "x"),
        ]

    def near(n):
        for copy in sent[n]:
            copy.wait()
        box = near_box[order[n] - 1]
        for i, to_rows, to_columns, rows_at, columns_at in places:
            add(box.at[to_rows, to_columns], results[n % 2][i].at[rows_at, columns_at])

    weights(0)
    weights(1)
    across = far()
    weights(2)
    near(1)
    weights(3)
    near(2)
    for copy in across:
        copy.wait()
    rest, full_width = slice(hidden_width, width), slice(0, hidden_width)
    for box, i, source in ((near_box[0], 0, far_in[0]), (near_box[1], 1, far_in[1])):
        _, to_rows, to_columns, _, _ = places[i]
        add(box.at[to_rows, to_columns], source)
    for box, i, source in ((near_box[0], 0, far_in[2]), (near_box[1], 1, far_in[3])):
        for index, columns_at in ((2 + i, full_width), (4 + i, rest)):
            _, to_rows, to_columns, _, _ = places[index]
            add(box.at[to_rows, to_columns], source.at[:, columns_at])
    stores = [moves.keep(box, target) for box, target in zip(near_box, nears)]
    for copy in sent[3] + stores:
        copy.wait()


def third_exchange(experts, kept):
    line = experts // PLANE
    low = jnp.bfloat16
    rows, inner = kept[0][0], kept[0][1]
    slots, width, hidden_width = rows.shape[1], rows.shape[2], inner.shape[2]
    half, down_half = width // 2, hidden_width // 2
    pieces = [(half, hidden_width), (half, hidden_width), (down_half, width)]
    far = pieces[:2] + [(down_half // 2, width)] * 2
    package = (packed(half, hidden_width, down_half, width)[1], hidden_width)
    out = pl.pallas_call(
        functools.partial(third_kernel, line, len(kept)),
        out_shape=[jax.ShapeDtypeStruct(size, low) for size in pieces * 2 + [package] * 2],
        in_specs=hbm(5 * len(kept)),
        out_specs=hbm(8),
        scratch_shapes=[
            pltpu.VMEM((len(kept) * slots, array.shape[2]), low) for array in list(kept[0]) * 2
        ]
        + [pltpu.VMEM(size, low) for size in pieces * 4]
        + [pltpu.VMEM(size, low) for size in pieces + far + [package] * 2]
        + [pltpu.VMEM((hidden_width, width), low)]
        + semaphores(2 * 3 + 2 * 6 + 4, 5 * PLANE * len(kept) + 3 + 2),
        compiler_params=pltpu.CompilerParams(
            collective_id=4, has_side_effects=True, vmem_limit_bytes=62 * 1024 * 1024
        ),
    )(*[array for parts in kept for array in parts])
    return out[:3], out[3:6], out[6:]


def sum_plans(width, hidden_width, extra_width):
    edge = width * 8 // 10
    half = width // 2
    gate_edge = hidden_width * 5 // 7
    return (
        (((0, 0, edge),), ((1, 0, half),), ((0, edge, width - edge),)),
        (((2, 0, edge),), ((1, half, width - half),), ((2, edge, width - edge),)),
        (
            ((3, 0, width - 128),),
            ((4, 0, gate_edge),),
            ((3, width - 128, 128), (7, 0, extra_width)),
        ),
        (
            ((5, 0, hidden_width), (4, gate_edge, hidden_width - gate_edge)),
            ((6, 0, gate_edge),),
            ((6, gate_edge, hidden_width - gate_edge),),
        ),
    )


def total_chain(moves, owns, crossed, arrived, totals, buffers):
    full = jnp.float32
    half, hidden_width = owns[0].shape
    down_half, width = owns[2].shape
    edge = down_half // 2
    places, _, _ = packed(half, hidden_width, down_half, width)
    jobs = []
    for i in range(2):
        for rows in range(0, half, half // 4):
            jobs.append((i, rows, half // 4))
    for rows in range(0, down_half, edge // 2):
        jobs.append((2, rows, edge // 2))
    loads, stores = {}, {}

    def box(n, i):
        wide = jobs[n][0] == 2
        return buffers[10 * (n % 2) + 5 * wide + i]

    def load(n):
        which, start, rows = jobs[n]
        at = pl.ds(start, rows)
        copies = [(owns[which].at[at], box(n, 0)), (crossed[which].at[at], box(n, 1))]
        for k, package in enumerate(arrived):
            for part, to_rows, to_columns, rows_at, columns_at in places:
                inside = rows_at.start <= start < rows_at.stop
                if part == which and inside:
                    copies.append(
                        (
                            package.at[
                                pl.ds(to_rows.start + start - rows_at.start, rows), to_columns
                            ],
                            box(n, 2 + k).at[:, columns_at],
                        )
                    )
        loads[n] = [moves.keep(source, target) for source, target in copies]

    load(0)
    for n, (which, start, rows) in enumerate(jobs):
        if n + 1 < len(jobs):
            load(n + 1)
        for copy in loads[n]:
            copy.wait()
        if n >= 2:
            for copy in stores[n - 2]:
                copy.wait()
        total = box(n, 4)
        total[...] = sum(box(n, i)[...].astype(full) for i in range(4)).astype(total.dtype)
        at = pl.ds(start, rows)
        target = totals[0].at[which, at] if which < 2 else totals[1].at[at]
        stores[n] = [moves.keep(total, target)]
        if n % 2:
            yield
    for n in (len(jobs) - 2, len(jobs) - 1):
        for copy in stores[n]:
            copy.wait()


def total_buffers(half, hidden_width, down_half, width, dtype):
    shapes = [(half // 4, hidden_width)] * 5 + [(down_half // 4, width)] * 5
    return [pltpu.VMEM(shape, dtype) for shape in shapes * 2]


def sum_kernel(line, plans, arrays, *refs):
    count = len(plans)
    grads, refs = refs[:arrays], refs[arrays:]
    owns, crossed, arrived, refs = refs[:3], refs[3:6], refs[6:8], refs[8:]
    sums, refs = refs[:arrays], refs[arrays:]
    totals, refs = refs[:2], refs[2:]
    buffers, refs = refs[:20], refs[20:]
    kept, refs = refs[: 3 * count], refs[3 * count :]
    core_in, refs = refs[: 3 * count], refs[3 * count :]
    first_in, refs = refs[: 3 * count], refs[3 * count :]
    second_in, refs = refs[: 3 * count], refs[3 * count :]
    third_in, refs = refs[: 3 * count], refs[3 * count :]
    spot = Spot(line)
    meet(spot)
    moves = Moves(spot, *refs)
    half, rest = line // 2, (line - 1) // 2
    everything = slice(None)
    orders = ("xyz", "yzx", "zxy")

    loads, swaps = [], []
    at = 0
    for n, plan in enumerate(plans):
        for o, pieces in enumerate(plan):
            mine, theirs = [], []
            start = 0
            for which, first, width in pieces:
                ref = grads[which]
                source = slice(first, first + width)
                target = slice(start, start + width)
                mine.append(
                    moves.keep(
                        ref.at[spot.core, :, :, :, :, source],
                        kept[3 * n + o].at[:, :, :, :, target],
                    )
                )
                theirs.append(
                    moves.start(
                        ref.at[1 - spot.core, :, :, :, :, source],
                        core_in[3 * n + o].at[:, :, :, :, target],
                        "core",
                    )
                )
                at += 1
                start += width
            loads.append(mine)
            swaps.append(theirs)

    def add(target, source):
        lead = target.shape[:-2]
        total = 1
        for extent in lead:
            total *= extent

        def one(i, carry):
            index = []
            for extent in reversed(lead):
                index.insert(0, lax.rem(i, extent))
                i = lax.div(i, extent)
            index = tuple(index)
            target[index] = (
                target[index].astype(jnp.float32) + source[index].astype(jnp.float32)
            ).astype(target.dtype)
            return carry

        lax.fori_loop(0, total, one, 0)

    def chain(n, o):
        buffer = kept[3 * n + o]
        mine, theirs = loads[3 * n + o], swaps[3 * n + o]
        for copy in mine:
            copy.wait()
        for copy in theirs:
            copy.wait()
        add(buffer, core_in[3 * n + o])
        inbox = [first_in[3 * n + o], second_in[3 * n + o], third_in[3 * n + o]]
        held = {"z": everything, "y": everything, "x": everything}

        def region(**other):
            at = dict(held, **other)
            return buffer.at[at["z"], at["y"], at["x"]]

        for stage, dim in enumerate(orders[o]):
            box = inbox[stage]
            if dim == "z":
                up = down = None
                for i in range(half, 0, -1):
                    down = moves.start(region(z=spot.around(-i)), box.at[i - 1], "down")
                    if i <= rest:
                        up = moves.start(region(z=spot.around(i)), box.at[half + i - 1], "up")
                    yield
                    down.wait()
                    add(region(z=spot.around(1 - i)), box.at[i - 1])
                    if i <= rest:
                        up.wait()
                        add(region(z=spot.around(i - 1)), box.at[half + i - 1])
                held[dim] = spot.at
            else:
                own = spot.y if dim == "y" else spot.x
                copy = moves.start(region(**{dim: 1 - own}), box, dim)
                yield
                copy.wait()
                held[dim] = own
                add(region(), box)
        results, start = [], 0
        for which, first, width in plans[n][o]:
            source = region().at[:, slice(start, start + width)]
            results.append(moves.keep(source, sums[which].at[:, slice(first, first + width)]))
            start += width
        yield
        for result in results:
            result.wait()

    chains = [chain(n, o) for n in range(count) for o in range(3)]
    chains.append(total_chain(moves, owns, crossed, arrived, totals, buffers))
    in_turn(chains)


def sum_all(experts, grads, plans, owns, crossed, arrived):
    line = experts // PLANE
    half, rest = line // 2, (line - 1) // 2
    rows = grads[0].shape[0] // (2 * experts)
    dtype = grads[0].dtype
    operands = [array.reshape(2, line, 2, 2, rows, array.shape[1]) for array in grads]
    shapes = [jax.ShapeDtypeStruct((rows, array.shape[1]), dtype) for array in grads]
    boxes = [[], [], [], [], []]
    for plan in plans:
        for o, pieces in enumerate(plan):
            steps = half + rest
            block = (rows, sum(width for _, _, width in pieces))
            boxes[0].append((line, 2, 2) + block)
            boxes[1].append((line, 2, 2) + block)
            if o == 0:
                inboxes = [(line, 2), (line,), (steps,)]
            elif o == 1:
                inboxes = [(line, 2), (steps, 2), ()]
            else:
                inboxes = [(steps, 2, 2), (2,), ()]
            for i, lead in enumerate(inboxes):
                boxes[2 + i].append(lead + block)
    count = len(plans)
    given = sum(len(pieces) for plan in plans for pieces in plan)
    number = given + 3 * count * (line + 1)
    others = list(owns) + list(crossed) + list(arrived)
    shapes += [
        jax.ShapeDtypeStruct((2,) + owns[0].shape, dtype),
        jax.ShapeDtypeStruct(owns[2].shape, dtype),
    ]
    return pl.pallas_call(
        functools.partial(sum_kernel, line, plans, len(grads)),
        out_shape=shapes,
        in_specs=hbm(len(operands) + len(others)),
        out_specs=hbm(len(grads) + 2),
        scratch_shapes=total_buffers(*owns[0].shape, *owns[2].shape, dtype)
        + [pltpu.VMEM(shape, dtype) for kind in boxes for shape in kind]
        + semaphores(number, 2 * given + 12 * 7),
        compiler_params=pltpu.CompilerParams(
            collective_id=2, has_side_effects=True, vmem_limit_bytes=60 * 1024 * 1024
        ),
    )(*operands, *others)


def turn(values, cosine, sine_table):
    return values * cosine + pltpu.roll(values, HD // 2, 1) * sine_table


def turn_back(values, cosine, sine_table):
    return values * cosine - pltpu.roll(values, HD // 2, 1) * sine_table


def probabilities(query, key, bias):
    scores = dot_nt(query, key) * HD ** (-0.5) + bias
    exps = jnp.exp(scores - jnp.max(scores, axis=1, keepdims=True))
    return exps / jnp.sum(exps, axis=1, keepdims=True)


def attend_kernel(
    steps,
    normed,
    query_weight,
    key_weight,
    value_weight,
    out_weight,
    bias,
    cosine,
    sine_table,
    inputs,
    gain,
    query_out,
    key_out,
    value_out,
    attended_out,
    hidden_out,
    normed_out,
):
    step = pl.program_id(0)
    low = jnp.bfloat16
    n1 = normed[...]
    cos, sin = cosine[...], sine_table[...]
    query = dot_nt(n1, query_weight[...])
    key = dot_nt(n1, key_weight[...])
    value_out[...] = dot_nt(n1, value_weight[...]).astype(low)
    for part in range(query.shape[1] // HD):
        columns = slice(part * HD, (part + 1) * HD)
        q = turn(query[:, columns], cos, sin).astype(low)
        k = turn(key[:, columns], cos, sin).astype(low)
        query_out[:, columns] = q
        key_out[:, columns] = k
        probs = probabilities(q, k, bias[...])
        attended_out[:, columns] = dot_nn(probs.astype(low), value_out[:, columns]).astype(low)
    branch = dot_nt(attended_out[...], out_weight[...])

    @pl.when(step == 0)
    def _():
        hidden_out[...] = inputs[...].astype(jnp.float32) + branch

    @pl.when(step > 0)
    def _():
        hidden_out[...] += branch

    @pl.when(step == steps - 1)
    def _():
        hidden = hidden_out[...]
        rstd = lax.rsqrt(jnp.mean(hidden * hidden, axis=1, keepdims=True) + eps_norm)
        normed_out[...] = (hidden * rstd * gain[...]).astype(low)


def attend(normed, weights, out_weight, bias, cosine, sine_table, inputs, gain):
    tokens, width = normed.shape
    group = 2 * HD
    steps = width // group
    low = jnp.bfloat16
    whole = lambda *shape: pl.BlockSpec(shape, lambda i: (0,) * len(shape))
    columns = pl.BlockSpec((tokens, group), lambda i: (0, i))
    return pl.pallas_call(
        functools.partial(attend_kernel, steps),
        grid=(steps,),
        in_specs=[whole(tokens, width)]
        + [pl.BlockSpec((group, width), lambda i, m=m: (i, m)) for m in range(3)]
        + [
            pl.BlockSpec((width, group), lambda i: (0, i)),
            whole(tokens, tokens),
            whole(tokens, HD),
            whole(tokens, HD),
            whole(tokens, width),
            whole(1, width),
        ],
        out_specs=[columns] * 4 + [whole(tokens, width)] * 2,
        out_shape=[jax.ShapeDtypeStruct((tokens, width), low)] * 4
        + [
            jax.ShapeDtypeStruct((tokens, width), jnp.float32),
            jax.ShapeDtypeStruct((tokens, width), low),
        ],
        compiler_params=pltpu.CompilerParams(vmem_limit_bytes=48 * 1024 * 1024),
        cost_estimate=pl.CostEstimate(
            flops=8 * tokens * width * width, bytes_accessed=20 * width * width, transcendentals=0
        ),
    )(normed, weights, weights, weights, out_weight, bias, cosine, sine_table, inputs, gain)


def attend_back_kernel(
    grad_branch,
    normed,
    query_in,
    key_in,
    value_in,
    attended_in,
    query_weight,
    key_weight,
    value_weight,
    out_weight,
    bias,
    cosine,
    sine_table,
    grad_query_weight,
    grad_key_weight,
    grad_value_weight,
    grad_out_weight,
    grad_normed,
    grads,
):
    step = pl.program_id(0)
    low = jnp.bfloat16
    da = grad_branch[...]
    n1 = normed[...]
    cos, sin = cosine[...], sine_table[...]
    scaling = HD ** (-0.5)
    group = query_in.shape[1]
    grad_out_weight[...] = dot_tn(da, attended_in[...]).astype(low)
    grad_attended = dot_nn(da, out_weight[...]).astype(low)
    for part in range(group // HD):
        columns = slice(part * HD, (part + 1) * HD)
        q, k, v = query_in[:, columns], key_in[:, columns], value_in[:, columns]
        do = grad_attended[:, columns]
        probs = probabilities(q, k, bias[...])
        grad_probs = dot_nt(do, v)
        grad_scores = probs * (grad_probs - jnp.sum(probs * grad_probs, axis=1, keepdims=True))
        grad_scores = grad_scores.astype(low)
        grads[0, :, columns] = turn_back(dot_nn(grad_scores, k) * scaling, cos, sin).astype(low)
        grads[1, :, columns] = turn_back(dot_tn(grad_scores, q) * scaling, cos, sin).astype(low)
        grads[2, :, columns] = dot_tn(probs.astype(low), do).astype(low)
    grad_query_weight[...] = dot_tn(grads[0], n1).astype(low)
    grad_key_weight[...] = dot_tn(grads[1], n1).astype(low)
    grad_value_weight[...] = dot_tn(grads[2], n1).astype(low)
    total = (
        dot_nn(grads[0], query_weight[...])
        + dot_nn(grads[1], key_weight[...])
        + dot_nn(grads[2], value_weight[...])
    )

    @pl.when(step == 0)
    def _():
        grad_normed[...] = total

    @pl.when(step > 0)
    def _():
        grad_normed[...] += total


def attend_back(
    grad_branch, normed, query, key, value, attended, weights, out_weight, bias, cosine, sine_table
):
    tokens, width = normed.shape
    group = 2 * HD
    steps = width // group
    low = jnp.bfloat16
    whole = lambda *shape: pl.BlockSpec(shape, lambda i: (0,) * len(shape))
    columns = pl.BlockSpec((tokens, group), lambda i: (0, i))
    return pl.pallas_call(
        attend_back_kernel,
        grid=(steps,),
        in_specs=[whole(tokens, width)] * 2
        + [columns] * 4
        + [pl.BlockSpec((group, width), lambda i, m=m: (i, m)) for m in range(3)]
        + [
            pl.BlockSpec((width, group), lambda i: (0, i)),
            whole(tokens, tokens),
            whole(tokens, HD),
            whole(tokens, HD),
        ],
        out_specs=[pl.BlockSpec((group, width), lambda i: (i, 0))] * 3
        + [pl.BlockSpec((width, group), lambda i: (0, i)), whole(tokens, width)],
        out_shape=[jax.ShapeDtypeStruct((width, width), low)] * 4
        + [jax.ShapeDtypeStruct((tokens, width), jnp.float32)],
        scratch_shapes=[pltpu.VMEM((3, tokens, group), low)],
        compiler_params=pltpu.CompilerParams(vmem_limit_bytes=48 * 1024 * 1024),
        cost_estimate=pl.CostEstimate(
            flops=16 * tokens * width * width, bytes_accessed=40 * width * width, transcendentals=0
        ),
    )(
        grad_branch,
        normed,
        query,
        key,
        value,
        attended,
        weights,
        weights,
        weights,
        out_weight,
        bias,
        cosine,
        sine_table,
    )


def expert_kernel(count, numbers, *refs):
    low, full = jnp.bfloat16, jnp.float32
    rows_in, grads_in, slots_in, gates_in = [refs[i * count : (i + 1) * count] for i in range(4)]
    gate_weight, up_weight, down_weight, *refs = refs[4 * count :]
    grad_total, result_total = refs[:count], refs[count : 2 * count]
    rows_out, inner_out, gated_out, grad_gate_out, grad_up_out = refs[2 * count : 2 * count + 5]
    hot_all, grad_all, result_all, word_sums = refs[2 * count + 5 :]
    tokens, width = slots_in[0].shape[2], rows_in[0].shape[1]
    slots = rows_out.shape[1] // count
    experts = word_sums.shape[1]
    q = pl.program_id(0)
    slot_ids = lax.broadcasted_iota(jnp.int32, (slots, tokens), 0).astype(full)
    parts = [slice(r * slots, (r + 1) * slots) for r in range(count)]
    here = pl.ds(pl.multiple_of(q * slots, slots), slots)
    places, gate_cols, grad_parts = [], [], []
    for r in range(count):
        place = slots_in[r][0] == slot_ids
        hot = place.astype(low)
        hot_all[r, here] = hot
        places.append(place)
        gate_cols.append(jnp.sum(jnp.where(place, gates_in[r][0], 0.0), axis=1, keepdims=True))
        rows_out[0, parts[r]] = dot_nn(hot, rows_in[r][:tokens]).astype(low)
        grad_parts.append(dot_nn(hot, grads_in[r][:tokens]))
    gate_col = jnp.concatenate(gate_cols, axis=0)
    grad_rows = jnp.concatenate(grad_parts, axis=0)
    rows = rows_out[0]
    gated = (grad_rows * gate_col).astype(low)
    gated_out[0] = gated
    gate_rows = dot_nn(rows, gate_weight[0])
    up_rows = dot_nn(rows, up_weight[0])
    logistic = jax.nn.sigmoid(gate_rows)
    silu_rows = gate_rows * logistic
    slope_rows = logistic * (1.0 + gate_rows * (1.0 - logistic))
    inner = (silu_rows * up_rows).astype(low)
    inner_out[0] = inner
    grad_inner = dot_nt(gated, down_weight[0])
    grad_gate_rows = (grad_inner * up_rows * slope_rows).astype(low)
    grad_up_rows = (grad_inner * silu_rows).astype(low)
    grad_gate_out[0] = grad_gate_rows
    grad_up_out[0] = grad_up_rows
    sent_grads = (
        dot_nt(grad_gate_rows, gate_weight[0]) + dot_nt(grad_up_rows, up_weight[0])
    ).astype(low)
    result_rows = dot_nn(inner, down_weight[0])
    gate_grad = jnp.sum(result_rows * grad_rows, axis=1, keepdims=True)
    sent_results = (result_rows * gate_col).astype(low)
    expert_ids = lax.broadcasted_iota(jnp.int32, (experts, width), 0)

    @pl.when(q == 0)
    def _():
        word_sums[...] = jnp.zeros_like(word_sums)

    for r in range(count):
        grad_all[r, here] = sent_grads[parts[r]]
        result_all[r, here] = sent_results[parts[r]]
        token_grad = jnp.sum(
            jnp.where(places[r], gate_grad[parts[r]], 0.0), axis=0, keepdims=True
        )
        words = jnp.concatenate(
            [word.astype(full) for word in split_words(token_grad)]
            + [jnp.zeros((1, width - 3 * tokens), full)],
            axis=1,
        )
        word_sums[r] += jnp.where(expert_ids == numbers[q], words, 0.0)

    @pl.when(q == PLANE - 1)
    def _():
        for r in range(count):
            grad_total[r][:tokens] = dot_tn(hot_all[r], grad_all[r]).astype(low)
            grad_total[r][tokens:] = word_sums[r].astype(low)
            result_total[r][...] = dot_tn(hot_all[r], result_all[r]).astype(low)


def run_experts(numbers, rows, grads, slot_rows, gate_rows, weights, slots):
    count = len(rows)
    extended, width = rows[0].shape
    tokens = slot_rows[0].shape[2]
    low = jnp.bfloat16
    hidden_width = weights[0].shape[2]
    whole = lambda *shape: pl.BlockSpec(shape, lambda q, numbers: (0,) * len(shape))
    each = lambda *shape: pl.BlockSpec((1,) + shape, lambda q, numbers: (q, 0, 0))
    sizes = (width, hidden_width, width, hidden_width, hidden_width)
    out = pl.pallas_call(
        functools.partial(expert_kernel, count),
        grid_spec=pltpu.PrefetchScalarGridSpec(
            num_scalar_prefetch=1,
            grid=(PLANE,),
            in_specs=[whole(extended, width)] * (2 * count)
            + [each(1, tokens)] * (2 * count)
            + [each(*array.shape[1:]) for array in weights],
            out_specs=[whole(extended, width)] * count
            + [whole(tokens, width)] * count
            + [each(count * slots, size) for size in sizes],
            scratch_shapes=[
                pltpu.VMEM((count, PLANE * slots, tokens), low),
                pltpu.VMEM((count, PLANE * slots, width), low),
                pltpu.VMEM((count, PLANE * slots, width), low),
                pltpu.VMEM((count, extended - tokens, width), jnp.float32),
            ],
        ),
        out_shape=[jax.ShapeDtypeStruct((extended, width), low)] * count
        + [jax.ShapeDtypeStruct((tokens, width), low)] * count
        + [jax.ShapeDtypeStruct((PLANE, count * slots, size), low) for size in sizes],
        compiler_params=pltpu.CompilerParams(vmem_limit_bytes=62 * 1024 * 1024),
        cost_estimate=pl.CostEstimate(
            flops=count * PLANE * slots * width * (10 * hidden_width + 8 * tokens),
            bytes_accessed=6 * PLANE * width * hidden_width,
            transcendentals=0,
        ),
    )(numbers, *rows, *grads, *slot_rows, *gate_rows, *weights)
    return out[:count], out[count : 2 * count], out[2 * count :]


FIRST_ORDERS = (0, 1, 2, 0, 1, 2)


def gather_plan(units, orders):
    least, more = divmod(units, len(orders))
    count = len(orders)
    return tuple((order, 128 * (least + (i >= count - more))) for i, order in enumerate(orders))


def split_words(values):
    words = []
    for _ in range(3):
        words.append(values.astype(jnp.bfloat16))
        values = values - words[-1].astype(jnp.float32)
    return words


def after(value, other):
    return lax.optimization_barrier((value, other))[0]


def add_low(a, b):
    return (a.astype(jnp.float32) + b.astype(jnp.float32)).astype(jnp.bfloat16)


class Grid:
    def __init__(self, experts):
        self.experts = experts
        self.line = experts // PLANE
        here = lax.axis_index("expert")
        self.core = lax.axis_index("dp")
        self.at_line = here // PLANE
        self.at_plane = here % PLANE

    def shift(self, block, amount):
        pairs = [
            (i, ((i // PLANE + amount) % self.line) * PLANE + i % PLANE)
            for i in range(self.experts)
        ]
        return lax.ppermute(block, "expert", pairs)

    def swap(self, block, flip):
        pairs = [(i, (i // PLANE) * PLANE + ((i % PLANE) ^ flip)) for i in range(self.experts)]
        return lax.ppermute(block, "expert", pairs)

    def line_gather(self, block, rising=None, falling=None):
        half, rest = self.line // 2, (self.line - 1) // 2
        rising = self.shift(block, 1) if rising is None else rising
        found = [block, rising] + [None] * (self.line - 2)
        for i in range(2, half + 1):
            found[i] = self.shift(found[i - 1], 1)
        if rest:
            found[-1] = self.shift(block, -1) if falling is None else falling
            for i in range(2, rest + 1):
                found[-i] = self.shift(found[1 - i], -1)
        return found


def local(
    tokens_in,
    lengths,
    key_keep,
    routes,
    cotangent,
    attention_in,
    attention_in_momentum,
    attention_in_average,
    attention_out,
    attention_out_momentum,
    attention_out_average,
    shared_in,
    shared_in_momentum,
    shared_in_average,
    shared_down,
    shared_down_momentum,
    shared_down_average,
    router,
    router_momentum,
    router_average,
    norm_gains,
    norm_gains_momentum,
    norm_gains_average,
    expert_in,
    expert_in_momentum,
    expert_in_average,
    expert_down,
    expert_down_momentum,
    expert_down_average,
):
    low = jnp.bfloat16
    full = jnp.float32
    tokens = tokens_in.shape[0]
    model_width = tokens_in.shape[1]
    top_count = routes.shape[1]
    block_rows = router.shape[0]
    experts = router.shape[1]
    hidden_width = shared_in.shape[2]
    grid = Grid(experts)
    capacity = 9 * tokens * top_count // (8 * experts)
    slots = -(-capacity // 16) * 16
    extra_width = -(-(experts + 2) // 128) * 128

    pack_one = jnp.concatenate(
        [attention_in[m].astype(low).T for m in range(3)]
        + [
            router.astype(low),
            norm_gains.astype(low).T,
            jnp.zeros((block_rows, extra_width - experts - 2), low),
        ],
        axis=1,
    )
    pack_out = attention_out.astype(low).T
    pack_shared = jnp.concatenate(
        [shared_in[0].astype(low), shared_in[1].astype(low), shared_down.astype(low).T], axis=1
    )
    position = jnp.arange(tokens, dtype=jnp.int32)
    usable = position < lengths[0]
    named = jnp.any(
        routes.T[None, :, :] == jnp.arange(experts, dtype=jnp.int32)[:, None, None], axis=1
    )
    member = named & usable[None, :]
    earlier = (position[:, None] < position[None, :]).astype(low)
    counted = dot_nn(member.astype(low), earlier)
    slot_of = jnp.where(member, counted, -1.0)
    wanted = grid.at_line * PLANE + (grid.at_plane ^ jnp.arange(PLANE, dtype=jnp.int32))
    choose = (wanted[:, None] == jnp.arange(experts, dtype=jnp.int32)[None, :]).astype(low)

    def widen(rows):
        return jnp.pad(rows, ((0, 0), (0, model_width - rows.shape[1])))

    pair, down = expert_in[0].astype(low), expert_down[0].astype(low)
    plans = (
        gather_plan(pack_one.shape[1] // 128, FIRST_ORDERS),
        gather_plan(model_width // 128, FIRST_ORDERS),
    )
    (all_one, turned_out), down_x, down_y = first_exchange(
        experts, [pack_one, pack_out], plans, down
    )
    line_grads, sent = after(
        (jnp.concatenate([cotangent, widen(slot_of.astype(low))], axis=0), pair), turned_out
    )
    line_grads = grid.line_gather(line_grads)
    pairs = [pair, grid.swap(sent, 1), grid.swap(sent, 2)]
    downs = [down, down_x, down_y]
    all_one = all_one.reshape(model_width, -1)
    turned_out = turned_out.reshape(model_width, model_width)
    extra = all_one[:, 3 * model_width :]
    router_low = extra[:, :experts]
    gains = extra[:, experts : experts + 2].astype(full).T
    gain_one, gain_two = gains[0], gains[1]
    inputs = tokens_in.astype(full)
    rstd_one = lax.rsqrt(jnp.mean(inputs * inputs, axis=-1, keepdims=True) + eps_norm)
    normed_one = (inputs * rstd_one * gain_one).astype(low)
    cosine, sine_table = rope_tables(tokens, HD)
    bias = jnp.where(allowed_keys(lengths[0], key_keep), 0.0, mask_fill)
    query, key_rot, value, attended, hidden, normed_two = attend(
        normed_one, all_one, turned_out, bias, cosine, sine_table, tokens_in, gain_two[None]
    )
    rstd_two = lax.rsqrt(jnp.mean(hidden * hidden, axis=-1, keepdims=True) + eps_norm)

    logits = lax.dot_general(
        router_low, normed_two, (((0,), (1,)), ((), ())), preferred_element_type=full
    )
    logits = jnp.where(named, logits, mask_fill)
    logit_exps = jnp.exp(logits - jnp.max(logits, axis=0, keepdims=True))
    gating = logit_exps / jnp.sum(logit_exps, axis=0, keepdims=True)
    gating_live = jnp.where(member, gating, 0.0)
    gate_words = jnp.concatenate(split_words(gating_live), axis=1)
    line_rows = jnp.concatenate([normed_two, widen(gate_words)], axis=0)
    line_rows = after(line_rows, [line_grads[1], line_grads[-1]])
    rising, falling, *weights = second_exchange(experts, line_rows, pairs, downs)
    line_rows = grid.line_gather(line_rows, rising, falling)
    weights = [part.reshape(PLANE, -1, part.shape[-1]) for part in weights]

    kept, grad_parts, result_parts = [], [], []
    last = weights
    for start in range(0, grid.line, 2):
        group = range(start, start + 2)
        line_part = [line_rows[r] for r in group], [line_grads[r] for r in group]
        rows, grads = after(line_part, last)
        slot_rows, gate_rows = [], []
        for part in rows:
            words = dot_nn(choose, part[tokens:, : 3 * tokens])
            gate_row = words[:, :tokens] + words[:, tokens : 2 * tokens] + words[:, 2 * tokens :]
            gate_rows.append(gate_row[:, None])
        for part in grads:
            slot_rows.append(dot_nn(choose, part[tokens:, :tokens])[:, None])
        grad_part, result_part, parts = run_experts(
            wanted, rows, grads, slot_rows, gate_rows, weights, slots
        )
        kept.append(parts)
        last = grad_part
        grad_parts += [grid.shift(part, -r) if r else part for r, part in zip(group, grad_part)]
        result_parts += result_part
    routed_grad = sum(part.astype(full) for part in grad_parts)
    result_parts = after(result_parts, routed_grad)
    routed_result = sum(
        (grid.shift(part, -r) if r else part).astype(full) for r, part in enumerate(result_parts)
    )
    owns, crossed, nears = third_exchange(experts, after(kept, last))
    arrived = [grid.swap(part, flip) for part, flip in zip(nears, (1, 2))]
    gate_grads = routed_grad[tokens:]
    routed_grad = routed_grad[:tokens]
    grad_gating = (
        gate_grads[:, :tokens]
        + gate_grads[:, tokens : 2 * tokens]
        + gate_grads[:, 2 * tokens : 3 * tokens]
    )
    grad_chosen = gating * (grad_gating - jnp.sum(gating * grad_gating, axis=0, keepdims=True))
    grad_logits = grad_chosen.astype(low)
    grad_router = lax.dot_general(
        normed_two, grad_logits, (((0,), (1,)), ((), ())), preferred_element_type=full
    )

    all_shared = lax.all_gather(
        after(pack_shared, weights), ("dp", "expert"), axis=0, tiled=True
    )
    shared_pair = [all_shared[:, m * hidden_width : (m + 1) * hidden_width] for m in range(2)]
    turned_down = all_shared[:, 2 * hidden_width :]
    grad_out = cotangent.astype(full)
    shared_gate = dot_nn(normed_two, shared_pair[0])
    shared_up = dot_nn(normed_two, shared_pair[1])
    shared_silu, shared_slope = silu_parts(shared_gate)
    shared_hidden = (shared_silu * shared_up).astype(low)
    shared_result = dot_nt(shared_hidden, turned_down)
    grad_shared_hidden = dot_nn(cotangent, turned_down)
    grad_shared_gate = (grad_shared_hidden * shared_up * shared_slope).astype(low)
    grad_shared_up = (grad_shared_hidden * shared_silu).astype(low)
    grad_normed_two = dot_nt(grad_shared_gate, shared_pair[0]) + dot_nt(
        grad_shared_up, shared_pair[1]
    )
    grad_normed_two = grad_normed_two + lax.dot_general(
        grad_logits, router_low, (((0,), (1,)), ((), ())), preferred_element_type=full
    )

    grad_normed_two = grad_normed_two + routed_grad
    scaled_two = grad_normed_two * gain_two
    grad_gain_two = jnp.sum(grad_normed_two * hidden * rstd_two, axis=0)
    grad_hidden = (
        grad_out
        + rstd_two * scaled_two
        - hidden * rstd_two**3 * jnp.mean(scaled_two * hidden, axis=-1, keepdims=True)
    )
    grad_branch = grad_hidden.astype(low)
    grads_shared = [
        dot_tn(normed_two, grad_shared_gate).astype(low),
        dot_tn(normed_two, grad_shared_up).astype(low),
        dot_tn(cotangent, shared_hidden).astype(low),
    ]
    *grads_attention, grad_normed_one = attend_back(
        grad_branch,
        normed_one,
        query,
        key_rot,
        value,
        attended,
        all_one,
        turned_out,
        bias,
        cosine,
        sine_table,
    )
    scaled_one = grad_normed_one * gain_one
    grad_gain_one = jnp.sum(grad_normed_one * inputs * rstd_one, axis=0)
    input_grad = (
        grad_hidden
        + rstd_one * scaled_one
        - inputs * rstd_one**3 * jnp.mean(scaled_one * inputs, axis=-1, keepdims=True)
    )
    grad_extra = jnp.concatenate(
        [
            grad_router.astype(low),
            jnp.stack([grad_gain_one, grad_gain_two], axis=1).astype(low),
            jnp.zeros((model_width, extra_width - experts - 2), low),
        ],
        axis=1,
    )
    *sums, total_in, total_down = sum_all(
        experts,
        grads_attention + grads_shared + [grad_extra],
        sum_plans(model_width, hidden_width, extra_width),
        owns,
        crossed,
        arrived,
    )
    output = (hidden + shared_result + routed_result).astype(low)

    sums = [part.astype(full) for part in sums]
    summed_in = jnp.stack([part.T for part in sums[:3]], axis=0)
    summed_out = sums[3].T
    summed_shared_in = jnp.stack(sums[4:6], axis=0)
    summed_shared_down = sums[6].T
    summed_router = sums[7][:, :experts]
    summed_gains = sums[7][:, experts : experts + 2].T
    upd_attn_in = advance(
        attention_in, attention_in_momentum, attention_in_average, summed_in, rate_attention_in
    )
    upd_attn_out = advance(
        attention_out, attention_out_momentum, attention_out_average, summed_out, rate_attention_out
    )
    upd_shared_in = advance(
        shared_in, shared_in_momentum, shared_in_average, summed_shared_in, rate_shared_in
    )
    upd_shared_down = advance(
        shared_down, shared_down_momentum, shared_down_average, summed_shared_down, rate_shared_down
    )
    upd_router = advance(router, router_momentum, router_average, summed_router, rate_router)
    upd_gains = advance(
        norm_gains, norm_gains_momentum, norm_gains_average, summed_gains, rate_gains
    )
    upd_expert_in = advance(
        expert_in,
        expert_in_momentum,
        expert_in_average,
        total_in.astype(full)[None],
        rate_expert_in,
    )
    upd_expert_down = advance(
        expert_down,
        expert_down_momentum,
        expert_down_average,
        total_down.astype(full)[None],
        rate_expert_down,
    )
    return (
        output,
        input_grad,
        upd_attn_in[0],
        upd_attn_in[1],
        upd_attn_in[2],
        upd_attn_out[0],
        upd_attn_out[1],
        upd_attn_out[2],
        upd_shared_in[0],
        upd_shared_in[1],
        upd_shared_in[2],
        upd_shared_down[0],
        upd_shared_down[1],
        upd_shared_down[2],
        upd_router[0],
        upd_router[1],
        upd_router[2],
        upd_gains[0],
        upd_gains[1],
        upd_gains[2],
        upd_expert_in[0],
        upd_expert_in[1],
        upd_expert_in[2],
        upd_expert_down[0],
        upd_expert_down[1],
        upd_expert_down[2],
    )


def solution(mesh):
    in_specs = (
        P(("dp", "expert"), None),
        P(("dp", "expert")),
        P(("dp", "expert")),
        P(("dp", "expert"), None),
        P(("dp", "expert"), None),
        P(None, None, ("dp", "expert")),
        P(None, None, ("dp", "expert")),
        P(None, None, ("dp", "expert")),
        P(None, ("dp", "expert")),
        P(None, ("dp", "expert")),
        P(None, ("dp", "expert")),
        P(None, ("dp", "expert"), None),
        P(None, ("dp", "expert"), None),
        P(None, ("dp", "expert"), None),
        P(None, ("dp", "expert")),
        P(None, ("dp", "expert")),
        P(None, ("dp", "expert")),
        P(("dp", "expert"), None),
        P(("dp", "expert"), None),
        P(("dp", "expert"), None),
        P(None, ("dp", "expert")),
        P(None, ("dp", "expert")),
        P(None, ("dp", "expert")),
        P("expert", None, "dp", None),
        P("expert", None, "dp", None),
        P("expert", None, "dp", None),
        P("expert", "dp", None),
        P("expert", "dp", None),
        P("expert", "dp", None),
    )
    out_specs = (
        P(("dp", "expert"), None),
        P(("dp", "expert"), None),
        P(None, None, ("dp", "expert")),
        P(None, None, ("dp", "expert")),
        P(None, None, ("dp", "expert")),
        P(None, ("dp", "expert")),
        P(None, ("dp", "expert")),
        P(None, ("dp", "expert")),
        P(None, ("dp", "expert"), None),
        P(None, ("dp", "expert"), None),
        P(None, ("dp", "expert"), None),
        P(None, ("dp", "expert")),
        P(None, ("dp", "expert")),
        P(None, ("dp", "expert")),
        P(("dp", "expert"), None),
        P(("dp", "expert"), None),
        P(("dp", "expert"), None),
        P(None, ("dp", "expert")),
        P(None, ("dp", "expert")),
        P(None, ("dp", "expert")),
        P("expert", None, "dp", None),
        P("expert", None, "dp", None),
        P("expert", None, "dp", None),
        P("expert", "dp", None),
        P("expert", "dp", None),
        P("expert", "dp", None),
    )
    return jax.shard_map(local, mesh=mesh, in_specs=in_specs, out_specs=out_specs, check_vma=False)
```

```python
import functools

import jax
import jax.numpy as jnp
from jax import lax
from jax.experimental import pallas as pl
from jax.experimental.pallas import tpu as pltpu
from jax.sharding import PartitionSpec as P

HD = 128
STEP = 4


eps_norm = 1e-06
theta_base = 10000.0
momentum_decay = 0.9
mask_fill = -1e30
rate_attention_in = 2e-05
rate_attention_out = 0.002
rate_shared_in = 3e-05
rate_shared_down = 0.0002
rate_router = 1.5e-05
rate_gains = 0.0002
rate_expert_in = 0.0004
rate_expert_down = 0.008


def rope_tables(length, head_width):
    half_width = head_width // 2
    frequency = theta_base ** (-(jnp.arange(half_width, dtype=jnp.float32) * 2.0 / head_width))
    angles = jnp.arange(length, dtype=jnp.float32)[:, None] * frequency[None, :]
    cosine, sine_table = jnp.cos(angles), jnp.sin(angles)
    return (
        jnp.concatenate([cosine, cosine], axis=1),
        jnp.concatenate([-sine_table, sine_table], axis=1),
    )


def allowed_keys(length, keep_flags):
    amount = keep_flags.shape[0]
    position = jnp.arange(amount)
    causal = position[None, :] <= position[:, None]
    usable = (position < length) & (keep_flags == 1)
    return causal & (usable[None, :] | (position[None, :] == position[:, None]))


def silu_parts(values):
    logistic = jax.nn.sigmoid(values)
    return (values * logistic, logistic * (1.0 + values * (1.0 - logistic)))


def advance(weight, moment, average, gradient, step_rate):
    moment_new = momentum_decay * moment + gradient
    weight_new = weight - step_rate * (gradient + momentum_decay * moment_new)
    average_new = average + (weight_new - average) / (STEP + 1)
    return (weight_new, moment_new, average_new)


def dot_nn(a, b):
    return lax.dot_general(a, b, (((1,), (0,)), ((), ())), preferred_element_type=jnp.float32)


def dot_nt(a, b):
    return lax.dot_general(a, b, (((1,), (1,)), ((), ())), preferred_element_type=jnp.float32)


def dot_tn(a, b):
    return lax.dot_general(a, b, (((0,), (0,)), ((), ())), preferred_element_type=jnp.float32)


PLANE = 4
MESH = pl.DeviceIdType.MESH


class Spot:
    def __init__(self, line):
        here = lax.axis_index("expert")
        self.line = line
        self.core = lax.axis_index("dp")
        self.at = lax.div(here, PLANE)
        rest = lax.rem(here, PLANE)
        self.y, self.x = lax.div(rest, 2), lax.rem(rest, 2)

    def chip(self, at, y, x):
        return (self.core, at * PLANE + y * 2 + x)

    def around(self, amount):
        return lax.rem(self.at + amount + self.line, self.line)

    def partner(self, way):
        if way == "core":
            return (1 - self.core, self.at * PLANE + self.y * 2 + self.x)
        if way == "x":
            return self.chip(self.at, self.y, 1 - self.x)
        if way == "y":
            return self.chip(self.at, 1 - self.y, self.x)
        return self.chip(self.around(1 if way == "up" else -1), self.y, self.x)


def meet(spot):
    barrier = pltpu.get_barrier_semaphore()
    for way in ("core", "x", "y", "up", "down"):
        pl.semaphore_signal(barrier, inc=1, device_id=spot.partner(way), device_id_type=MESH)
    pl.semaphore_wait(barrier, 5)


class Moves:
    def __init__(self, spot, send_sems, recv_sems, local_sems):
        self.spot, self.send_sems, self.recv_sems = spot, send_sems, recv_sems
        self.local_sems = local_sems
        self.made, self.kept, self.loose = 0, 0, []

    def start(self, source, target, way, later=False):
        copy = pltpu.make_async_remote_copy(
            src_ref=source,
            dst_ref=target,
            send_sem=self.send_sems.at[self.made],
            recv_sem=self.recv_sems.at[self.made],
            device_id=self.spot.partner(way),
            device_id_type=MESH,
        )
        self.made += 1
        copy.start()
        if later:
            self.loose.append(copy)
        return copy

    def keep(self, source, target, later=False):
        copy = pltpu.make_async_copy(source, target, self.local_sems.at[self.kept])
        self.kept += 1
        copy.start()
        if later:
            self.loose.append(copy)
        return copy

    def finish(self):
        for copy in self.loose:
            copy.wait()


def in_steps(chains):
    while chains:
        left = []
        for chain in chains:
            try:
                next(chain)
                left.append(chain)
            except StopIteration:
                pass
        chains = left
        yield


def in_turn(chains):
    for _ in in_steps(chains):
        pass


def place_chain(moves, source, buffer, target):
    copy = moves.keep(source, buffer)
    yield
    copy.wait()
    moves.keep(buffer, target, later=True)


def core_chain(moves, own, whole, buffer):
    core = moves.spot.core
    moves.start(own, whole.at[core], "core", later=True)
    return place_chain(moves, own, buffer, whole.at[core])


def dense_chain(moves, whole, columns, order):
    spot = moves.spot
    half, rest = spot.line // 2, (spot.line - 1) // 2
    everything = slice(None)
    held = {"z": spot.at, "y": spot.y, "x": spot.x}

    def region(**other):
        at = dict(held, **other)
        return whole.at[spot.core, at["z"], at["y"], at["x"], everything, columns]

    def forward(part):
        moves.start(part, part, "core", later=True)

    for stage, dim in enumerate(order):
        if dim == "z":
            up = down = None
            for i in range(1, half + 1):
                part = region(z=spot.around(1 - i))
                up = moves.start(part, part, "up")
                if i <= rest:
                    part = region(z=spot.around(i - 1))
                    down = moves.start(part, part, "down")
                if stage == 0 and i == 1:
                    forward(region())
                yield
                up.wait()
                forward(region(z=spot.around(-i)))
                if i <= rest:
                    down.wait()
                    forward(region(z=spot.around(i)))
        else:
            part = region()
            copy = moves.start(part, part, dim)
            if stage == 0:
                forward(region())
            yield
            copy.wait()
            forward(region(**{dim: 1 - held[dim]}))
        held[dim] = everything


ORDERS = ("xyz", "yzx", "zxy", "zyx")


def first_kernel(line, plans, *refs):
    count = len(plans)
    shards, down, refs = refs[:count], refs[count], refs[count + 1 :]
    results, over_x, over_y, refs = refs[:count], refs[count], refs[count + 1], refs[count + 2 :]
    wholes, refs = refs[:count], refs[count:]
    spot = Spot(line)
    meet(spot)
    moves = Moves(spot, *refs)
    loads = [
        moves.keep(shards[n], wholes[n].at[spot.core, spot.at, spot.y, spot.x])
        for n in range(count)
    ]
    for copy in loads:
        copy.wait()
    chains = []
    for n, plan in enumerate(plans):
        start = 0
        for order, width in plan:
            columns = slice(start, start + width)
            chains.append(dense_chain(moves, wholes[n], columns, ORDERS[order]))
            start += width
    stages = 0
    for _ in in_steps(chains):
        stages += 1
        if stages == 1:
            moves.start(down, over_x, "x", later=True)
            moves.start(down, over_y, "y", later=True)
    moves.finish()
    stores = [moves.keep(wholes[n], results[n]) for n in range(count)]
    for copy in stores:
        copy.wait()


def hbm(count):
    return [pl.BlockSpec(memory_space=pl.ANY)] * count


def semaphores(remote, local):
    return [
        pltpu.SemaphoreType.DMA((remote,)),
        pltpu.SemaphoreType.DMA((remote,)),
        pltpu.SemaphoreType.DMA((local,)),
    ]


def both_halves(array):
    return jax.ShapeDtypeStruct((2,) + array.shape, array.dtype)


def first_exchange(experts, shards, plans, down):
    line = experts // PLANE
    count = len(shards)
    remote = sum(len(plan) for plan in plans) * (2 * line + 3) + 2
    out = pl.pallas_call(
        functools.partial(first_kernel, line, plans),
        out_shape=[
            jax.ShapeDtypeStruct((2, line, 2, 2) + shard.shape, shard.dtype) for shard in shards
        ]
        + [jax.ShapeDtypeStruct(down.shape, down.dtype)] * 2,
        in_specs=hbm(count + 1),
        out_specs=hbm(count + 2),
        scratch_shapes=[
            pltpu.VMEM((2, line, 2, 2) + shard.shape, shard.dtype) for shard in shards
        ]
        + semaphores(remote, 2 * count),
        compiler_params=pltpu.CompilerParams(
            collective_id=1, has_side_effects=True, vmem_limit_bytes=60 * 1024 * 1024
        ),
    )(*shards, down)
    return out[:count], out[count], out[count + 1]


def second_kernel(line, *refs):
    rows, pairs, downs, refs = refs[0], refs[1:4], refs[4:7], refs[7:]
    rising, falling, wholes, refs = refs[0], refs[1], refs[2:5], refs[5:]
    buffers, refs = refs[:9], refs[9:]
    spot = Spot(line)
    meet(spot)
    moves = Moves(spot, *refs)
    core = spot.core
    gate, up, down = wholes
    (_, pair_x, pair_y), (_, down_x, down_y) = pairs, downs
    half = down_x.shape[0] // 2

    def far_chain(source, target, way):
        copy = moves.start(source, target, way)
        yield
        copy.wait()
        moves.start(target, target, "core", later=True)

    moves.start(rows, rising, "up", later=True)
    moves.start(rows, falling, "down", later=True)
    upper, lower = pl.ds(0, half), pl.ds(half, half)
    in_turn(
        [
            far_chain(pair_y.at[1], up.at[3, core], "x"),
            far_chain(pair_x.at[0], gate.at[3, core], "y"),
            far_chain(down_y.at[lower], down.at[3, core, lower], "x"),
            far_chain(down_x.at[upper], down.at[3, core, upper], "y"),
        ]
        + [
            core_chain(moves, half_of, wholes[i].at[q], buffers[3 * q + i])
            for q in range(3)
            for i, half_of in enumerate((pairs[q].at[0], pairs[q].at[1], downs[q]))
        ]
    )
    moves.finish()


def second_exchange(experts, rows, pairs, downs):
    line = experts // PLANE
    low = rows.dtype
    shapes = [pairs[0].shape[1:]] * 2 + [downs[0].shape]
    return pl.pallas_call(
        functools.partial(second_kernel, line),
        out_shape=[jax.ShapeDtypeStruct(rows.shape, low)] * 2
        + [jax.ShapeDtypeStruct((PLANE, 2) + shape, low) for shape in shapes],
        in_specs=hbm(7),
        out_specs=hbm(5),
        scratch_shapes=[pltpu.VMEM(shape, low) for shape in shapes * 3] + semaphores(19, 18),
        compiler_params=pltpu.CompilerParams(
            collective_id=3, has_side_effects=True, vmem_limit_bytes=60 * 1024 * 1024
        ),
    )(rows, *pairs, *downs)


def packed(half, hidden_width, down_half, width):
    edge, more = down_half // 2, width - hidden_width
    below = 2 * half + down_half
    full = slice(0, hidden_width)
    rest = slice(hidden_width, width)
    places = [
        (0, slice(0, half), full, slice(0, half), full),
        (1, slice(half, 2 * half), full, slice(0, half), full),
        (2, slice(2 * half, 2 * half + edge), full, slice(0, edge), full),
        (2, slice(2 * half + edge, below), full, slice(edge, down_half), full),
        (2, slice(below, below + edge), slice(0, more), slice(0, edge), rest),
        (2, slice(below, below + edge), slice(more, 2 * more), slice(edge, down_half), rest),
    ]
    return places, below + edge, 2 * more


def third_kernel(line, groups, *refs):
    low, full = jnp.bfloat16, jnp.float32
    kept = [refs[5 * r : 5 * r + 5] for r in range(groups)]
    refs = refs[5 * groups :]
    owns, crossed, nears, refs = refs[:3], refs[3:6], refs[6:8], refs[8:]
    loaded, refs = [refs[:5], refs[5:10]], refs[10:]
    results, refs = [refs[:6], refs[6:12]], refs[12:]
    far_box, far_in, near_box, down_grad, refs = refs[:3], refs[3:7], refs[7:9], refs[9], refs[10:]
    spot = Spot(line)
    meet(spot)
    moves = Moves(spot, *refs)
    order = (3, 1, 2, 0)
    slots = kept[0][0].shape[1]
    loads = {}
    rows_half, hidden_width = results[0][0].shape
    down_half, width = results[0][2].shape
    edge = down_half // 2
    places, _, used = packed(rows_half, hidden_width, down_half, width)

    def load(n):
        loads[n] = [
            moves.keep(kept[r][i].at[order[n]], loaded[n % 2][i].at[pl.ds(r * slots, slots)])
            for r in range(groups)
            for i in range(5)
        ]

    def add(target, source):
        target[...] = (target[...].astype(full) + source[...].astype(full)).astype(low)

    load(0)
    for box in near_box:
        spare = (slice(2 * rows_half + down_half, box.shape[0]), slice(used, hidden_width))
        box[spare] = jnp.zeros((edge, hidden_width - used), low)
    sent = {}

    def weights(n):
        if n + 1 < PLANE:
            load(n + 1)
        for copy in loads[n]:
            copy.wait()
        rows, inner, gated, grad_gate, grad_up = loaded[n % 2]
        buffers = results[n % 2]
        down_grad[...] = dot_tn(inner[...], gated[...]).astype(low)
        q = order[n]
        for which in (1, 0):
            place = jnp.bitwise_xor(spot.core, which)
            gate_out, up_out, down_out = buffers[3 * which : 3 * which + 3]
            part = rows[:, pl.ds(pl.multiple_of(place * rows_half, 128), rows_half)]
            gate_out[...] = dot_tn(part, grad_gate[...]).astype(low)
            up_out[...] = dot_tn(part, grad_up[...]).astype(low)
            down_out[...] = down_grad[pl.ds(pl.multiple_of(place * down_half, 16), down_half), :]
            if which and q in (0, 3):
                targets = crossed if q == 0 else far_box
                sent[n] = [moves.start(buffers[3 + i], targets[i], "core") for i in range(3)]
            elif which:
                sent[n] = [
                    moves.start(
                        buffers[3 + i].at[rows_at, columns_at],
                        near_box[q - 1].at[to_rows, to_columns],
                        "core",
                    )
                    for i, to_rows, to_columns, rows_at, columns_at in places
                ]
            elif q == 0:
                sent[n] += [moves.keep(buffers[i], owns[i]) for i in range(3)]

    def far():
        for copy in sent[0]:
            copy.wait()
        mine = results[0][:3]
        for i in range(3):
            add(far_box[i], mine[i])
        upper, lower = pl.ds(0, edge), pl.ds(edge, edge)
        return [
            moves.start(far_box[0], far_in[0], "y"),
            moves.start(far_box[1], far_in[1], "x"),
            moves.start(far_box[2].at[upper], far_in[2], "y"),
            moves.start(far_box[2].at[lower], far_in[3], "x"),
        ]

    def near(n):
        for copy in sent[n]:
            copy.wait()
        box = near_box[order[n] - 1]
        for i, to_rows, to_columns, rows_at, columns_at in places:
            add(box.at[to_rows, to_columns], results[n % 2][i].at[rows_at, columns_at])

    weights(0)
    weights(1)
    across = far()
    weights(2)
    near(1)
    weights(3)
    near(2)
    for copy in across:
        copy.wait()
    rest, full_width = slice(hidden_width, width), slice(0, hidden_width)
    for box, i, source in ((near_box[0], 0, far_in[0]), (near_box[1], 1, far_in[1])):
        _, to_rows, to_columns, _, _ = places[i]
        add(box.at[to_rows, to_columns], source)
    for box, i, source in ((near_box[0], 0, far_in[2]), (near_box[1], 1, far_in[3])):
        for index, columns_at in ((2 + i, full_width), (4 + i, rest)):
            _, to_rows, to_columns, _, _ = places[index]
            add(box.at[to_rows, to_columns], source.at[:, columns_at])
    stores = [moves.keep(box, target) for box, target in zip(near_box, nears)]
    for copy in sent[3] + stores:
        copy.wait()


def third_exchange(experts, kept):
    line = experts // PLANE
    low = jnp.bfloat16
    rows, inner = kept[0][0], kept[0][1]
    slots, width, hidden_width = rows.shape[1], rows.shape[2], inner.shape[2]
    half, down_half = width // 2, hidden_width // 2
    pieces = [(half, hidden_width), (half, hidden_width), (down_half, width)]
    far = pieces[:2] + [(down_half // 2, width)] * 2
    package = (packed(half, hidden_width, down_half, width)[1], hidden_width)
    out = pl.pallas_call(
        functools.partial(third_kernel, line, len(kept)),
        out_shape=[jax.ShapeDtypeStruct(size, low) for size in pieces * 2 + [package] * 2],
        in_specs=hbm(5 * len(kept)),
        out_specs=hbm(8),
        scratch_shapes=[
            pltpu.VMEM((len(kept) * slots, array.shape[2]), low) for array in list(kept[0]) * 2
        ]
        + [pltpu.VMEM(size, low) for size in pieces * 4]
        + [pltpu.VMEM(size, low) for size in pieces + far + [package] * 2]
        + [pltpu.VMEM((hidden_width, width), low)]
        + semaphores(2 * 3 + 2 * 6 + 4, 5 * PLANE * len(kept) + 3 + 2),
        compiler_params=pltpu.CompilerParams(
            collective_id=4, has_side_effects=True, vmem_limit_bytes=62 * 1024 * 1024
        ),
    )(*[array for parts in kept for array in parts])
    return out[:3], out[3:6], out[6:]


def sum_plans(width, hidden_width, extra_width):
    edge, half = width * 6 // 10, width // 2
    out_edge = width * 7 // 10
    gate_edge, down_edge = hidden_width * 5 // 7, hidden_width * 4 // 7
    return (
        (((0, 0, edge),), ((1, 0, half),), ((0, edge, width - edge),)),
        (((2, 0, edge),), ((1, half, width - half),), ((2, edge, width - edge),)),
        (
            ((3, 0, out_edge),),
            ((4, 0, gate_edge),),
            ((3, out_edge, width - out_edge), (7, 0, extra_width)),
        ),
        (
            ((5, 0, hidden_width), (4, gate_edge, hidden_width - gate_edge)),
            ((6, 0, down_edge),),
            ((6, down_edge, hidden_width - down_edge),),
        ),
    )


def total_chain(moves, owns, crossed, arrived, totals, buffers):
    full = jnp.float32
    half, hidden_width = owns[0].shape
    down_half, width = owns[2].shape
    edge = down_half // 2
    places, _, _ = packed(half, hidden_width, down_half, width)
    jobs = []
    for i in range(2):
        for rows in range(0, half, half // 4):
            jobs.append((i, rows, half // 4))
    for rows in range(0, down_half, edge // 2):
        jobs.append((2, rows, edge // 2))
    loads, stores = {}, {}

    def box(n, i):
        wide = jobs[n][0] == 2
        return buffers[10 * (n % 2) + 5 * wide + i]

    def load(n):
        which, start, rows = jobs[n]
        at = pl.ds(start, rows)
        copies = [(owns[which].at[at], box(n, 0)), (crossed[which].at[at], box(n, 1))]
        for k, package in enumerate(arrived):
            for part, to_rows, to_columns, rows_at, columns_at in places:
                inside = rows_at.start <= start < rows_at.stop
                if part == which and inside:
                    copies.append(
                        (
                            package.at[
                                pl.ds(to_rows.start + start - rows_at.start, rows), to_columns
                            ],
                            box(n, 2 + k).at[:, columns_at],
                        )
                    )
        loads[n] = [moves.keep(source, target) for source, target in copies]

    load(0)
    for n, (which, start, rows) in enumerate(jobs):
        if n + 1 < len(jobs):
            load(n + 1)
        for copy in loads[n]:
            copy.wait()
        if n >= 2:
            for copy in stores[n - 2]:
                copy.wait()
        total = box(n, 4)
        total[...] = sum(box(n, i)[...].astype(full) for i in range(4)).astype(total.dtype)
        at = pl.ds(start, rows)
        target = totals[0].at[which, at] if which < 2 else totals[1].at[at]
        stores[n] = [moves.keep(total, target)]
        if n % 2:
            yield
    for n in (len(jobs) - 2, len(jobs) - 1):
        for copy in stores[n]:
            copy.wait()


def total_buffers(half, hidden_width, down_half, width, dtype):
    shapes = [(half // 4, hidden_width)] * 5 + [(down_half // 4, width)] * 5
    return [pltpu.VMEM(shape, dtype) for shape in shapes * 2]


def sum_kernel(line, plans, arrays, *refs):
    count = len(plans)
    grads, refs = refs[:arrays], refs[arrays:]
    owns, crossed, arrived, refs = refs[:3], refs[3:6], refs[6:8], refs[8:]
    sums, refs = refs[:arrays], refs[arrays:]
    totals, refs = refs[:2], refs[2:]
    buffers, refs = refs[:20], refs[20:]
    kept, refs = refs[: 3 * count], refs[3 * count :]
    core_in, refs = refs[: 3 * count], refs[3 * count :]
    first_in, refs = refs[: 3 * count], refs[3 * count :]
    second_in, refs = refs[: 3 * count], refs[3 * count :]
    third_in, refs = refs[: 3 * count], refs[3 * count :]
    spot = Spot(line)
    meet(spot)
    moves = Moves(spot, *refs)
    half, rest = line // 2, (line - 1) // 2
    everything = slice(None)
    orders = ("xyz", "yzx", "zxy")

    loads, swaps = [], []
    at = 0
    for n, plan in enumerate(plans):
        for o, pieces in enumerate(plan):
            mine, theirs = [], []
            start = 0
            for which, first, width in pieces:
                ref = grads[which]
                source = slice(first, first + width)
                target = slice(start, start + width)
                mine.append(
                    moves.keep(
                        ref.at[spot.core, :, :, :, :, source],
                        kept[3 * n + o].at[:, :, :, :, target],
                    )
                )
                theirs.append(
                    moves.start(
                        ref.at[1 - spot.core, :, :, :, :, source],
                        core_in[3 * n + o].at[:, :, :, :, target],
                        "core",
                    )
                )
                at += 1
                start += width
            loads.append(mine)
            swaps.append(theirs)

    def add(target, source):
        lead = target.shape[:-2]
        total = 1
        for extent in lead:
            total *= extent

        def one(i, carry):
            index = []
            for extent in reversed(lead):
                index.insert(0, lax.rem(i, extent))
                i = lax.div(i, extent)
            index = tuple(index)
            target[index] = (
                target[index].astype(jnp.float32) + source[index].astype(jnp.float32)
            ).astype(target.dtype)
            return carry

        lax.fori_loop(0, total, one, 0)

    def chain(n, o):
        buffer = kept[3 * n + o]
        mine, theirs = loads[3 * n + o], swaps[3 * n + o]
        for copy in mine:
            copy.wait()
        for copy in theirs:
            copy.wait()
        add(buffer, core_in[3 * n + o])
        inbox = [first_in[3 * n + o], second_in[3 * n + o], third_in[3 * n + o]]
        held = {"z": everything, "y": everything, "x": everything}

        def region(**other):
            at = dict(held, **other)
            return buffer.at[at["z"], at["y"], at["x"]]

        for stage, dim in enumerate(orders[o]):
            box = inbox[stage]
            if dim == "z":
                up = down = None
                for i in range(half, 0, -1):
                    down = moves.start(region(z=spot.around(-i)), box.at[i - 1], "down")
                    if i <= rest:
                        up = moves.start(region(z=spot.around(i)), box.at[half + i - 1], "up")
                    yield
                    down.wait()
                    add(region(z=spot.around(1 - i)), box.at[i - 1])
                    if i <= rest:
                        up.wait()
                        add(region(z=spot.around(i - 1)), box.at[half + i - 1])
                held[dim] = spot.at
            else:
                own = spot.y if dim == "y" else spot.x
                copy = moves.start(region(**{dim: 1 - own}), box, dim)
                yield
                copy.wait()
                held[dim] = own
                add(region(), box)
        results, start = [], 0
        for which, first, width in plans[n][o]:
            source = region().at[:, slice(start, start + width)]
            results.append(moves.keep(source, sums[which].at[:, slice(first, first + width)]))
            start += width
        yield
        for result in results:
            result.wait()

    chains = [chain(n, o) for n in range(count) for o in range(3)]
    chains.append(total_chain(moves, owns, crossed, arrived, totals, buffers))
    in_turn(chains)


def sum_all(experts, grads, plans, owns, crossed, arrived):
    line = experts // PLANE
    half, rest = line // 2, (line - 1) // 2
    rows = grads[0].shape[0] // (2 * experts)
    dtype = grads[0].dtype
    operands = [array.reshape(2, line, 2, 2, rows, array.shape[1]) for array in grads]
    shapes = [jax.ShapeDtypeStruct((rows, array.shape[1]), dtype) for array in grads]
    boxes = [[], [], [], [], []]
    for plan in plans:
        for o, pieces in enumerate(plan):
            steps = half + rest
            block = (rows, sum(width for _, _, width in pieces))
            boxes[0].append((line, 2, 2) + block)
            boxes[1].append((line, 2, 2) + block)
            if o == 0:
                inboxes = [(line, 2), (line,), (steps,)]
            elif o == 1:
                inboxes = [(line, 2), (steps, 2), ()]
            else:
                inboxes = [(steps, 2, 2), (2,), ()]
            for i, lead in enumerate(inboxes):
                boxes[2 + i].append(lead + block)
    count = len(plans)
    given = sum(len(pieces) for plan in plans for pieces in plan)
    number = given + 3 * count * (line + 1)
    others = list(owns) + list(crossed) + list(arrived)
    shapes += [
        jax.ShapeDtypeStruct((2,) + owns[0].shape, dtype),
        jax.ShapeDtypeStruct(owns[2].shape, dtype),
    ]
    return pl.pallas_call(
        functools.partial(sum_kernel, line, plans, len(grads)),
        out_shape=shapes,
        in_specs=hbm(len(operands) + len(others)),
        out_specs=hbm(len(grads) + 2),
        scratch_shapes=total_buffers(*owns[0].shape, *owns[2].shape, dtype)
        + [pltpu.VMEM(shape, dtype) for kind in boxes for shape in kind]
        + semaphores(number, 2 * given + 12 * 7),
        compiler_params=pltpu.CompilerParams(
            collective_id=2, has_side_effects=True, vmem_limit_bytes=60 * 1024 * 1024
        ),
    )(*operands, *others)


def turn(values, cosine, sine_table):
    return values * cosine + pltpu.roll(values, HD // 2, 1) * sine_table


def turn_back(values, cosine, sine_table):
    return values * cosine - pltpu.roll(values, HD // 2, 1) * sine_table


def probabilities(query, key, bias):
    scores = dot_nt(query, key) * HD ** (-0.5) + bias
    exps = jnp.exp(scores - jnp.max(scores, axis=1, keepdims=True))
    return exps / jnp.sum(exps, axis=1, keepdims=True)


def attend_kernel(
    steps,
    normed,
    query_weight,
    key_weight,
    value_weight,
    out_weight,
    bias,
    cosine,
    sine_table,
    inputs,
    gain,
    query_out,
    key_out,
    value_out,
    attended_out,
    hidden_out,
    normed_out,
):
    step = pl.program_id(0)
    low = jnp.bfloat16
    n1 = normed[...]
    cos, sin = cosine[...], sine_table[...]
    query = dot_nt(n1, query_weight[...])
    key = dot_nt(n1, key_weight[...])
    value_out[...] = dot_nt(n1, value_weight[...]).astype(low)
    for part in range(query.shape[1] // HD):
        columns = slice(part * HD, (part + 1) * HD)
        q = turn(query[:, columns], cos, sin).astype(low)
        k = turn(key[:, columns], cos, sin).astype(low)
        query_out[:, columns] = q
        key_out[:, columns] = k
        probs = probabilities(q, k, bias[...])
        attended_out[:, columns] = dot_nn(probs.astype(low), value_out[:, columns]).astype(low)
    branch = dot_nt(attended_out[...], out_weight[...])

    @pl.when(step == 0)
    def _():
        hidden_out[...] = inputs[...].astype(jnp.float32) + branch

    @pl.when(step > 0)
    def _():
        hidden_out[...] += branch

    @pl.when(step == steps - 1)
    def _():
        hidden = hidden_out[...]
        rstd = lax.rsqrt(jnp.mean(hidden * hidden, axis=1, keepdims=True) + eps_norm)
        normed_out[...] = (hidden * rstd * gain[...]).astype(low)


def attend(normed, weights, out_weight, bias, cosine, sine_table, inputs, gain):
    tokens, width = normed.shape
    group = 2 * HD
    steps = width // group
    low = jnp.bfloat16
    whole = lambda *shape: pl.BlockSpec(shape, lambda i: (0,) * len(shape))
    columns = pl.BlockSpec((tokens, group), lambda i: (0, i))
    return pl.pallas_call(
        functools.partial(attend_kernel, steps),
        grid=(steps,),
        in_specs=[whole(tokens, width)]
        + [pl.BlockSpec((group, width), lambda i, m=m: (i, m)) for m in range(3)]
        + [
            pl.BlockSpec((width, group), lambda i: (0, i)),
            whole(tokens, tokens),
            whole(tokens, HD),
            whole(tokens, HD),
            whole(tokens, width),
            whole(1, width),
        ],
        out_specs=[columns] * 4 + [whole(tokens, width)] * 2,
        out_shape=[jax.ShapeDtypeStruct((tokens, width), low)] * 4
        + [
            jax.ShapeDtypeStruct((tokens, width), jnp.float32),
            jax.ShapeDtypeStruct((tokens, width), low),
        ],
        compiler_params=pltpu.CompilerParams(vmem_limit_bytes=48 * 1024 * 1024),
        cost_estimate=pl.CostEstimate(
            flops=8 * tokens * width * width, bytes_accessed=20 * width * width, transcendentals=0
        ),
    )(normed, weights, weights, weights, out_weight, bias, cosine, sine_table, inputs, gain)


def attend_back_kernel(
    grad_branch,
    normed,
    query_in,
    key_in,
    value_in,
    attended_in,
    query_weight,
    key_weight,
    value_weight,
    out_weight,
    bias,
    cosine,
    sine_table,
    grad_query_weight,
    grad_key_weight,
    grad_value_weight,
    grad_out_weight,
    grad_normed,
    grads,
):
    step = pl.program_id(0)
    low = jnp.bfloat16
    da = grad_branch[...]
    n1 = normed[...]
    cos, sin = cosine[...], sine_table[...]
    scaling = HD ** (-0.5)
    group = query_in.shape[1]
    grad_out_weight[...] = dot_tn(da, attended_in[...]).astype(low)
    grad_attended = dot_nn(da, out_weight[...]).astype(low)
    for part in range(group // HD):
        columns = slice(part * HD, (part + 1) * HD)
        q, k, v = query_in[:, columns], key_in[:, columns], value_in[:, columns]
        do = grad_attended[:, columns]
        probs = probabilities(q, k, bias[...])
        grad_probs = dot_nt(do, v)
        grad_scores = probs * (grad_probs - jnp.sum(probs * grad_probs, axis=1, keepdims=True))
        grad_scores = grad_scores.astype(low)
        grads[0, :, columns] = turn_back(dot_nn(grad_scores, k) * scaling, cos, sin).astype(low)
        grads[1, :, columns] = turn_back(dot_tn(grad_scores, q) * scaling, cos, sin).astype(low)
        grads[2, :, columns] = dot_tn(probs.astype(low), do).astype(low)
    grad_query_weight[...] = dot_tn(grads[0], n1).astype(low)
    grad_key_weight[...] = dot_tn(grads[1], n1).astype(low)
    grad_value_weight[...] = dot_tn(grads[2], n1).astype(low)
    total = (
        dot_nn(grads[0], query_weight[...])
        + dot_nn(grads[1], key_weight[...])
        + dot_nn(grads[2], value_weight[...])
    )

    @pl.when(step == 0)
    def _():
        grad_normed[...] = total

    @pl.when(step > 0)
    def _():
        grad_normed[...] += total


def attend_back(
    grad_branch, normed, query, key, value, attended, weights, out_weight, bias, cosine, sine_table
):
    tokens, width = normed.shape
    group = 2 * HD
    steps = width // group
    low = jnp.bfloat16
    whole = lambda *shape: pl.BlockSpec(shape, lambda i: (0,) * len(shape))
    columns = pl.BlockSpec((tokens, group), lambda i: (0, i))
    return pl.pallas_call(
        attend_back_kernel,
        grid=(steps,),
        in_specs=[whole(tokens, width)] * 2
        + [columns] * 4
        + [pl.BlockSpec((group, width), lambda i, m=m: (i, m)) for m in range(3)]
        + [
            pl.BlockSpec((width, group), lambda i: (0, i)),
            whole(tokens, tokens),
            whole(tokens, HD),
            whole(tokens, HD),
        ],
        out_specs=[pl.BlockSpec((group, width), lambda i: (i, 0))] * 3
        + [pl.BlockSpec((width, group), lambda i: (0, i)), whole(tokens, width)],
        out_shape=[jax.ShapeDtypeStruct((width, width), low)] * 4
        + [jax.ShapeDtypeStruct((tokens, width), jnp.float32)],
        scratch_shapes=[pltpu.VMEM((3, tokens, group), low)],
        compiler_params=pltpu.CompilerParams(vmem_limit_bytes=48 * 1024 * 1024),
        cost_estimate=pl.CostEstimate(
            flops=16 * tokens * width * width, bytes_accessed=40 * width * width, transcendentals=0
        ),
    )(
        grad_branch,
        normed,
        query,
        key,
        value,
        attended,
        weights,
        weights,
        weights,
        out_weight,
        bias,
        cosine,
        sine_table,
    )


def expert_kernel(count, numbers, *refs):
    low, full = jnp.bfloat16, jnp.float32
    rows_in, grads_in, slots_in, gates_in = [refs[i * count : (i + 1) * count] for i in range(4)]
    gate_weight, up_weight, down_weight, *refs = refs[4 * count :]
    grad_total, result_total = refs[:count], refs[count : 2 * count]
    rows_out, inner_out, gated_out, grad_gate_out, grad_up_out = refs[2 * count : 2 * count + 5]
    hot_all, grad_all, result_all, word_sums = refs[2 * count + 5 :]
    tokens, width = slots_in[0].shape[2], rows_in[0].shape[1]
    slots = rows_out.shape[1] // count
    experts = word_sums.shape[1]
    q = pl.program_id(0)
    slot_ids = lax.broadcasted_iota(jnp.int32, (slots, tokens), 0).astype(full)
    parts = [slice(r * slots, (r + 1) * slots) for r in range(count)]
    here = pl.ds(pl.multiple_of(q * slots, slots), slots)
    places, gate_cols, grad_parts = [], [], []
    for r in range(count):
        place = slots_in[r][0] == slot_ids
        hot = place.astype(low)
        hot_all[r, here] = hot
        places.append(place)
        gate_cols.append(jnp.sum(jnp.where(place, gates_in[r][0], 0.0), axis=1, keepdims=True))
        rows_out[0, parts[r]] = dot_nn(hot, rows_in[r][:tokens]).astype(low)
        grad_parts.append(dot_nn(hot, grads_in[r][:tokens]))
    gate_col = jnp.concatenate(gate_cols, axis=0)
    grad_rows = jnp.concatenate(grad_parts, axis=0)
    rows = rows_out[0]
    gated = (grad_rows * gate_col).astype(low)
    gated_out[0] = gated
    gate_rows = dot_nn(rows, gate_weight[0])
    up_rows = dot_nn(rows, up_weight[0])
    logistic = jax.nn.sigmoid(gate_rows)
    silu_rows = gate_rows * logistic
    slope_rows = logistic * (1.0 + gate_rows * (1.0 - logistic))
    inner = (silu_rows * up_rows).astype(low)
    inner_out[0] = inner
    grad_inner = dot_nt(gated, down_weight[0])
    grad_gate_rows = (grad_inner * up_rows * slope_rows).astype(low)
    grad_up_rows = (grad_inner * silu_rows).astype(low)
    grad_gate_out[0] = grad_gate_rows
    grad_up_out[0] = grad_up_rows
    sent_grads = (
        dot_nt(grad_gate_rows, gate_weight[0]) + dot_nt(grad_up_rows, up_weight[0])
    ).astype(low)
    result_rows = dot_nn(inner, down_weight[0])
    gate_grad = jnp.sum(result_rows * grad_rows, axis=1, keepdims=True)
    sent_results = (result_rows * gate_col).astype(low)
    expert_ids = lax.broadcasted_iota(jnp.int32, (experts, width), 0)

    @pl.when(q == 0)
    def _():
        word_sums[...] = jnp.zeros_like(word_sums)

    for r in range(count):
        grad_all[r, here] = sent_grads[parts[r]]
        result_all[r, here] = sent_results[parts[r]]
        token_grad = jnp.sum(
            jnp.where(places[r], gate_grad[parts[r]], 0.0), axis=0, keepdims=True
        )
        words = jnp.concatenate(
            [word.astype(full) for word in split_words(token_grad)]
            + [jnp.zeros((1, width - 3 * tokens), full)],
            axis=1,
        )
        word_sums[r] += jnp.where(expert_ids == numbers[q], words, 0.0)

    @pl.when(q == PLANE - 1)
    def _():
        for r in range(count):
            grad_total[r][:tokens] = dot_tn(hot_all[r], grad_all[r]).astype(low)
            grad_total[r][tokens:] = word_sums[r].astype(low)
            result_total[r][...] = dot_tn(hot_all[r], result_all[r]).astype(low)


def run_experts(numbers, rows, grads, slot_rows, gate_rows, weights, slots):
    count = len(rows)
    extended, width = rows[0].shape
    tokens = slot_rows[0].shape[2]
    low = jnp.bfloat16
    hidden_width = weights[0].shape[2]
    whole = lambda *shape: pl.BlockSpec(shape, lambda q, numbers: (0,) * len(shape))
    each = lambda *shape: pl.BlockSpec((1,) + shape, lambda q, numbers: (q, 0, 0))
    sizes = (width, hidden_width, width, hidden_width, hidden_width)
    out = pl.pallas_call(
        functools.partial(expert_kernel, count),
        grid_spec=pltpu.PrefetchScalarGridSpec(
            num_scalar_prefetch=1,
            grid=(PLANE,),
            in_specs=[whole(extended, width)] * (2 * count)
            + [each(1, tokens)] * (2 * count)
            + [each(*array.shape[1:]) for array in weights],
            out_specs=[whole(extended, width)] * count
            + [whole(tokens, width)] * count
            + [each(count * slots, size) for size in sizes],
            scratch_shapes=[
                pltpu.VMEM((count, PLANE * slots, tokens), low),
                pltpu.VMEM((count, PLANE * slots, width), low),
                pltpu.VMEM((count, PLANE * slots, width), low),
                pltpu.VMEM((count, extended - tokens, width), jnp.float32),
            ],
        ),
        out_shape=[jax.ShapeDtypeStruct((extended, width), low)] * count
        + [jax.ShapeDtypeStruct((tokens, width), low)] * count
        + [jax.ShapeDtypeStruct((PLANE, count * slots, size), low) for size in sizes],
        compiler_params=pltpu.CompilerParams(vmem_limit_bytes=62 * 1024 * 1024),
        cost_estimate=pl.CostEstimate(
            flops=count * PLANE * slots * width * (10 * hidden_width + 8 * tokens),
            bytes_accessed=6 * PLANE * width * hidden_width,
            transcendentals=0,
        ),
    )(numbers, *rows, *grads, *slot_rows, *gate_rows, *weights)
    return out[:count], out[count : 2 * count], out[2 * count :]


FIRST_ORDERS = (0, 1, 2, 0, 1, 2)


def gather_plan(units, orders):
    least, more = divmod(units, len(orders))
    widths = [least] * len(orders)
    for i in sorted(range(len(orders)), key=lambda i: (-orders[i], -i))[:more]:
        widths[i] += 1
    if least > 2:
        for i, order in enumerate(orders):
            widths[i] += order - 1
    return tuple((order, 128 * width) for order, width in zip(orders, widths))


def shared_grads_kernel(rows, grad_gate, grad_up, grads, inner, gate_out, up_out, down_out):
    low = jnp.bfloat16
    gate_out[...] = dot_tn(rows[...], grad_gate[...]).astype(low)
    up_out[...] = dot_tn(rows[...], grad_up[...]).astype(low)
    down_out[...] = dot_tn(grads[...], inner[...]).astype(low)


def shared_grads(rows, grad_gate, grad_up, grads, inner):
    shape = jax.ShapeDtypeStruct((rows.shape[1], inner.shape[1]), jnp.bfloat16)
    return pl.pallas_call(
        shared_grads_kernel,
        in_specs=[pl.BlockSpec(memory_space=pltpu.VMEM)] * 5,
        out_specs=[pl.BlockSpec(memory_space=pltpu.VMEM)] * 3,
        out_shape=[shape] * 3,
        compiler_params=pltpu.CompilerParams(vmem_limit_bytes=32 * 1024 * 1024),
        cost_estimate=pl.CostEstimate(
            flops=6 * rows.size * inner.shape[1],
            bytes_accessed=4 * rows.size + 6 * rows.shape[1] * inner.shape[1],
            transcendentals=0,
        ),
    )(rows, grad_gate, grad_up, grads, inner)


def split_words(values):
    words = []
    for _ in range(3):
        words.append(values.astype(jnp.bfloat16))
        values = values - words[-1].astype(jnp.float32)
    return words


def after(value, other):
    return lax.optimization_barrier((value, other))[0]


def add_low(a, b):
    return (a.astype(jnp.float32) + b.astype(jnp.float32)).astype(jnp.bfloat16)


class Grid:
    def __init__(self, experts):
        self.experts = experts
        self.line = experts // PLANE
        here = lax.axis_index("expert")
        self.core = lax.axis_index("dp")
        self.at_line = here // PLANE
        self.at_plane = here % PLANE

    def shift(self, block, amount):
        pairs = [
            (i, ((i // PLANE + amount) % self.line) * PLANE + i % PLANE)
            for i in range(self.experts)
        ]
        return lax.ppermute(block, "expert", pairs)

    def swap(self, block, flip):
        pairs = [(i, (i // PLANE) * PLANE + ((i % PLANE) ^ flip)) for i in range(self.experts)]
        return lax.ppermute(block, "expert", pairs)

    def line_gather(self, block, rising=None, falling=None):
        half, rest = self.line // 2, (self.line - 1) // 2
        rising = self.shift(block, 1) if rising is None else rising
        found = [block, rising] + [None] * (self.line - 2)
        for i in range(2, half + 1):
            found[i] = self.shift(found[i - 1], 1)
        if rest:
            found[-1] = self.shift(block, -1) if falling is None else falling
            for i in range(2, rest + 1):
                found[-i] = self.shift(found[1 - i], -1)
        return found


def local(
    tokens_in,
    lengths,
    key_keep,
    routes,
    cotangent,
    attention_in,
    attention_in_momentum,
    attention_in_average,
    attention_out,
    attention_out_momentum,
    attention_out_average,
    shared_in,
    shared_in_momentum,
    shared_in_average,
    shared_down,
    shared_down_momentum,
    shared_down_average,
    router,
    router_momentum,
    router_average,
    norm_gains,
    norm_gains_momentum,
    norm_gains_average,
    expert_in,
    expert_in_momentum,
    expert_in_average,
    expert_down,
    expert_down_momentum,
    expert_down_average,
):
    low = jnp.bfloat16
    full = jnp.float32
    tokens = tokens_in.shape[0]
    model_width = tokens_in.shape[1]
    top_count = routes.shape[1]
    block_rows = router.shape[0]
    experts = router.shape[1]
    hidden_width = shared_in.shape[2]
    grid = Grid(experts)
    capacity = 9 * tokens * top_count // (8 * experts)
    slots = -(-capacity // 16) * 16
    extra_width = -(-(experts + 2) // 128) * 128

    pack_one = jnp.concatenate(
        [attention_in[m].astype(low).T for m in range(3)]
        + [
            router.astype(low),
            norm_gains.astype(low).T,
            jnp.zeros((block_rows, extra_width - experts - 2), low),
        ],
        axis=1,
    )
    pack_out = attention_out.astype(low).T
    pack_shared = jnp.concatenate(
        [shared_in[0].astype(low), shared_in[1].astype(low), shared_down.astype(low).T], axis=1
    )
    position = jnp.arange(tokens, dtype=jnp.int32)
    usable = position < lengths[0]
    named = jnp.any(
        routes.T[None, :, :] == jnp.arange(experts, dtype=jnp.int32)[:, None, None], axis=1
    )
    member = named & usable[None, :]
    earlier = (position[:, None] < position[None, :]).astype(low)
    counted = dot_nn(member.astype(low), earlier)
    slot_of = jnp.where(member, counted, -1.0)
    wanted = grid.at_line * PLANE + (grid.at_plane ^ jnp.arange(PLANE, dtype=jnp.int32))
    choose = (wanted[:, None] == jnp.arange(experts, dtype=jnp.int32)[None, :]).astype(low)

    def widen(rows):
        return jnp.pad(rows, ((0, 0), (0, model_width - rows.shape[1])))

    pair, down = expert_in[0].astype(low), expert_down[0].astype(low)
    plans = (
        gather_plan(pack_one.shape[1] // 128, FIRST_ORDERS),
        gather_plan(model_width // 128, FIRST_ORDERS),
    )
    (all_one, turned_out), down_x, down_y = first_exchange(
        experts, [pack_one, pack_out], plans, down
    )
    line_grads, sent = after(
        (jnp.concatenate([cotangent, widen(slot_of.astype(low))], axis=0), pair), turned_out
    )
    line_grads = grid.line_gather(line_grads)
    pairs = [pair, grid.swap(sent, 1), grid.swap(sent, 2)]
    downs = [down, down_x, down_y]
    all_one = all_one.reshape(model_width, -1)
    turned_out = turned_out.reshape(model_width, model_width)
    extra = all_one[:, 3 * model_width :]
    router_low = extra[:, :experts]
    gains = extra[:, experts : experts + 2].astype(full).T
    gain_one, gain_two = gains[0], gains[1]
    inputs = tokens_in.astype(full)
    rstd_one = lax.rsqrt(jnp.mean(inputs * inputs, axis=-1, keepdims=True) + eps_norm)
    normed_one = (inputs * rstd_one * gain_one).astype(low)
    cosine, sine_table = rope_tables(tokens, HD)
    bias = jnp.where(allowed_keys(lengths[0], key_keep), 0.0, mask_fill)
    query, key_rot, value, attended, hidden, normed_two = attend(
        normed_one, all_one, turned_out, bias, cosine, sine_table, tokens_in, gain_two[None]
    )
    rstd_two = lax.rsqrt(jnp.mean(hidden * hidden, axis=-1, keepdims=True) + eps_norm)

    logits = lax.dot_general(
        router_low, normed_two, (((0,), (1,)), ((), ())), preferred_element_type=full
    )
    logits = jnp.where(named, logits, mask_fill)
    logit_exps = jnp.exp(logits - jnp.max(logits, axis=0, keepdims=True))
    gating = logit_exps / jnp.sum(logit_exps, axis=0, keepdims=True)
    gating_live = jnp.where(member, gating, 0.0)
    gate_words = jnp.concatenate(split_words(gating_live), axis=1)
    line_rows = jnp.concatenate([normed_two, widen(gate_words)], axis=0)
    line_rows = after(line_rows, [line_grads[1], line_grads[-1]])
    rising, falling, *weights = second_exchange(experts, line_rows, pairs, downs)
    line_rows = grid.line_gather(line_rows, rising, falling)
    weights = [part.reshape(PLANE, -1, part.shape[-1]) for part in weights]

    kept, grad_parts, result_parts = [], [], []
    last = weights
    for start in range(0, grid.line, 2):
        group = range(start, start + 2)
        line_part = [line_rows[r] for r in group], [line_grads[r] for r in group]
        rows, grads = after(line_part, last)
        slot_rows, gate_rows = [], []
        for part in rows:
            words = dot_nn(choose, part[tokens:, : 3 * tokens])
            gate_row = words[:, :tokens] + words[:, tokens : 2 * tokens] + words[:, 2 * tokens :]
            gate_rows.append(gate_row[:, None])
        for part in grads:
            slot_rows.append(dot_nn(choose, part[tokens:, :tokens])[:, None])
        grad_part, result_part, parts = run_experts(
            wanted, rows, grads, slot_rows, gate_rows, weights, slots
        )
        kept.append(parts)
        last = grad_part
        grad_parts += [grid.shift(part, -r) if r else part for r, part in zip(group, grad_part)]
        result_parts += result_part
    routed_grad = sum(part.astype(full) for part in grad_parts)
    result_parts = after(result_parts, routed_grad)
    routed_result = sum(
        (grid.shift(part, -r) if r else part).astype(full) for r, part in enumerate(result_parts)
    )
    owns, crossed, nears = third_exchange(experts, after(kept, last))
    arrived = [grid.swap(part, flip) for part, flip in zip(nears, (1, 2))]
    gate_grads = routed_grad[tokens:]
    routed_grad = routed_grad[:tokens]
    grad_gating = (
        gate_grads[:, :tokens]
        + gate_grads[:, tokens : 2 * tokens]
        + gate_grads[:, 2 * tokens : 3 * tokens]
    )
    grad_chosen = gating * (grad_gating - jnp.sum(gating * grad_gating, axis=0, keepdims=True))
    grad_logits = grad_chosen.astype(low)
    grad_router = lax.dot_general(
        normed_two, grad_logits, (((0,), (1,)), ((), ())), preferred_element_type=full
    )

    all_shared = lax.all_gather(
        after(pack_shared, weights), ("dp", "expert"), axis=0, tiled=True
    )
    shared_pair = [all_shared[:, m * hidden_width : (m + 1) * hidden_width] for m in range(2)]
    turned_down = all_shared[:, 2 * hidden_width :]
    grad_out = cotangent.astype(full)
    shared_gate = dot_nn(normed_two, shared_pair[0])
    shared_up = dot_nn(normed_two, shared_pair[1])
    shared_silu, shared_slope = silu_parts(shared_gate)
    shared_hidden = (shared_silu * shared_up).astype(low)
    shared_result = dot_nt(shared_hidden, turned_down)
    grad_shared_hidden = dot_nn(cotangent, turned_down)
    grad_shared_gate = (grad_shared_hidden * shared_up * shared_slope).astype(low)
    grad_shared_up = (grad_shared_hidden * shared_silu).astype(low)
    grad_normed_two = dot_nt(grad_shared_gate, shared_pair[0]) + dot_nt(
        grad_shared_up, shared_pair[1]
    )
    grad_normed_two = grad_normed_two + lax.dot_general(
        grad_logits, router_low, (((0,), (1,)), ((), ())), preferred_element_type=full
    )

    grad_normed_two = grad_normed_two + routed_grad
    scaled_two = grad_normed_two * gain_two
    grad_gain_two = jnp.sum(grad_normed_two * hidden * rstd_two, axis=0)
    grad_hidden = (
        grad_out
        + rstd_two * scaled_two
        - hidden * rstd_two**3 * jnp.mean(scaled_two * hidden, axis=-1, keepdims=True)
    )
    grad_branch = grad_hidden.astype(low)
    grads_shared = shared_grads(
        normed_two, grad_shared_gate, grad_shared_up, cotangent, shared_hidden
    )
    *grads_attention, grad_normed_one = attend_back(
        grad_branch,
        normed_one,
        query,
        key_rot,
        value,
        attended,
        all_one,
        turned_out,
        bias,
        cosine,
        sine_table,
    )
    scaled_one = grad_normed_one * gain_one
    grad_gain_one = jnp.sum(grad_normed_one * inputs * rstd_one, axis=0)
    input_grad = (
        grad_hidden
        + rstd_one * scaled_one
        - inputs * rstd_one**3 * jnp.mean(scaled_one * inputs, axis=-1, keepdims=True)
    )
    grad_extra = jnp.concatenate(
        [
            grad_router.astype(low),
            jnp.stack([grad_gain_one, grad_gain_two], axis=1).astype(low),
            jnp.zeros((model_width, extra_width - experts - 2), low),
        ],
        axis=1,
    )
    *sums, total_in, total_down = sum_all(
        experts,
        grads_attention + list(grads_shared) + [grad_extra],
        sum_plans(model_width, hidden_width, extra_width),
        owns,
        crossed,
        arrived,
    )
    output = (hidden + shared_result + routed_result).astype(low)

    sums = [part.astype(full) for part in sums]
    summed_in = jnp.stack([part.T for part in sums[:3]], axis=0)
    summed_out = sums[3].T
    summed_shared_in = jnp.stack(sums[4:6], axis=0)
    summed_shared_down = sums[6].T
    summed_router = sums[7][:, :experts]
    summed_gains = sums[7][:, experts : experts + 2].T
    upd_attn_in = advance(
        attention_in, attention_in_momentum, attention_in_average, summed_in, rate_attention_in
    )
    upd_attn_out = advance(
        attention_out, attention_out_momentum, attention_out_average, summed_out, rate_attention_out
    )
    upd_shared_in = advance(
        shared_in, shared_in_momentum, shared_in_average, summed_shared_in, rate_shared_in
    )
    upd_shared_down = advance(
        shared_down, shared_down_momentum, shared_down_average, summed_shared_down, rate_shared_down
    )
    upd_router = advance(router, router_momentum, router_average, summed_router, rate_router)
    upd_gains = advance(
        norm_gains, norm_gains_momentum, norm_gains_average, summed_gains, rate_gains
    )
    upd_expert_in = advance(
        expert_in,
        expert_in_momentum,
        expert_in_average,
        total_in.astype(full)[None],
        rate_expert_in,
    )
    upd_expert_down = advance(
        expert_down,
        expert_down_momentum,
        expert_down_average,
        total_down.astype(full)[None],
        rate_expert_down,
    )
    return (
        output,
        input_grad,
        upd_attn_in[0],
        upd_attn_in[1],
        upd_attn_in[2],
        upd_attn_out[0],
        upd_attn_out[1],
        upd_attn_out[2],
        upd_shared_in[0],
        upd_shared_in[1],
        upd_shared_in[2],
        upd_shared_down[0],
        upd_shared_down[1],
        upd_shared_down[2],
        upd_router[0],
        upd_router[1],
        upd_router[2],
        upd_gains[0],
        upd_gains[1],
        upd_gains[2],
        upd_expert_in[0],
        upd_expert_in[1],
        upd_expert_in[2],
        upd_expert_down[0],
        upd_expert_down[1],
        upd_expert_down[2],
    )


def solution(mesh):
    in_specs = (
        P(("dp", "expert"), None),
        P(("dp", "expert")),
        P(("dp", "expert")),
        P(("dp", "expert"), None),
        P(("dp", "expert"), None),
        P(None, None, ("dp", "expert")),
        P(None, None, ("dp", "expert")),
        P(None, None, ("dp", "expert")),
        P(None, ("dp", "expert")),
        P(None, ("dp", "expert")),
        P(None, ("dp", "expert")),
        P(None, ("dp", "expert"), None),
        P(None, ("dp", "expert"), None),
        P(None, ("dp", "expert"), None),
        P(None, ("dp", "expert")),
        P(None, ("dp", "expert")),
        P(None, ("dp", "expert")),
        P(("dp", "expert"), None),
        P(("dp", "expert"), None),
        P(("dp", "expert"), None),
        P(None, ("dp", "expert")),
        P(None, ("dp", "expert")),
        P(None, ("dp", "expert")),
        P("expert", None, "dp", None),
        P("expert", None, "dp", None),
        P("expert", None, "dp", None),
        P("expert", "dp", None),
        P("expert", "dp", None),
        P("expert", "dp", None),
    )
    out_specs = (
        P(("dp", "expert"), None),
        P(("dp", "expert"), None),
        P(None, None, ("dp", "expert")),
        P(None, None, ("dp", "expert")),
        P(None, None, ("dp", "expert")),
        P(None, ("dp", "expert")),
        P(None, ("dp", "expert")),
        P(None, ("dp", "expert")),
        P(None, ("dp", "expert"), None),
        P(None, ("dp", "expert"), None),
        P(None, ("dp", "expert"), None),
        P(None, ("dp", "expert")),
        P(None, ("dp", "expert")),
        P(None, ("dp", "expert")),
        P(("dp", "expert"), None),
        P(("dp", "expert"), None),
        P(("dp", "expert"), None),
        P(None, ("dp", "expert")),
        P(None, ("dp", "expert")),
        P(None, ("dp", "expert")),
        P("expert", None, "dp", None),
        P("expert", None, "dp", None),
        P("expert", None, "dp", None),
        P("expert", "dp", None),
        P("expert", "dp", None),
        P("expert", "dp", None),
    )
    return jax.shard_map(local, mesh=mesh, in_specs=in_specs, out_specs=out_specs, check_vma=False)
```

```python
import functools

import jax
import jax.numpy as jnp
from jax import lax
from jax.experimental import pallas as pl
from jax.experimental.pallas import tpu as pltpu
from jax.sharding import PartitionSpec as P

HD = 128
STEP = 4


eps_norm = 1e-06
theta_base = 10000.0
momentum_decay = 0.9
mask_fill = -1e30
rate_attention_in = 2e-05
rate_attention_out = 0.002
rate_shared_in = 3e-05
rate_shared_down = 0.0002
rate_router = 1.5e-05
rate_gains = 0.0002
rate_expert_in = 0.0004
rate_expert_down = 0.008


def rope_tables(length, head_width):
    half_width = head_width // 2
    frequency = theta_base ** (-(jnp.arange(half_width, dtype=jnp.float32) * 2.0 / head_width))
    angles = jnp.arange(length, dtype=jnp.float32)[:, None] * frequency[None, :]
    cosine, sine_table = jnp.cos(angles), jnp.sin(angles)
    return (
        jnp.concatenate([cosine, cosine], axis=1),
        jnp.concatenate([-sine_table, sine_table], axis=1),
    )


def allowed_keys(length, keep_flags):
    amount = keep_flags.shape[0]
    position = jnp.arange(amount)
    causal = position[None, :] <= position[:, None]
    usable = (position < length) & (keep_flags == 1)
    return causal & (usable[None, :] | (position[None, :] == position[:, None]))


def silu_parts(values):
    logistic = jax.nn.sigmoid(values)
    return (values * logistic, logistic * (1.0 + values * (1.0 - logistic)))


def advance(weight, moment, average, gradient, step_rate):
    moment_new = momentum_decay * moment + gradient
    weight_new = weight - step_rate * (gradient + momentum_decay * moment_new)
    average_new = average + (weight_new - average) / (STEP + 1)
    return (weight_new, moment_new, average_new)


def dot_nn(a, b):
    return lax.dot_general(a, b, (((1,), (0,)), ((), ())), preferred_element_type=jnp.float32)


def dot_nt(a, b):
    return lax.dot_general(a, b, (((1,), (1,)), ((), ())), preferred_element_type=jnp.float32)


def dot_tn(a, b):
    return lax.dot_general(a, b, (((0,), (0,)), ((), ())), preferred_element_type=jnp.float32)


PLANE = 4
MESH = pl.DeviceIdType.MESH


class Spot:
    def __init__(self, line):
        here = lax.axis_index("expert")
        self.line = line
        self.core = lax.axis_index("dp")
        self.at = lax.div(here, PLANE)
        rest = lax.rem(here, PLANE)
        self.y, self.x = lax.div(rest, 2), lax.rem(rest, 2)

    def chip(self, at, y, x):
        return (self.core, at * PLANE + y * 2 + x)

    def around(self, amount):
        return lax.rem(self.at + amount + self.line, self.line)

    def partner(self, way):
        if way == "core":
            return (1 - self.core, self.at * PLANE + self.y * 2 + self.x)
        if way == "x":
            return self.chip(self.at, self.y, 1 - self.x)
        if way == "y":
            return self.chip(self.at, 1 - self.y, self.x)
        return self.chip(self.around(1 if way == "up" else -1), self.y, self.x)


def meet(spot):
    barrier = pltpu.get_barrier_semaphore()
    for way in ("core", "x", "y", "up", "down"):
        pl.semaphore_signal(barrier, inc=1, device_id=spot.partner(way), device_id_type=MESH)
    pl.semaphore_wait(barrier, 5)


class Moves:
    def __init__(self, spot, send_sems, recv_sems, local_sems):
        self.spot, self.send_sems, self.recv_sems = spot, send_sems, recv_sems
        self.local_sems = local_sems
        self.made, self.kept, self.loose = 0, 0, []

    def start(self, source, target, way, later=False):
        copy = pltpu.make_async_remote_copy(
            src_ref=source,
            dst_ref=target,
            send_sem=self.send_sems.at[self.made],
            recv_sem=self.recv_sems.at[self.made],
            device_id=self.spot.partner(way),
            device_id_type=MESH,
        )
        self.made += 1
        copy.start()
        if later:
            self.loose.append(copy)
        return copy

    def keep(self, source, target, later=False):
        copy = pltpu.make_async_copy(source, target, self.local_sems.at[self.kept])
        self.kept += 1
        copy.start()
        if later:
            self.loose.append(copy)
        return copy

    def finish(self):
        for copy in self.loose:
            copy.wait()


def in_steps(chains):
    while chains:
        left = []
        for chain in chains:
            try:
                next(chain)
                left.append(chain)
            except StopIteration:
                pass
        chains = left
        yield


def in_turn(chains):
    for _ in in_steps(chains):
        pass


def place_chain(moves, source, buffer, target):
    copy = moves.keep(source, buffer)
    yield
    copy.wait()
    moves.keep(buffer, target, later=True)


def core_chain(moves, own, whole, buffer):
    core = moves.spot.core
    moves.start(own, whole.at[core], "core", later=True)
    return place_chain(moves, own, buffer, whole.at[core])


def dense_chain(moves, whole, columns, order):
    spot = moves.spot
    half, rest = spot.line // 2, (spot.line - 1) // 2
    everything = slice(None)
    held = {"z": spot.at, "y": spot.y, "x": spot.x}

    def region(**other):
        at = dict(held, **other)
        return whole.at[spot.core, at["z"], at["y"], at["x"], everything, columns]

    def forward(part):
        moves.start(part, part, "core", later=True)

    for stage, dim in enumerate(order):
        if dim == "z":
            up = down = None
            for i in range(1, half + 1):
                part = region(z=spot.around(1 - i))
                up = moves.start(part, part, "up")
                if i <= rest:
                    part = region(z=spot.around(i - 1))
                    down = moves.start(part, part, "down")
                if stage == 0 and i == 1:
                    forward(region())
                yield
                up.wait()
                forward(region(z=spot.around(-i)))
                if i <= rest:
                    down.wait()
                    forward(region(z=spot.around(i)))
        else:
            part = region()
            copy = moves.start(part, part, dim)
            if stage == 0:
                forward(region())
            yield
            copy.wait()
            forward(region(**{dim: 1 - held[dim]}))
        held[dim] = everything


ORDERS = ("xyz", "yzx", "zxy", "zyx")


def first_kernel(line, plans, *refs):
    count = len(plans)
    shards, down, refs = refs[:count], refs[count], refs[count + 1 :]
    results, over_x, over_y, refs = refs[:count], refs[count], refs[count + 1], refs[count + 2 :]
    wholes, refs = refs[:count], refs[count:]
    spot = Spot(line)
    meet(spot)
    moves = Moves(spot, *refs)
    loads = [
        moves.keep(shards[n], wholes[n].at[spot.core, spot.at, spot.y, spot.x])
        for n in range(count)
    ]
    for copy in loads:
        copy.wait()
    chains = []
    for n, plan in enumerate(plans):
        start = 0
        for order, width in plan:
            columns = slice(start, start + width)
            chains.append(dense_chain(moves, wholes[n], columns, ORDERS[order]))
            start += width
    stages = 0
    for _ in in_steps(chains):
        stages += 1
        if stages == 1:
            moves.start(down, over_x, "x", later=True)
            moves.start(down, over_y, "y", later=True)
    moves.finish()
    stores = [moves.keep(wholes[n], results[n]) for n in range(count)]
    for copy in stores:
        copy.wait()


def hbm(count):
    return [pl.BlockSpec(memory_space=pl.ANY)] * count


def semaphores(remote, local):
    return [
        pltpu.SemaphoreType.DMA((remote,)),
        pltpu.SemaphoreType.DMA((remote,)),
        pltpu.SemaphoreType.DMA((local,)),
    ]


def both_halves(array):
    return jax.ShapeDtypeStruct((2,) + array.shape, array.dtype)


def first_exchange(experts, shards, plans, down):
    line = experts // PLANE
    count = len(shards)
    remote = sum(len(plan) for plan in plans) * (2 * line + 3) + 2
    out = pl.pallas_call(
        functools.partial(first_kernel, line, plans),
        out_shape=[
            jax.ShapeDtypeStruct((2, line, 2, 2) + shard.shape, shard.dtype) for shard in shards
        ]
        + [jax.ShapeDtypeStruct(down.shape, down.dtype)] * 2,
        in_specs=hbm(count + 1),
        out_specs=hbm(count + 2),
        scratch_shapes=[
            pltpu.VMEM((2, line, 2, 2) + shard.shape, shard.dtype) for shard in shards
        ]
        + semaphores(remote, 2 * count),
        compiler_params=pltpu.CompilerParams(
            collective_id=1, has_side_effects=True, vmem_limit_bytes=60 * 1024 * 1024
        ),
    )(*shards, down)
    return out[:count], out[count], out[count + 1]


def second_kernel(line, *refs):
    rows, pairs, downs, refs = refs[0], refs[1:4], refs[4:7], refs[7:]
    rising, falling, wholes, refs = refs[0], refs[1], refs[2:5], refs[5:]
    buffers, refs = refs[:9], refs[9:]
    spot = Spot(line)
    meet(spot)
    moves = Moves(spot, *refs)
    core = spot.core
    gate, up, down = wholes
    (_, pair_x, pair_y), (_, down_x, down_y) = pairs, downs
    half = down_x.shape[0] // 2

    def far_chain(source, target, way):
        copy = moves.start(source, target, way)
        yield
        copy.wait()
        moves.start(target, target, "core", later=True)

    moves.start(rows, rising, "up", later=True)
    moves.start(rows, falling, "down", later=True)
    upper, lower = pl.ds(0, half), pl.ds(half, half)
    in_turn(
        [
            far_chain(pair_y.at[1], up.at[3, core], "x"),
            far_chain(pair_x.at[0], gate.at[3, core], "y"),
            far_chain(down_y.at[lower], down.at[3, core, lower], "x"),
            far_chain(down_x.at[upper], down.at[3, core, upper], "y"),
        ]
        + [
            core_chain(moves, half_of, wholes[i].at[q], buffers[3 * q + i])
            for q in range(3)
            for i, half_of in enumerate((pairs[q].at[0], pairs[q].at[1], downs[q]))
        ]
    )
    moves.finish()


def second_exchange(experts, rows, pairs, downs):
    line = experts // PLANE
    low = rows.dtype
    shapes = [pairs[0].shape[1:]] * 2 + [downs[0].shape]
    return pl.pallas_call(
        functools.partial(second_kernel, line),
        out_shape=[jax.ShapeDtypeStruct(rows.shape, low)] * 2
        + [jax.ShapeDtypeStruct((PLANE, 2) + shape, low) for shape in shapes],
        in_specs=hbm(7),
        out_specs=hbm(5),
        scratch_shapes=[pltpu.VMEM(shape, low) for shape in shapes * 3] + semaphores(19, 18),
        compiler_params=pltpu.CompilerParams(
            collective_id=3, has_side_effects=True, vmem_limit_bytes=60 * 1024 * 1024
        ),
    )(rows, *pairs, *downs)


def packed(half, hidden_width, down_half, width):
    edge, more = down_half // 2, width - hidden_width
    below = 2 * half + down_half
    full = slice(0, hidden_width)
    rest = slice(hidden_width, width)
    places = [
        (0, slice(0, half), full, slice(0, half), full),
        (1, slice(half, 2 * half), full, slice(0, half), full),
        (2, slice(2 * half, 2 * half + edge), full, slice(0, edge), full),
        (2, slice(2 * half + edge, below), full, slice(edge, down_half), full),
        (2, slice(below, below + edge), slice(0, more), slice(0, edge), rest),
        (2, slice(below, below + edge), slice(more, 2 * more), slice(edge, down_half), rest),
    ]
    return places, below + edge, 2 * more


def third_kernel(line, groups, *refs):
    low, full = jnp.bfloat16, jnp.float32
    kept = [refs[5 * r : 5 * r + 5] for r in range(groups)]
    refs = refs[5 * groups :]
    owns, crossed, nears, refs = refs[:3], refs[3:6], refs[6:8], refs[8:]
    loaded, refs = [refs[:5], refs[5:10]], refs[10:]
    results, refs = [refs[:6], refs[6:12]], refs[12:]
    far_box, far_in, near_box, down_grad, refs = refs[:3], refs[3:7], refs[7:9], refs[9], refs[10:]
    spot = Spot(line)
    meet(spot)
    moves = Moves(spot, *refs)
    order = (3, 1, 2, 0)
    slots = kept[0][0].shape[1]
    loads = {}
    rows_half, hidden_width = results[0][0].shape
    down_half, width = results[0][2].shape
    edge = down_half // 2
    places, _, used = packed(rows_half, hidden_width, down_half, width)

    def load(n):
        loads[n] = [
            moves.keep(kept[r][i].at[order[n]], loaded[n % 2][i].at[pl.ds(r * slots, slots)])
            for r in range(groups)
            for i in range(5)
        ]

    def add(target, source):
        target[...] = (target[...].astype(full) + source[...].astype(full)).astype(low)

    load(0)
    for box in near_box:
        spare = (slice(2 * rows_half + down_half, box.shape[0]), slice(used, hidden_width))
        box[spare] = jnp.zeros((edge, hidden_width - used), low)
    sent = {}

    def weights(n):
        if n + 1 < PLANE:
            load(n + 1)
        for copy in loads[n]:
            copy.wait()
        rows, inner, gated, grad_gate, grad_up = loaded[n % 2]
        buffers = results[n % 2]
        down_grad[...] = dot_tn(inner[...], gated[...]).astype(low)
        q = order[n]
        for which in (1, 0):
            place = jnp.bitwise_xor(spot.core, which)
            gate_out, up_out, down_out = buffers[3 * which : 3 * which + 3]
            part = rows[:, pl.ds(pl.multiple_of(place * rows_half, 128), rows_half)]
            gate_out[...] = dot_tn(part, grad_gate[...]).astype(low)
            up_out[...] = dot_tn(part, grad_up[...]).astype(low)
            down_out[...] = down_grad[pl.ds(pl.multiple_of(place * down_half, 16), down_half), :]
            if which and q in (0, 3):
                targets = crossed if q == 0 else far_box
                sent[n] = [moves.start(buffers[3 + i], targets[i], "core") for i in range(3)]
            elif which:
                sent[n] = [
                    moves.start(
                        buffers[3 + i].at[rows_at, columns_at],
                        near_box[q - 1].at[to_rows, to_columns],
                        "core",
                    )
                    for i, to_rows, to_columns, rows_at, columns_at in places
                ]
            elif q == 0:
                sent[n] += [moves.keep(buffers[i], owns[i]) for i in range(3)]

    def far():
        for copy in sent[0]:
            copy.wait()
        mine = results[0][:3]
        for i in range(3):
            add(far_box[i], mine[i])
        upper, lower = pl.ds(0, edge), pl.ds(edge, edge)
        return [
            moves.start(far_box[0], far_in[0], "y"),
            moves.start(far_box[1], far_in[1], "x"),
            moves.start(far_box[2].at[upper], far_in[2], "y"),
            moves.start(far_box[2].at[lower], far_in[3], "x"),
        ]

    def near(n):
        for copy in sent[n]:
            copy.wait()
        box = near_box[order[n] - 1]
        for i, to_rows, to_columns, rows_at, columns_at in places:
            add(box.at[to_rows, to_columns], results[n % 2][i].at[rows_at, columns_at])

    weights(0)
    weights(1)
    across = far()
    weights(2)
    near(1)
    weights(3)
    near(2)
    for copy in across:
        copy.wait()
    rest, full_width = slice(hidden_width, width), slice(0, hidden_width)
    for box, i, source in ((near_box[0], 0, far_in[0]), (near_box[1], 1, far_in[1])):
        _, to_rows, to_columns, _, _ = places[i]
        add(box.at[to_rows, to_columns], source)
    for box, i, source in ((near_box[0], 0, far_in[2]), (near_box[1], 1, far_in[3])):
        for index, columns_at in ((2 + i, full_width), (4 + i, rest)):
            _, to_rows, to_columns, _, _ = places[index]
            add(box.at[to_rows, to_columns], source.at[:, columns_at])
    stores = [moves.keep(box, target) for box, target in zip(near_box, nears)]
    for copy in sent[3] + stores:
        copy.wait()


def third_exchange(experts, kept):
    line = experts // PLANE
    low = jnp.bfloat16
    rows, inner = kept[0][0], kept[0][1]
    slots, width, hidden_width = rows.shape[1], rows.shape[2], inner.shape[2]
    half, down_half = width // 2, hidden_width // 2
    pieces = [(half, hidden_width), (half, hidden_width), (down_half, width)]
    far = pieces[:2] + [(down_half // 2, width)] * 2
    package = (packed(half, hidden_width, down_half, width)[1], hidden_width)
    out = pl.pallas_call(
        functools.partial(third_kernel, line, len(kept)),
        out_shape=[jax.ShapeDtypeStruct(size, low) for size in pieces * 2 + [package] * 2],
        in_specs=hbm(5 * len(kept)),
        out_specs=hbm(8),
        scratch_shapes=[
            pltpu.VMEM((len(kept) * slots, array.shape[2]), low) for array in list(kept[0]) * 2
        ]
        + [pltpu.VMEM(size, low) for size in pieces * 4]
        + [pltpu.VMEM(size, low) for size in pieces + far + [package] * 2]
        + [pltpu.VMEM((hidden_width, width), low)]
        + semaphores(2 * 3 + 2 * 6 + 4, 5 * PLANE * len(kept) + 3 + 2),
        compiler_params=pltpu.CompilerParams(
            collective_id=4, has_side_effects=True, vmem_limit_bytes=62 * 1024 * 1024
        ),
    )(*[array for parts in kept for array in parts])
    return out[:3], out[3:6], out[6:]


def sum_plans(width, hidden_width, extra_width):
    edge, half = width * 6 // 10, width // 2
    out_edge = width * 7 // 10
    gate_edge, down_edge = hidden_width * 5 // 7, hidden_width * 4 // 7
    return (
        (((0, 0, edge),), ((1, 0, half),), ((0, edge, width - edge),)),
        (((2, 0, edge),), ((1, half, width - half),), ((2, edge, width - edge),)),
        (
            ((3, 0, out_edge),),
            ((4, 0, gate_edge),),
            ((3, out_edge, width - out_edge), (7, 0, extra_width)),
        ),
        (
            ((5, 0, hidden_width), (4, gate_edge, hidden_width - gate_edge)),
            ((6, 0, down_edge),),
            ((6, down_edge, hidden_width - down_edge),),
        ),
    )


def total_chain(moves, owns, crossed, totals, buffers):
    full = jnp.float32
    half, hidden_width = owns[0].shape
    down_half, width = owns[2].shape
    edge = down_half // 2
    jobs = []
    for i in range(2):
        for rows in range(0, half, half // 4):
            jobs.append((i, rows, half // 4))
    for rows in range(0, down_half, edge // 2):
        jobs.append((2, rows, edge // 2))
    loads, stores = {}, {}

    def box(n, i):
        wide = jobs[n][0] == 2
        return buffers[10 * (n % 2) + 5 * wide + i]

    def load(n):
        which, start, rows = jobs[n]
        at = pl.ds(start, rows)
        copies = [(owns[which].at[at], box(n, 0)), (crossed[which].at[at], box(n, 1))]
        loads[n] = [moves.keep(source, target) for source, target in copies]

    load(0)
    for n, (which, start, rows) in enumerate(jobs):
        if n + 1 < len(jobs):
            load(n + 1)
        for copy in loads[n]:
            copy.wait()
        if n >= 2:
            for copy in stores[n - 2]:
                copy.wait()
        total = box(n, 4)
        total[...] = sum(box(n, i)[...].astype(full) for i in range(2)).astype(total.dtype)
        at = pl.ds(start, rows)
        target = totals[0].at[which, at] if which < 2 else totals[1].at[at]
        stores[n] = [moves.keep(total, target)]
        if n % 2:
            yield
    for n in (len(jobs) - 2, len(jobs) - 1):
        for copy in stores[n]:
            copy.wait()


def total_buffers(half, hidden_width, down_half, width, dtype):
    shapes = [(half // 4, hidden_width)] * 5 + [(down_half // 4, width)] * 5
    return [pltpu.VMEM(shape, dtype) for shape in shapes * 2]


def sum_kernel(line, plans, arrays, *refs):
    count = len(plans)
    grads, refs = refs[:arrays], refs[arrays:]
    owns, crossed, refs = refs[:3], refs[3:6], refs[6:]
    sums, refs = refs[:arrays], refs[arrays:]
    totals, refs = refs[:2], refs[2:]
    buffers, refs = refs[:20], refs[20:]
    kept, refs = refs[: 3 * count], refs[3 * count :]
    core_in, refs = refs[: 3 * count], refs[3 * count :]
    first_in, refs = refs[: 3 * count], refs[3 * count :]
    second_in, refs = refs[: 3 * count], refs[3 * count :]
    third_in, refs = refs[: 3 * count], refs[3 * count :]
    spot = Spot(line)
    meet(spot)
    moves = Moves(spot, *refs)
    half, rest = line // 2, (line - 1) // 2
    everything = slice(None)
    orders = ("xyz", "yzx", "zxy")

    loads, swaps = [], []
    at = 0
    for n, plan in enumerate(plans):
        for o, pieces in enumerate(plan):
            mine, theirs = [], []
            start = 0
            for which, first, width in pieces:
                ref = grads[which]
                source = slice(first, first + width)
                target = slice(start, start + width)
                mine.append(
                    moves.keep(
                        ref.at[spot.core, :, :, :, :, source],
                        kept[3 * n + o].at[:, :, :, :, target],
                    )
                )
                theirs.append(
                    moves.start(
                        ref.at[1 - spot.core, :, :, :, :, source],
                        core_in[3 * n + o].at[:, :, :, :, target],
                        "core",
                    )
                )
                at += 1
                start += width
            loads.append(mine)
            swaps.append(theirs)

    def add(target, source):
        lead = target.shape[:-2]
        total = 1
        for extent in lead:
            total *= extent

        def one(i, carry):
            index = []
            for extent in reversed(lead):
                index.insert(0, lax.rem(i, extent))
                i = lax.div(i, extent)
            index = tuple(index)
            target[index] = (
                target[index].astype(jnp.float32) + source[index].astype(jnp.float32)
            ).astype(target.dtype)
            return carry

        lax.fori_loop(0, total, one, 0)

    def chain(n, o):
        buffer = kept[3 * n + o]
        mine, theirs = loads[3 * n + o], swaps[3 * n + o]
        for copy in mine:
            copy.wait()
        for copy in theirs:
            copy.wait()
        add(buffer, core_in[3 * n + o])
        inbox = [first_in[3 * n + o], second_in[3 * n + o], third_in[3 * n + o]]
        held = {"z": everything, "y": everything, "x": everything}

        def region(**other):
            at = dict(held, **other)
            return buffer.at[at["z"], at["y"], at["x"]]

        for stage, dim in enumerate(orders[o]):
            box = inbox[stage]
            if dim == "z":
                up = down = None
                for i in range(half, 0, -1):
                    down = moves.start(region(z=spot.around(-i)), box.at[i - 1], "down")
                    if i <= rest:
                        up = moves.start(region(z=spot.around(i)), box.at[half + i - 1], "up")
                    yield
                    down.wait()
                    add(region(z=spot.around(1 - i)), box.at[i - 1])
                    if i <= rest:
                        up.wait()
                        add(region(z=spot.around(i - 1)), box.at[half + i - 1])
                held[dim] = spot.at
            else:
                own = spot.y if dim == "y" else spot.x
                copy = moves.start(region(**{dim: 1 - own}), box, dim)
                yield
                copy.wait()
                held[dim] = own
                add(region(), box)
        results, start = [], 0
        for which, first, width in plans[n][o]:
            source = region().at[:, slice(start, start + width)]
            results.append(moves.keep(source, sums[which].at[:, slice(first, first + width)]))
            start += width
        yield
        for result in results:
            result.wait()

    chains = [chain(n, o) for n in range(count) for o in range(3)]
    chains.append(total_chain(moves, owns, crossed, totals, buffers))
    in_turn(chains)


def sum_all(experts, grads, plans, owns, crossed):
    line = experts // PLANE
    half, rest = line // 2, (line - 1) // 2
    rows = grads[0].shape[0] // (2 * experts)
    dtype = grads[0].dtype
    operands = [array.reshape(2, line, 2, 2, rows, array.shape[1]) for array in grads]
    shapes = [jax.ShapeDtypeStruct((rows, array.shape[1]), dtype) for array in grads]
    boxes = [[], [], [], [], []]
    for plan in plans:
        for o, pieces in enumerate(plan):
            steps = half + rest
            block = (rows, sum(width for _, _, width in pieces))
            boxes[0].append((line, 2, 2) + block)
            boxes[1].append((line, 2, 2) + block)
            if o == 0:
                inboxes = [(line, 2), (line,), (steps,)]
            elif o == 1:
                inboxes = [(line, 2), (steps, 2), ()]
            else:
                inboxes = [(steps, 2, 2), (2,), ()]
            for i, lead in enumerate(inboxes):
                boxes[2 + i].append(lead + block)
    count = len(plans)
    given = sum(len(pieces) for plan in plans for pieces in plan)
    number = given + 3 * count * (line + 1)
    others = list(owns) + list(crossed)
    shapes += [
        jax.ShapeDtypeStruct((2,) + owns[0].shape, dtype),
        jax.ShapeDtypeStruct(owns[2].shape, dtype),
    ]
    return pl.pallas_call(
        functools.partial(sum_kernel, line, plans, len(grads)),
        out_shape=shapes,
        in_specs=hbm(len(operands) + len(others)),
        out_specs=hbm(len(grads) + 2),
        scratch_shapes=total_buffers(*owns[0].shape, *owns[2].shape, dtype)
        + [pltpu.VMEM(shape, dtype) for kind in boxes for shape in kind]
        + semaphores(number, 2 * given + 12 * 7),
        compiler_params=pltpu.CompilerParams(
            collective_id=2, has_side_effects=True, vmem_limit_bytes=60 * 1024 * 1024
        ),
    )(*operands, *others)


def turn(values, cosine, sine_table):
    return values * cosine + pltpu.roll(values, HD // 2, 1) * sine_table


def turn_back(values, cosine, sine_table):
    return values * cosine - pltpu.roll(values, HD // 2, 1) * sine_table


def probabilities(query, key, bias):
    scores = dot_nt(query, key) * HD ** (-0.5) + bias
    exps = jnp.exp(scores - jnp.max(scores, axis=1, keepdims=True))
    return exps / jnp.sum(exps, axis=1, keepdims=True)


def attend_kernel(
    steps,
    normed,
    query_weight,
    key_weight,
    value_weight,
    out_weight,
    bias,
    cosine,
    sine_table,
    inputs,
    gain,
    query_out,
    key_out,
    value_out,
    attended_out,
    hidden_out,
    normed_out,
):
    step = pl.program_id(0)
    low = jnp.bfloat16
    n1 = normed[...]
    cos, sin = cosine[...], sine_table[...]
    query = dot_nt(n1, query_weight[...])
    key = dot_nt(n1, key_weight[...])
    value_out[...] = dot_nt(n1, value_weight[...]).astype(low)
    for part in range(query.shape[1] // HD):
        columns = slice(part * HD, (part + 1) * HD)
        q = turn(query[:, columns], cos, sin).astype(low)
        k = turn(key[:, columns], cos, sin).astype(low)
        query_out[:, columns] = q
        key_out[:, columns] = k
        probs = probabilities(q, k, bias[...])
        attended_out[:, columns] = dot_nn(probs.astype(low), value_out[:, columns]).astype(low)
    branch = dot_nt(attended_out[...], out_weight[...])

    @pl.when(step == 0)
    def _():
        hidden_out[...] = inputs[...].astype(jnp.float32) + branch

    @pl.when(step > 0)
    def _():
        hidden_out[...] += branch

    @pl.when(step == steps - 1)
    def _():
        hidden = hidden_out[...]
        rstd = lax.rsqrt(jnp.mean(hidden * hidden, axis=1, keepdims=True) + eps_norm)
        normed_out[...] = (hidden * rstd * gain[...]).astype(low)


def attend(normed, weights, out_weight, bias, cosine, sine_table, inputs, gain):
    tokens, width = normed.shape
    group = 2 * HD
    steps = width // group
    low = jnp.bfloat16
    whole = lambda *shape: pl.BlockSpec(shape, lambda i: (0,) * len(shape))
    columns = pl.BlockSpec((tokens, group), lambda i: (0, i))
    return pl.pallas_call(
        functools.partial(attend_kernel, steps),
        grid=(steps,),
        in_specs=[whole(tokens, width)]
        + [pl.BlockSpec((group, width), lambda i, m=m: (i, m)) for m in range(3)]
        + [
            pl.BlockSpec((width, group), lambda i: (0, i)),
            whole(tokens, tokens),
            whole(tokens, HD),
            whole(tokens, HD),
            whole(tokens, width),
            whole(1, width),
        ],
        out_specs=[columns] * 4 + [whole(tokens, width)] * 2,
        out_shape=[jax.ShapeDtypeStruct((tokens, width), low)] * 4
        + [
            jax.ShapeDtypeStruct((tokens, width), jnp.float32),
            jax.ShapeDtypeStruct((tokens, width), low),
        ],
        compiler_params=pltpu.CompilerParams(vmem_limit_bytes=48 * 1024 * 1024),
        cost_estimate=pl.CostEstimate(
            flops=8 * tokens * width * width, bytes_accessed=20 * width * width, transcendentals=0
        ),
    )(normed, weights, weights, weights, out_weight, bias, cosine, sine_table, inputs, gain)


def attend_back_kernel(
    grad_branch,
    normed,
    query_in,
    key_in,
    value_in,
    attended_in,
    query_weight,
    key_weight,
    value_weight,
    out_weight,
    bias,
    cosine,
    sine_table,
    grad_query_weight,
    grad_key_weight,
    grad_value_weight,
    grad_out_weight,
    grad_normed,
    grads,
):
    step = pl.program_id(0)
    low = jnp.bfloat16
    da = grad_branch[...]
    n1 = normed[...]
    cos, sin = cosine[...], sine_table[...]
    scaling = HD ** (-0.5)
    group = query_in.shape[1]
    grad_out_weight[...] = dot_tn(da, attended_in[...]).astype(low)
    grad_attended = dot_nn(da, out_weight[...]).astype(low)
    for part in range(group // HD):
        columns = slice(part * HD, (part + 1) * HD)
        q, k, v = query_in[:, columns], key_in[:, columns], value_in[:, columns]
        do = grad_attended[:, columns]
        probs = probabilities(q, k, bias[...])
        grad_probs = dot_nt(do, v)
        grad_scores = probs * (grad_probs - jnp.sum(probs * grad_probs, axis=1, keepdims=True))
        grad_scores = grad_scores.astype(low)
        grads[0, :, columns] = turn_back(dot_nn(grad_scores, k) * scaling, cos, sin).astype(low)
        grads[1, :, columns] = turn_back(dot_tn(grad_scores, q) * scaling, cos, sin).astype(low)
        grads[2, :, columns] = dot_tn(probs.astype(low), do).astype(low)
    grad_query_weight[...] = dot_tn(grads[0], n1).astype(low)
    grad_key_weight[...] = dot_tn(grads[1], n1).astype(low)
    grad_value_weight[...] = dot_tn(grads[2], n1).astype(low)
    total = (
        dot_nn(grads[0], query_weight[...])
        + dot_nn(grads[1], key_weight[...])
        + dot_nn(grads[2], value_weight[...])
    )

    @pl.when(step == 0)
    def _():
        grad_normed[...] = total

    @pl.when(step > 0)
    def _():
        grad_normed[...] += total


def attend_back(
    grad_branch, normed, query, key, value, attended, weights, out_weight, bias, cosine, sine_table
):
    tokens, width = normed.shape
    group = 2 * HD
    steps = width // group
    low = jnp.bfloat16
    whole = lambda *shape: pl.BlockSpec(shape, lambda i: (0,) * len(shape))
    columns = pl.BlockSpec((tokens, group), lambda i: (0, i))
    return pl.pallas_call(
        attend_back_kernel,
        grid=(steps,),
        in_specs=[whole(tokens, width)] * 2
        + [columns] * 4
        + [pl.BlockSpec((group, width), lambda i, m=m: (i, m)) for m in range(3)]
        + [
            pl.BlockSpec((width, group), lambda i: (0, i)),
            whole(tokens, tokens),
            whole(tokens, HD),
            whole(tokens, HD),
        ],
        out_specs=[pl.BlockSpec((group, width), lambda i: (i, 0))] * 3
        + [pl.BlockSpec((width, group), lambda i: (0, i)), whole(tokens, width)],
        out_shape=[jax.ShapeDtypeStruct((width, width), low)] * 4
        + [jax.ShapeDtypeStruct((tokens, width), jnp.float32)],
        scratch_shapes=[pltpu.VMEM((3, tokens, group), low)],
        compiler_params=pltpu.CompilerParams(vmem_limit_bytes=48 * 1024 * 1024),
        cost_estimate=pl.CostEstimate(
            flops=16 * tokens * width * width, bytes_accessed=40 * width * width, transcendentals=0
        ),
    )(
        grad_branch,
        normed,
        query,
        key,
        value,
        attended,
        weights,
        weights,
        weights,
        out_weight,
        bias,
        cosine,
        sine_table,
    )


def expert_kernel(count, numbers, *refs):
    low, full = jnp.bfloat16, jnp.float32
    rows_in, grads_in, slots_in, gates_in = [refs[i * count : (i + 1) * count] for i in range(4)]
    gate_weight, up_weight, down_weight, *refs = refs[4 * count :]
    grad_total, result_total = refs[:count], refs[count : 2 * count]
    rows_out, inner_out, gated_out, grad_gate_out, grad_up_out = refs[2 * count : 2 * count + 5]
    hot_all, grad_all, result_all, word_sums = refs[2 * count + 5 :]
    tokens, width = slots_in[0].shape[2], rows_in[0].shape[1]
    slots = rows_out.shape[1] // count
    experts = word_sums.shape[1]
    q = pl.program_id(0)
    slot_ids = lax.broadcasted_iota(jnp.int32, (slots, tokens), 0).astype(full)
    parts = [slice(r * slots, (r + 1) * slots) for r in range(count)]
    here = pl.ds(pl.multiple_of(q * slots, slots), slots)
    places, gate_cols, grad_parts = [], [], []
    for r in range(count):
        place = slots_in[r][0] == slot_ids
        hot = place.astype(low)
        hot_all[r, here] = hot
        places.append(place)
        gate_cols.append(jnp.sum(jnp.where(place, gates_in[r][0], 0.0), axis=1, keepdims=True))
        rows_out[0, parts[r]] = dot_nn(hot, rows_in[r][:tokens]).astype(low)
        grad_parts.append(dot_nn(hot, grads_in[r][:tokens]))
    gate_col = jnp.concatenate(gate_cols, axis=0)
    grad_rows = jnp.concatenate(grad_parts, axis=0)
    rows = rows_out[0]
    gated = (grad_rows * gate_col).astype(low)
    gated_out[0] = gated
    gate_rows = dot_nn(rows, gate_weight[0])
    up_rows = dot_nn(rows, up_weight[0])
    logistic = jax.nn.sigmoid(gate_rows)
    silu_rows = gate_rows * logistic
    slope_rows = logistic * (1.0 + gate_rows * (1.0 - logistic))
    inner = (silu_rows * up_rows).astype(low)
    inner_out[0] = inner
    grad_inner = dot_nt(gated, down_weight[0])
    grad_gate_rows = (grad_inner * up_rows * slope_rows).astype(low)
    grad_up_rows = (grad_inner * silu_rows).astype(low)
    grad_gate_out[0] = grad_gate_rows
    grad_up_out[0] = grad_up_rows
    sent_grads = (
        dot_nt(grad_gate_rows, gate_weight[0]) + dot_nt(grad_up_rows, up_weight[0])
    ).astype(low)
    result_rows = dot_nn(inner, down_weight[0])
    gate_grad = jnp.sum(result_rows * grad_rows, axis=1, keepdims=True)
    sent_results = (result_rows * gate_col).astype(low)
    expert_ids = lax.broadcasted_iota(jnp.int32, (experts, width), 0)

    @pl.when(q == 0)
    def _():
        word_sums[...] = jnp.zeros_like(word_sums)

    for r in range(count):
        grad_all[r, here] = sent_grads[parts[r]]
        result_all[r, here] = sent_results[parts[r]]
        token_grad = jnp.sum(
            jnp.where(places[r], gate_grad[parts[r]], 0.0), axis=0, keepdims=True
        )
        words = jnp.concatenate(
            [word.astype(full) for word in split_words(token_grad)]
            + [jnp.zeros((1, width - 3 * tokens), full)],
            axis=1,
        )
        word_sums[r] += jnp.where(expert_ids == numbers[q], words, 0.0)

    @pl.when(q == PLANE - 1)
    def _():
        for r in range(count):
            grad_total[r][:tokens] = dot_tn(hot_all[r], grad_all[r]).astype(low)
            grad_total[r][tokens:] = word_sums[r].astype(low)
            result_total[r][...] = dot_tn(hot_all[r], result_all[r]).astype(low)


def run_experts(numbers, rows, grads, slot_rows, gate_rows, weights, slots):
    count = len(rows)
    extended, width = rows[0].shape
    tokens = slot_rows[0].shape[2]
    low = jnp.bfloat16
    hidden_width = weights[0].shape[2]
    whole = lambda *shape: pl.BlockSpec(shape, lambda q, numbers: (0,) * len(shape))
    each = lambda *shape: pl.BlockSpec((1,) + shape, lambda q, numbers: (q, 0, 0))
    sizes = (width, hidden_width, width, hidden_width, hidden_width)
    out = pl.pallas_call(
        functools.partial(expert_kernel, count),
        grid_spec=pltpu.PrefetchScalarGridSpec(
            num_scalar_prefetch=1,
            grid=(PLANE,),
            in_specs=[whole(extended, width)] * (2 * count)
            + [each(1, tokens)] * (2 * count)
            + [each(*array.shape[1:]) for array in weights],
            out_specs=[whole(extended, width)] * count
            + [whole(tokens, width)] * count
            + [each(count * slots, size) for size in sizes],
            scratch_shapes=[
                pltpu.VMEM((count, PLANE * slots, tokens), low),
                pltpu.VMEM((count, PLANE * slots, width), low),
                pltpu.VMEM((count, PLANE * slots, width), low),
                pltpu.VMEM((count, extended - tokens, width), jnp.float32),
            ],
        ),
        out_shape=[jax.ShapeDtypeStruct((extended, width), low)] * count
        + [jax.ShapeDtypeStruct((tokens, width), low)] * count
        + [jax.ShapeDtypeStruct((PLANE, count * slots, size), low) for size in sizes],
        compiler_params=pltpu.CompilerParams(vmem_limit_bytes=62 * 1024 * 1024),
        cost_estimate=pl.CostEstimate(
            flops=count * PLANE * slots * width * (10 * hidden_width + 8 * tokens),
            bytes_accessed=6 * PLANE * width * hidden_width,
            transcendentals=0,
        ),
    )(numbers, *rows, *grads, *slot_rows, *gate_rows, *weights)
    return out[:count], out[count : 2 * count], out[2 * count :]


FIRST_ORDERS = (0, 1, 2, 0, 1, 2)


def gather_plan(units, orders):
    least, more = divmod(units, len(orders))
    widths = [least] * len(orders)
    for i in sorted(range(len(orders)), key=lambda i: (-orders[i], -i))[:more]:
        widths[i] += 1
    if least > 2:
        for i, order in enumerate(orders):
            widths[i] += order - 1
    return tuple((order, 128 * width) for order, width in zip(orders, widths))


def shared_grads_kernel(rows, grad_gate, grad_up, grads, inner, gate_out, up_out, down_out):
    low = jnp.bfloat16
    gate_out[...] = dot_tn(rows[...], grad_gate[...]).astype(low)
    up_out[...] = dot_tn(rows[...], grad_up[...]).astype(low)
    down_out[...] = dot_tn(grads[...], inner[...]).astype(low)


def shared_grads(rows, grad_gate, grad_up, grads, inner):
    shape = jax.ShapeDtypeStruct((rows.shape[1], inner.shape[1]), jnp.bfloat16)
    return pl.pallas_call(
        shared_grads_kernel,
        in_specs=[pl.BlockSpec(memory_space=pltpu.VMEM)] * 5,
        out_specs=[pl.BlockSpec(memory_space=pltpu.VMEM)] * 3,
        out_shape=[shape] * 3,
        compiler_params=pltpu.CompilerParams(vmem_limit_bytes=32 * 1024 * 1024),
        cost_estimate=pl.CostEstimate(
            flops=6 * rows.size * inner.shape[1],
            bytes_accessed=4 * rows.size + 6 * rows.shape[1] * inner.shape[1],
            transcendentals=0,
        ),
    )(rows, grad_gate, grad_up, grads, inner)


def split_words(values):
    words = []
    for _ in range(3):
        words.append(values.astype(jnp.bfloat16))
        values = values - words[-1].astype(jnp.float32)
    return words


def after(value, other):
    return lax.optimization_barrier((value, other))[0]


def add_low(a, b):
    return (a.astype(jnp.float32) + b.astype(jnp.float32)).astype(jnp.bfloat16)


class Grid:
    def __init__(self, experts):
        self.experts = experts
        self.line = experts // PLANE
        here = lax.axis_index("expert")
        self.core = lax.axis_index("dp")
        self.at_line = here // PLANE
        self.at_plane = here % PLANE

    def shift(self, block, amount):
        pairs = [
            (i, ((i // PLANE + amount) % self.line) * PLANE + i % PLANE)
            for i in range(self.experts)
        ]
        return lax.ppermute(block, "expert", pairs)

    def swap(self, block, flip):
        pairs = [(i, (i // PLANE) * PLANE + ((i % PLANE) ^ flip)) for i in range(self.experts)]
        return lax.ppermute(block, "expert", pairs)

    def line_gather(self, block, rising=None, falling=None):
        half, rest = self.line // 2, (self.line - 1) // 2
        rising = self.shift(block, 1) if rising is None else rising
        found = [block, rising] + [None] * (self.line - 2)
        for i in range(2, half + 1):
            found[i] = self.shift(found[i - 1], 1)
        if rest:
            found[-1] = self.shift(block, -1) if falling is None else falling
            for i in range(2, rest + 1):
                found[-i] = self.shift(found[1 - i], -1)
        return found


def local(
    tokens_in,
    lengths,
    key_keep,
    routes,
    cotangent,
    attention_in,
    attention_in_momentum,
    attention_in_average,
    attention_out,
    attention_out_momentum,
    attention_out_average,
    shared_in,
    shared_in_momentum,
    shared_in_average,
    shared_down,
    shared_down_momentum,
    shared_down_average,
    router,
    router_momentum,
    router_average,
    norm_gains,
    norm_gains_momentum,
    norm_gains_average,
    expert_in,
    expert_in_momentum,
    expert_in_average,
    expert_down,
    expert_down_momentum,
    expert_down_average,
):
    low = jnp.bfloat16
    full = jnp.float32
    tokens = tokens_in.shape[0]
    model_width = tokens_in.shape[1]
    top_count = routes.shape[1]
    block_rows = router.shape[0]
    experts = router.shape[1]
    hidden_width = shared_in.shape[2]
    grid = Grid(experts)
    capacity = 9 * tokens * top_count // (8 * experts)
    slots = -(-capacity // 16) * 16
    extra_width = -(-(experts + 2) // 128) * 128

    pack_one = jnp.concatenate(
        [attention_in[m].astype(low).T for m in range(3)]
        + [
            router.astype(low),
            norm_gains.astype(low).T,
            jnp.zeros((block_rows, extra_width - experts - 2), low),
        ],
        axis=1,
    )
    pack_out = attention_out.astype(low).T
    pack_shared = jnp.concatenate(
        [shared_in[0].astype(low), shared_in[1].astype(low), shared_down.astype(low).T], axis=1
    )
    position = jnp.arange(tokens, dtype=jnp.int32)
    usable = position < lengths[0]
    named = jnp.any(
        routes.T[None, :, :] == jnp.arange(experts, dtype=jnp.int32)[:, None, None], axis=1
    )
    member = named & usable[None, :]
    earlier = (position[:, None] < position[None, :]).astype(low)
    counted = dot_nn(member.astype(low), earlier)
    slot_of = jnp.where(member, counted, -1.0)
    wanted = grid.at_line * PLANE + (grid.at_plane ^ jnp.arange(PLANE, dtype=jnp.int32))
    choose = (wanted[:, None] == jnp.arange(experts, dtype=jnp.int32)[None, :]).astype(low)

    def widen(rows):
        return jnp.pad(rows, ((0, 0), (0, model_width - rows.shape[1])))

    pair, down = expert_in[0].astype(low), expert_down[0].astype(low)
    plans = (
        gather_plan(pack_one.shape[1] // 128, FIRST_ORDERS),
        gather_plan(model_width // 128, FIRST_ORDERS),
    )
    (all_one, turned_out), down_x, down_y = first_exchange(
        experts, [pack_one, pack_out], plans, down
    )
    line_grads, sent = after(
        (jnp.concatenate([cotangent, widen(slot_of.astype(low))], axis=0), pair), turned_out
    )
    line_grads = grid.line_gather(line_grads)
    pairs = [pair, grid.swap(sent, 1), grid.swap(sent, 2)]
    downs = [down, down_x, down_y]
    all_one = all_one.reshape(model_width, -1)
    turned_out = turned_out.reshape(model_width, model_width)
    extra = all_one[:, 3 * model_width :]
    router_low = extra[:, :experts]
    gains = extra[:, experts : experts + 2].astype(full).T
    gain_one, gain_two = gains[0], gains[1]
    inputs = tokens_in.astype(full)
    rstd_one = lax.rsqrt(jnp.mean(inputs * inputs, axis=-1, keepdims=True) + eps_norm)
    normed_one = (inputs * rstd_one * gain_one).astype(low)
    cosine, sine_table = rope_tables(tokens, HD)
    bias = jnp.where(allowed_keys(lengths[0], key_keep), 0.0, mask_fill)
    query, key_rot, value, attended, hidden, normed_two = attend(
        normed_one, all_one, turned_out, bias, cosine, sine_table, tokens_in, gain_two[None]
    )
    rstd_two = lax.rsqrt(jnp.mean(hidden * hidden, axis=-1, keepdims=True) + eps_norm)

    logits = lax.dot_general(
        router_low, normed_two, (((0,), (1,)), ((), ())), preferred_element_type=full
    )
    logits = jnp.where(named, logits, mask_fill)
    logit_exps = jnp.exp(logits - jnp.max(logits, axis=0, keepdims=True))
    gating = logit_exps / jnp.sum(logit_exps, axis=0, keepdims=True)
    gating_live = jnp.where(member, gating, 0.0)
    gate_words = jnp.concatenate(split_words(gating_live), axis=1)
    line_rows = jnp.concatenate([normed_two, widen(gate_words)], axis=0)
    line_rows = after(line_rows, [line_grads[1], line_grads[-1]])
    rising, falling, *weights = second_exchange(experts, line_rows, pairs, downs)
    line_rows = grid.line_gather(line_rows, rising, falling)
    weights = [part.reshape(PLANE, -1, part.shape[-1]) for part in weights]

    kept, grad_parts, result_parts = [], [], []
    last = weights
    for start in range(0, grid.line, 2):
        group = range(start, start + 2)
        line_part = [line_rows[r] for r in group], [line_grads[r] for r in group]
        rows, grads = after(line_part, last)
        slot_rows, gate_rows = [], []
        for part in rows:
            words = dot_nn(choose, part[tokens:, : 3 * tokens])
            gate_row = words[:, :tokens] + words[:, tokens : 2 * tokens] + words[:, 2 * tokens :]
            gate_rows.append(gate_row[:, None])
        for part in grads:
            slot_rows.append(dot_nn(choose, part[tokens:, :tokens])[:, None])
        grad_part, result_part, parts = run_experts(
            wanted, rows, grads, slot_rows, gate_rows, weights, slots
        )
        kept.append(parts)
        last = grad_part
        grad_parts += [grid.shift(part, -r) if r else part for r, part in zip(group, grad_part)]
        result_parts += result_part
    routed_grad = sum(part.astype(full) for part in grad_parts)
    result_parts = after(result_parts, routed_grad)
    result_parts = [grid.shift(part, -r) if r else part for r, part in enumerate(result_parts)]
    owns, crossed, nears = third_exchange(experts, after(kept, last))
    arrived = [grid.swap(part, flip) for part, flip in zip(nears, (1, 2))]
    gate_grads = routed_grad[tokens:]
    routed_grad = routed_grad[:tokens]
    grad_gating = (
        gate_grads[:, :tokens]
        + gate_grads[:, tokens : 2 * tokens]
        + gate_grads[:, 2 * tokens : 3 * tokens]
    )
    grad_chosen = gating * (grad_gating - jnp.sum(gating * grad_gating, axis=0, keepdims=True))
    grad_logits = grad_chosen.astype(low)
    grad_router = lax.dot_general(
        normed_two, grad_logits, (((0,), (1,)), ((), ())), preferred_element_type=full
    )

    all_shared = lax.all_gather(
        after(pack_shared, weights), ("dp", "expert"), axis=0, tiled=True
    )
    shared_pair = [all_shared[:, m * hidden_width : (m + 1) * hidden_width] for m in range(2)]
    turned_down = all_shared[:, 2 * hidden_width :]
    grad_out = cotangent.astype(full)
    shared_gate = dot_nn(normed_two, shared_pair[0])
    shared_up = dot_nn(normed_two, shared_pair[1])
    shared_silu, shared_slope = silu_parts(shared_gate)
    shared_hidden = (shared_silu * shared_up).astype(low)
    shared_result = dot_nt(shared_hidden, turned_down)
    grad_shared_hidden = dot_nn(cotangent, turned_down)
    grad_shared_gate = (grad_shared_hidden * shared_up * shared_slope).astype(low)
    grad_shared_up = (grad_shared_hidden * shared_silu).astype(low)
    grad_normed_two = dot_nt(grad_shared_gate, shared_pair[0]) + dot_nt(
        grad_shared_up, shared_pair[1]
    )
    grad_normed_two = grad_normed_two + lax.dot_general(
        grad_logits, router_low, (((0,), (1,)), ((), ())), preferred_element_type=full
    )

    grad_normed_two = grad_normed_two + routed_grad
    scaled_two = grad_normed_two * gain_two
    grad_gain_two = jnp.sum(grad_normed_two * hidden * rstd_two, axis=0)
    grad_hidden = (
        grad_out
        + rstd_two * scaled_two
        - hidden * rstd_two**3 * jnp.mean(scaled_two * hidden, axis=-1, keepdims=True)
    )
    grad_branch = grad_hidden.astype(low)
    grads_shared = shared_grads(
        normed_two, grad_shared_gate, grad_shared_up, cotangent, shared_hidden
    )
    *grads_attention, grad_normed_one = attend_back(
        grad_branch,
        normed_one,
        query,
        key_rot,
        value,
        attended,
        all_one,
        turned_out,
        bias,
        cosine,
        sine_table,
    )
    scaled_one = grad_normed_one * gain_one
    grad_gain_one = jnp.sum(grad_normed_one * inputs * rstd_one, axis=0)
    input_grad = (
        grad_hidden
        + rstd_one * scaled_one
        - inputs * rstd_one**3 * jnp.mean(scaled_one * inputs, axis=-1, keepdims=True)
    )
    grad_extra = jnp.concatenate(
        [
            grad_router.astype(low),
            jnp.stack([grad_gain_one, grad_gain_two], axis=1).astype(low),
            jnp.zeros((model_width, extra_width - experts - 2), low),
        ],
        axis=1,
    )
    *sums, total_in, total_down = sum_all(
        experts,
        grads_attention + list(grads_shared) + [grad_extra],
        sum_plans(model_width, hidden_width, extra_width),
        owns,
        crossed,
    )
    half, down_half = model_width // 2, hidden_width // 2
    more = model_width - hidden_width
    total_in, total_down = total_in.astype(full), total_down.astype(full)
    for package in after(arrived, total_in):
        total_in = total_in + package[: 2 * half].reshape(2, half, hidden_width).astype(full)
        below = package[2 * half + down_half :]
        below = jnp.concatenate([below[:, :more], below[:, more : 2 * more]], axis=0)
        down = package[2 * half : 2 * half + down_half]
        total_down = total_down + jnp.concatenate([down, below], axis=1).astype(full)
    result_parts = after(result_parts, total_in)
    routed_result = sum(part.astype(full) for part in result_parts)
    output = (hidden + shared_result + routed_result).astype(low)

    sums = [part.astype(full) for part in sums]
    summed_in = jnp.stack([part.T for part in sums[:3]], axis=0)
    summed_out = sums[3].T
    summed_shared_in = jnp.stack(sums[4:6], axis=0)
    summed_shared_down = sums[6].T
    summed_router = sums[7][:, :experts]
    summed_gains = sums[7][:, experts : experts + 2].T
    upd_attn_in = advance(
        attention_in, attention_in_momentum, attention_in_average, summed_in, rate_attention_in
    )
    upd_attn_out = advance(
        attention_out, attention_out_momentum, attention_out_average, summed_out, rate_attention_out
    )
    upd_shared_in = advance(
        shared_in, shared_in_momentum, shared_in_average, summed_shared_in, rate_shared_in
    )
    upd_shared_down = advance(
        shared_down, shared_down_momentum, shared_down_average, summed_shared_down, rate_shared_down
    )
    upd_router = advance(router, router_momentum, router_average, summed_router, rate_router)
    upd_gains = advance(
        norm_gains, norm_gains_momentum, norm_gains_average, summed_gains, rate_gains
    )
    upd_expert_in = advance(
        expert_in,
        expert_in_momentum,
        expert_in_average,
        total_in[None],
        rate_expert_in,
    )
    upd_expert_down = advance(
        expert_down,
        expert_down_momentum,
        expert_down_average,
        total_down[None],
        rate_expert_down,
    )
    return (
        output,
        input_grad,
        upd_attn_in[0],
        upd_attn_in[1],
        upd_attn_in[2],
        upd_attn_out[0],
        upd_attn_out[1],
        upd_attn_out[2],
        upd_shared_in[0],
        upd_shared_in[1],
        upd_shared_in[2],
        upd_shared_down[0],
        upd_shared_down[1],
        upd_shared_down[2],
        upd_router[0],
        upd_router[1],
        upd_router[2],
        upd_gains[0],
        upd_gains[1],
        upd_gains[2],
        upd_expert_in[0],
        upd_expert_in[1],
        upd_expert_in[2],
        upd_expert_down[0],
        upd_expert_down[1],
        upd_expert_down[2],
    )


def solution(mesh):
    in_specs = (
        P(("dp", "expert"), None),
        P(("dp", "expert")),
        P(("dp", "expert")),
        P(("dp", "expert"), None),
        P(("dp", "expert"), None),
        P(None, None, ("dp", "expert")),
        P(None, None, ("dp", "expert")),
        P(None, None, ("dp", "expert")),
        P(None, ("dp", "expert")),
        P(None, ("dp", "expert")),
        P(None, ("dp", "expert")),
        P(None, ("dp", "expert"), None),
        P(None, ("dp", "expert"), None),
        P(None, ("dp", "expert"), None),
        P(None, ("dp", "expert")),
        P(None, ("dp", "expert")),
        P(None, ("dp", "expert")),
        P(("dp", "expert"), None),
        P(("dp", "expert"), None),
        P(("dp", "expert"), None),
        P(None, ("dp", "expert")),
        P(None, ("dp", "expert")),
        P(None, ("dp", "expert")),
        P("expert", None, "dp", None),
        P("expert", None, "dp", None),
        P("expert", None, "dp", None),
        P("expert", "dp", None),
        P("expert", "dp", None),
        P("expert", "dp", None),
    )
    out_specs = (
        P(("dp", "expert"), None),
        P(("dp", "expert"), None),
        P(None, None, ("dp", "expert")),
        P(None, None, ("dp", "expert")),
        P(None, None, ("dp", "expert")),
        P(None, ("dp", "expert")),
        P(None, ("dp", "expert")),
        P(None, ("dp", "expert")),
        P(None, ("dp", "expert"), None),
        P(None, ("dp", "expert"), None),
        P(None, ("dp", "expert"), None),
        P(None, ("dp", "expert")),
        P(None, ("dp", "expert")),
        P(None, ("dp", "expert")),
        P(("dp", "expert"), None),
        P(("dp", "expert"), None),
        P(("dp", "expert"), None),
        P(None, ("dp", "expert")),
        P(None, ("dp", "expert")),
        P(None, ("dp", "expert")),
        P("expert", None, "dp", None),
        P("expert", None, "dp", None),
        P("expert", None, "dp", None),
        P("expert", "dp", None),
        P("expert", "dp", None),
        P("expert", "dp", None),
    )
    return jax.shard_map(local, mesh=mesh, in_specs=in_specs, out_specs=out_specs, check_vma=False)
```
